32 devices in a mesh: gx: 2 (over x), gy: 4 (over y, core), ta: 4 (over z).
Axes of the slice: x: 2, y: 2, z: 4, core: 2. Of those that a mesh axis runs over, the one named last changes fastest.
Arguments:
- frames: bfloat16 [32, 16, 256, 128], P('ta', 'gx', 'gy'), may hold values from -6 to 6
- in_weight: bfloat16 [3, 3, 128, 128], replicated, may hold values from -0.1875 to 0.1875
- out_weight: bfloat16 [3, 3, 128, 128], replicated, may hold values from -0.1875 to 0.1875
- decays: float32 [32, 128], P('ta'), may hold values from 0.05 to 0.999, as said below
Outputs:
- mixed_frames: bfloat16 [32, 16, 256, 128], P('ta', 'gx', 'gy')
The draws below stay inside these ranges and needn't reach their ends.
Inputs may be any that keep to these rules, and one draw needn't show every extreme that they name: `decays`: every factor lies strictly between 0 and 1.
All inputs are finite; a program needn't handle non-finite values.
Results may differ from the reference program's by a relative error of at most 0.0031.
Values may be sent and summed in bfloat16 or wider, within the bound.
No kernel may reach another device: no remote copies, remote signals or barrier semaphores. Data moves between devices by JAX's collectives and lax.ppermute only.
A program may use at most 64 MiB of HBM per device.

```python
import math
import jax
import jax.numpy as jnp
from jax import lax

FEAT = 128
LATENT_FEATURES = 128
SEQUENCE_LENGTH = 32
HEIGHT = 16
WIDTH = 256


def draw_decays(key, part):
    generator_seeds = jax.random.split(jax.random.fold_in(key, 11), 6)
    share = 0.5
    quick = jax.random.uniform(generator_seeds[0], (LATENT_FEATURES,)) < share
    quick_rate = jax.random.uniform(generator_seeds[1], (LATENT_FEATURES,), jnp.float32, 0.2, 0.6)
    slow_rate = jnp.exp(-jax.random.uniform(generator_seeds[2], (LATENT_FEATURES,), jnp.float32, 0.05, 0.4) * math.log(10.0) / SEQUENCE_LENGTH)
    nominal_level = jnp.where(quick, quick_rate, slow_rate)
    spike_occurred = jax.random.uniform(generator_seeds[3], (SEQUENCE_LENGTH, LATENT_FEATURES)) < 1.5 / SEQUENCE_LENGTH
    spike_sample = jnp.where(spike_occurred, jax.random.uniform(generator_seeds[4], (SEQUENCE_LENGTH, LATENT_FEATURES), jnp.float32, 0.5, 0.8), 1.0)
    small_perturbation = jnp.where(quick[None, :], jax.random.uniform(generator_seeds[5], (SEQUENCE_LENGTH, LATENT_FEATURES), jnp.float32, 0.6, 1.0), 1.0)
    return (nominal_level[None, :] * spike_sample * small_perturbation).astype(jnp.float32)


def steps_of(rng, shape, cuts, low, largest):
    gain, own = 1.0, jax.random.fold_in(rng, 6)
    for axis_at, blocks in cuts:
        steps = jnp.exp(jax.random.uniform(jax.random.fold_in(own, axis_at), (blocks,), jnp.float32, low / len(cuts), largest / len(cuts)))
        gain = gain * jnp.repeat(steps, shape[axis_at] // blocks).reshape([-1 if axis == axis_at else 1 for axis in range(len(shape))])
    return gain


def noise(stream_key, shape, deviation, limit, shards=(), dtype=jnp.bfloat16):
    entries = deviation * jax.random.normal(stream_key, shape, jnp.float32)
    if shards:
        entries = entries * steps_of(stream_key, shape, shards, -0.22, 0.18)
    return jnp.clip(entries, -limit, limit).astype(dtype)


def setup_inputs(seed: int = 0) -> dict:
    seeds = jax.random.split(jax.random.key(seed), 5)
    frames = noise(seeds[0], (SEQUENCE_LENGTH, HEIGHT, WIDTH, FEAT), 1.0, 6.0, ((0, 4), (1, 2), (2, 4)))
    in_weight = noise(seeds[1], (3, 3, FEAT, LATENT_FEATURES), (9 * FEAT) ** -0.5, 0.1875)
    out_weight = noise(seeds[2], (3, 3, LATENT_FEATURES, FEAT), (9 * LATENT_FEATURES) ** -0.5, 0.1875)
    decays = draw_decays(jax.random.fold_in(seeds[4], 71), 0)
    return {"frames": frames, "in_weight": in_weight, "out_weight": out_weight, "decays": decays}


def convolve(picture, weight):
    return lax.conv_general_dilated(picture[None], weight, (1, 1), 'SAME', dimension_numbers=('NHWC', 'HWIO', 'NHWC'), preferred_element_type=jnp.float32)[0]

def reference(frames, in_weight, out_weight, decays):

    def advance(carried, inputs):
        picture, factors = inputs
        driven = convolve(picture, in_weight)
        carried = factors * carried + jnp.sqrt(1.0 - factors * factors) * driven
        mixed = convolve(carried.astype(jnp.bfloat16), out_weight)
        result = (picture.astype(jnp.float32) + jax.nn.gelu(mixed)).astype(jnp.bfloat16)
        return (carried, result)
    initial = jnp.zeros((HEIGHT, WIDTH, LATENT_FEATURES), jnp.float32)
    return lax.scan(advance, initial, (frames, decays))[1]
```

```python
import functools

import jax
import jax.numpy as jnp
from jax import lax
from jax.experimental import pallas as pl
from jax.experimental.pallas import tpu as pltpu
from jax.sharding import PartitionSpec as P

F32, BF16 = jnp.float32, jnp.bfloat16
VMEM = pl.BlockSpec(memory_space=pltpu.VMEM)
SMEM = pl.BlockSpec(memory_space=pltpu.SMEM)


def pair_weights(w_ref, wt, flip):
    chan_in, chan_out = w_ref.shape[2:]
    for k in range(4):
        for b in range(3):
            for rr in range(2):
                at = (k * 3 + b) * chan_in
                a = k - rr
                if 0 <= a <= 2:
                    block = w_ref[jnp.where(flip == 1, 2 - a, a), b]
                else:
                    block = jnp.zeros((chan_in, chan_out), BF16)
                wt[at : at + chan_in, rr * chan_out : (rr + 1) * chan_out] = block


def clear_margins(rowbuf):
    across = rowbuf.shape[1] - 16
    zeros = jnp.zeros((rowbuf.shape[0], 8, rowbuf.shape[2]), F32)
    rowbuf[:, 0:8, :] = zeros
    rowbuf[:, 8 + across : 16 + across, :] = zeros


def three_taps(rowbuf, slot, x3, row, f, middle):
    across = rowbuf.shape[1] - 16
    chan = rowbuf.shape[2]
    at = pl.ds(f * across, across)
    x3[row, at, 0:chan] = rowbuf[slot, 7 : 7 + across, :].astype(BF16)
    x3[row, at, chan : 2 * chan] = middle
    x3[row, at, 2 * chan : 3 * chan] = rowbuf[slot, 9 : 9 + across, :].astype(BF16)


def pair_dot(x3, slots, wt):
    width = x3.shape[2]
    first = next(k for k in range(4) if slots[k] is not None)
    rows = jnp.concatenate([x3[s] for s in slots[first:]], axis=1)
    return jnp.dot(rows, wt[first * width : 4 * width, :], preferred_element_type=F32)


def scan_rows(y, decays, scales, across, keep):
    frames = decays.shape[0]
    chan = decays.shape[1]
    finals = []
    for rr in range(2):
        s = None
        for f in range(frames):
            u = scales[f : f + 1] * y[f * across : (f + 1) * across, rr * chan : (rr + 1) * chan]
            s = u if s is None else decays[f : f + 1] * s + u
            keep(rr, f, s)
        finals.append(s)
    return finals


def load_decays(dec_ref):
    decays = dec_ref[...]
    return decays, jnp.sqrt(1.0 - decays * decays)


def inner_kernel(two, where_ref, frames_ref, w_ref, dec_ref, p_ref, f_ref, wt, rowbuf, x3):
    frames, height, across, chan = frames_ref.shape
    flip = where_ref[0]
    pair_weights(w_ref, wt, flip)
    clear_margins(rowbuf)
    decays, scales = load_decays(dec_ref)
    for r in range(height):
        natural = jnp.where(flip == 1, height - 1 - r, r)
        for f in range(frames):
            slot = (r * frames + f) % rowbuf.shape[0]
            x = frames_ref[f, natural]
            rowbuf[slot, 8 : 8 + across, :] = x.astype(F32)
            three_taps(rowbuf, slot, x3, r, f, x)
    first, first_row = (0, 1) if two else (1, 0)
    for p in range(first, height // 2):
        slots = [r if r >= 0 else None for r in range(2 * p - 2, 2 * p + 2)]
        y = pair_dot(x3, slots, wt)
        base = 2 * (p - first)

        def keep(rr, f, s, base=base):
            if base + rr >= first_row:
                p_ref[base + rr - first_row, f] = s

        for rr, s in enumerate(scan_rows(y, decays, scales, across, keep)):
            at = base + rr - first_row
            if at >= 0:
                f_ref[at * across : (at + 1) * across, :] = s.astype(BF16)
    total = decays[0:1]
    for f in range(1, frames):
        total = total * decays[f : f + 1]
    high = total.astype(BF16)
    rest = total - high.astype(F32)
    middle = rest.astype(BF16)
    low = rest - middle.astype(F32)
    row = lax.broadcasted_iota(jnp.int32, (16, chan), 0)
    parts = jnp.where(row == 0, high.astype(F32), jnp.where(row == 1, middle.astype(F32), jnp.where(row == 2, low, 0.0)))
    end = f_ref.shape[0]
    f_ref[end - 16 : end, :] = parts.astype(BF16)


def edge_kernel(
    two, where_ref, frames_ref, halo_ref, e_ref, l_ref, r_ref, w_ref, dec_ref,
    p_ref, pc_ref, f_ref, wt, rowbuf, x3, xc, yc,
):
    frames, height, across, chan = frames_ref.shape
    flip = where_ref[0]
    pair_weights(w_ref, wt, flip)
    clear_margins(rowbuf)
    decays, scales = load_decays(dec_ref)
    pairs = [height // 2] if two else [0, height // 2]
    for i, p in enumerate(pairs):
        for k in range(4):
            r = 2 * p - 2 + k
            for f in range(frames):
                slot = (k * frames + f) % rowbuf.shape[0]
                if 0 <= r < height:
                    x = frames_ref[f, jnp.where(flip == 1, height - 1 - r, r)]
                elif two:
                    x = halo_ref[f, jnp.where(flip == 1, 1 - (r - height), r - height)]
                else:
                    x = halo_ref[f, r + 2 if r < 0 else r - height + 2]
                rowbuf[slot, 8 : 8 + across, :] = x.astype(F32)
                three_taps(rowbuf, slot, x3, i * 4 + k, f, x)
        y = pair_dot(x3, [i * 4 + k for k in range(4)], wt)
        inside = 1.0
        if not two:
            inside = where_ref[3 if p == 0 else 4].astype(F32)

        def keep(rr, f, s, i=i, p=p, inside=inside):
            border = (rr == 0) if p == 0 else (rr == 1)
            p_ref[2 * i + rr, f] = s * inside if border and not two else s

        for rr, s in enumerate(scan_rows(y, decays, scales, across, keep)):
            border = (rr == 0) if p == 0 else (rr == 1)
            s = s * inside if border and not two else s
            f_ref[(2 * i + rr) * across : (2 * i + rr + 1) * across, :] = s.astype(BF16)

    n_pairs = height // 2 + 1
    for p in range(n_pairs):
        for k in range(4):
            r = 2 * p - 2 + k
            if two:
                at = None if r < 0 else jnp.where(flip == 1, height + 1 - r, r)
            else:
                at = r + 2
            to = slice(p * 4 * frames, (p + 1) * 4 * frames)
            lanes = k * 3 * chan
            if at is None:
                xc[to, lanes : lanes + 3 * chan] = jnp.zeros((4 * frames, 3 * chan), BF16)
                continue
            own = e_ref[at].astype(F32)
            left = l_ref[at].astype(F32)
            right = r_ref[at].astype(F32)
            cols = [left[:frames], left[frames:]] + [own[c * frames : (c + 1) * frames] for c in range(4)]
            cols += [right[:frames], right[frames:]]
            for b in range(3):
                piece = jnp.concatenate([cols[c + b] for c in (0, 1, 4, 5)], axis=0)
                xc[to, lanes + b * chan : lanes + (b + 1) * chan] = piece.astype(BF16)
    edge = jnp.dot(xc[...], wt[...], preferred_element_type=F32)
    for h in range(2):
        yc[h] = edge[:, h * chan : (h + 1) * chan]
    count = n_pairs * 4
    place = lax.broadcasted_iota(jnp.int32, (count, 2 * chan), 0)
    lane = lax.broadcasted_iota(jnp.int32, (count, 2 * chan), 1)
    mask = jnp.where(place % 4 == 0, where_ref[1].astype(F32), jnp.where(place % 4 == 3, where_ref[2].astype(F32), 1.0))
    above = (place < 4) & (lane < chan)
    if two:
        mask = jnp.where(above, 0.0, mask)
    else:
        below = (place >= count - 4) & (lane >= chan)
        mask = jnp.where(above, mask * where_ref[3].astype(F32), mask)
        mask = jnp.where(below, mask * where_ref[4].astype(F32), mask)
    s = None
    for f in range(frames):
        both = [jnp.concatenate([v[f : f + 1]] * 2, axis=1) for v in (decays, scales)]
        halves = [yc[h, pl.ds(f, count, stride=frames), :] for h in range(2)]
        u = both[1] * jnp.concatenate(halves, axis=1) * mask
        s = u if s is None else both[0] * s + u
        for h in range(2):
            pc_ref[h, pl.ds(f, count, stride=frames), :] = s[:, h * chan : (h + 1) * chan]
    base = len(pairs) * 2 * across
    pad = jnp.zeros((32 - count, chan), F32)
    for h in range(2):
        half = jnp.concatenate([s[:, h * chan : (h + 1) * chan], pad], axis=0)
        f_ref[base + 32 * h : base + 32 * (h + 1), :] = half.astype(BF16)


def outer_kernel(
    two, where_ref, frames_ref, pa_ref, pb_ref, pc_ref, ra_ref, za_ref, rb_ref, zb_ref, mix_ref, w_ref, dec_ref,
    out_ref, wt, rowbuf, x3, sc, ia, ib,
):
    frames, height, across, chan = frames_ref.shape
    flip = where_ref[0]
    pair_weights(w_ref, wt, flip)
    decays = dec_ref[...]
    alpha, beta = mix_ref[0:1], mix_ref[1:2]
    rows_a = pa_ref.shape[0]
    ia[...] = alpha * ra_ref[0 : rows_a * across].astype(F32) + beta * za_ref[0 : rows_a * across].astype(F32)
    ib[...] = alpha * rb_ref[...].astype(F32) + beta * zb_ref[...].astype(F32)
    running = [decays[0:1]]
    for f in range(1, frames):
        running.append(running[-1] * decays[f : f + 1])
    count = (height // 2 + 1) * 4
    base = pb_ref.shape[0] * across
    for f in range(frames):
        for h in range(2):
            part = pc_ref[h, pl.ds(f, count, stride=frames), :]
            sc[f, h, 0:count, :] = part + running[f] * ib[base + 32 * h : base + 32 * h + count, :]
    for n in range(height + 2):
        if two and n == 0:
            continue
        if two:
            src, at = ((pa_ref, ia), n - 1) if n < height else ((pb_ref, ib), n - height)
        elif 2 <= n < height:
            src, at = (pa_ref, ia), n - 2
        else:
            src, at = (pb_ref, ib), n if n < 2 else n - height + 2
        incoming = src[1][at * across : (at + 1) * across, :]
        for f in range(frames):
            slot = (n * frames + f) % rowbuf.shape[0]
            rowbuf[slot, 8 : 8 + across, :] = src[0][at, f] + running[f] * incoming
            corner = (n // 2) * 4
            h = n % 2
            rowbuf[slot, 7:8, :] = sc[f, h, corner : corner + 1, :]
            rowbuf[slot, 8:9, :] = sc[f, h, corner + 1 : corner + 2, :]
            rowbuf[slot, 7 + across : 8 + across, :] = sc[f, h, corner + 2 : corner + 3, :]
            rowbuf[slot, 8 + across : 9 + across, :] = sc[f, h, corner + 3 : corner + 4, :]
            three_taps(rowbuf, slot, x3, n, f, rowbuf[slot, 8 : 8 + across, :].astype(BF16))
    for p in range(height // 2):
        slots = [n if n > 0 or not two else None for n in range(2 * p, 2 * p + 4)]
        y = pair_dot(x3, slots, wt)
        for rr in range(2):
            r = 2 * p + rr
            natural = jnp.where(flip == 1, height - 1 - r, r)
            for f in range(frames):
                mixed = y[f * across : (f + 1) * across, rr * chan : (rr + 1) * chan]
                out_ref[f, natural] = (frames_ref[f, natural].astype(F32) + jax.nn.gelu(mixed)).astype(BF16)


def call(body, outs, scratch, flops, n_in):
    return pl.pallas_call(
        body,
        out_shape=outs,
        in_specs=[SMEM] + [VMEM] * (n_in - 1),
        out_specs=jax.tree.map(lambda _: VMEM, outs),
        scratch_shapes=scratch,
        compiler_params=pltpu.CompilerParams(vmem_limit_bytes=56 * 2**20),
        cost_estimate=pl.CostEstimate(flops=flops, bytes_accessed=4 * 2**20, transcendentals=0),
    )


def forward(ends):
    return [(i, i + 1) for i in range(ends - 1)]


def backward(ends):
    return [(i + 1, i) for i in range(ends - 1)]


def carry_general(locals_, total, ta):
    step = 1
    while step < ta:
        pairs = [(i, i + step) for i in range(ta - step)]
        moved = [lax.ppermute(v, "ta", pairs) for v in locals_]
        moved_total = lax.ppermute(total, "ta", pairs)
        has = lax.axis_index("ta") >= step
        locals_ = [(v.astype(F32) + total * m.astype(F32)).astype(BF16) for v, m in zip(locals_, moved)]
        total = jnp.where(has, total * moved_total, total)
        step *= 2
    return [lax.ppermute(v, "ta", forward(ta)) for v in locals_]


def on_device(gx, gy, ta, frames, in_weight, out_weight, decays):
    n_frames, height, across, chan = frames.shape
    two = gx == 2
    x, y, t = (lax.axis_index(a) for a in ("gx", "gy", "ta"))
    flip = x if two else jnp.zeros_like(x)
    where = jnp.stack([flip, (y > 0), (y < gy - 1), (x > 0), (x < gx - 1)]).astype(jnp.int32)

    cols = jnp.concatenate([frames[:, :, :2], frames[:, :, across - 2 :]], axis=2)
    cols = cols.transpose(1, 2, 0, 3).reshape(height, 4 * n_frames, chan)
    if two:
        swap = [(0, 1), (1, 0)]
        start = jnp.where(x == 1, 0, height - 2)
        halo = lax.ppermute(lax.dynamic_slice_in_dim(frames, start, 2, axis=1), "gx", swap)
        corner = lax.ppermute(lax.dynamic_slice_in_dim(cols, start, 2, axis=0), "gx", swap)
        cols = jnp.where(x == 1, jnp.concatenate([corner, cols]), jnp.concatenate([cols, corner]))
    else:
        above = lax.ppermute(frames[:, height - 2 :], "gx", forward(gx))
        below = lax.ppermute(frames[:, :2], "gx", backward(gx))
        halo = jnp.concatenate([above, below], axis=1)
        over = lax.ppermute(cols[height - 2 :], "gx", forward(gx))
        under = lax.ppermute(cols[:2], "gx", backward(gx))
        cols = jnp.concatenate([over, cols, under])

    rows_a = height - 1 if two else height - 2
    rows_b = 2 if two else 4
    wt = pltpu.VMEM((12 * chan, 2 * chan), BF16)
    rowbuf = pltpu.VMEM((16, across + 16, chan), F32)
    cells = n_frames * across
    flops = 2 * 9 * chan * chan * cells
    sds = jax.ShapeDtypeStruct
    pa, fa = call(
        functools.partial(inner_kernel, two),
        (sds((rows_a, n_frames, across, chan), F32), sds((rows_a * across + 16, chan), BF16)),
        [wt, rowbuf, pltpu.VMEM((height, cells, 3 * chan), BF16)],
        flops * height, 4,
    )(where, frames, in_weight, decays)

    left = lax.ppermute(cols[:, 2 * n_frames :], "gy", forward(gy))
    right = lax.ppermute(cols[:, : 2 * n_frames], "gy", backward(gy))
    n_cols = (height // 2 + 1) * 4
    pb, pc, fb = call(
        functools.partial(edge_kernel, two),
        (
            sds((rows_b, n_frames, across, chan), F32),
            sds((2, n_cols * n_frames, chan), F32),
            sds((rows_b * across + 64, chan), BF16),
        ),
        [
            wt, rowbuf, pltpu.VMEM((2 * rows_b, cells, 3 * chan), BF16),
            pltpu.VMEM((n_cols * n_frames, 12 * chan), BF16), pltpu.VMEM((2, n_cols * n_frames, chan), F32),
        ],
        flops * rows_b, 8,
    )(where, frames, halo, cols, left, right, in_weight, decays)

    total = jnp.prod(decays, axis=0)[None]
    if ta == 4:
        near, far = [(0, 1), (1, 0), (2, 3)], [(1, 2), (0, 3)]
        ra = lax.ppermute(fa, "ta", near)
        other = jnp.sum(ra[rows_a * across :].astype(F32), axis=0, keepdims=True)

        def joined(mine, theirs):
            mine, theirs = mine.astype(F32), theirs.astype(F32)
            return jnp.where(t == 0, theirs + other * mine, mine + total * theirs).astype(BF16)

        za = lax.ppermute(joined(fa, ra), "ta", far)
        rb = lax.ppermute(fb, "ta", near)
        zb = lax.ppermute(joined(fb, rb), "ta", far)
        alpha = jnp.where((t == 1) | (t == 3), 1.0, 0.0) * jnp.ones_like(total)
        beta = jnp.where(t == 2, 1.0, jnp.where(t == 3, other, 0.0))
    else:
        ra, rb = carry_general([fa, fb], total, ta)
        za, zb = ra, rb
        alpha, beta = jnp.ones_like(total), jnp.zeros_like(total)
    mix = jnp.concatenate([alpha, beta])

    return call(
        functools.partial(outer_kernel, two),
        sds(frames.shape, BF16),
        [
            wt, rowbuf, pltpu.VMEM((height + 2, cells, 3 * chan), BF16),
            pltpu.VMEM((n_frames, 2, (n_cols + 7) // 8 * 8, chan), F32),
            pltpu.VMEM((rows_a * across, chan), F32), pltpu.VMEM((rows_b * across + 64, chan), F32),
        ],
        flops * height, 12,
    )(where, frames, pa, pb, pc, ra, za, rb, zb, mix, out_weight, decays)


def solution(mesh):
    sizes = [mesh.shape[a] for a in ("gx", "gy", "ta")]
    placed = (P("ta", "gx", "gy", None), P(), P(), P("ta", None))
    return jax.shard_map(
        functools.partial(on_device, *sizes), mesh=mesh, in_specs=placed,
        out_specs=P("ta", "gx", "gy", None), check_vma=False,
    )
```

```python
import functools

import jax
import jax.numpy as jnp
from jax import lax
from jax.experimental import pallas as pl
from jax.experimental.pallas import tpu as pltpu
from jax.sharding import PartitionSpec as P

F32, BF16 = jnp.float32, jnp.bfloat16
VMEM = pl.BlockSpec(memory_space=pltpu.VMEM)


def pair_weights(w_ref, wt, flip):
    chan_in, chan_out = w_ref.shape[2:]
    for k in range(4):
        for b in range(3):
            for rr in range(2):
                at = (k * 3 + b) * chan_in
                a = k - rr
                if 0 <= a <= 2:
                    block = w_ref[jnp.where(flip == 1, 2 - a, a), b]
                else:
                    block = jnp.zeros((chan_in, chan_out), BF16)
                wt[at : at + chan_in, rr * chan_out : (rr + 1) * chan_out] = block


def clear_margins(rowbuf):
    across = rowbuf.shape[1] - 16
    zeros = jnp.zeros((rowbuf.shape[0], 8, rowbuf.shape[2]), F32)
    rowbuf[:, 0:8, :] = zeros
    rowbuf[:, 8 + across : 16 + across, :] = zeros


def three_taps(rowbuf, slot, x3, row, f, middle):
    across = rowbuf.shape[1] - 16
    chan = rowbuf.shape[2]
    at = pl.ds(f * across, across)
    x3[row, at, 0:chan] = rowbuf[slot, 7 : 7 + across, :].astype(BF16)
    x3[row, at, chan : 2 * chan] = middle
    x3[row, at, 2 * chan : 3 * chan] = rowbuf[slot, 9 : 9 + across, :].astype(BF16)


def pair_dot(x3, slots, wt):
    width = x3.shape[2]
    first = next(k for k in range(4) if slots[k] is not None)
    rows = jnp.concatenate([x3[s] for s in slots[first:]], axis=1)
    return jnp.dot(rows, wt[first * width : 4 * width, :], preferred_element_type=F32)


def scan_rows(y, decays, scales, across, keep):
    frames = decays.shape[0]
    chan = decays.shape[1]
    finals = []
    for rr in range(2):
        s = None
        for f in range(frames):
            u = scales[f : f + 1] * y[f * across : (f + 1) * across, rr * chan : (rr + 1) * chan]
            s = u if s is None else decays[f : f + 1] * s + u
            keep(rr, f, s)
        finals.append(s)
    return finals


def load_decays(dec_ref):
    decays = dec_ref[...]
    return decays, jnp.sqrt(1.0 - decays * decays)


def inner_kernel(two, frames_ref, w_ref, dec_ref, p_ref, f_ref, wt, rowbuf, x3):
    frames, height, across, chan = frames_ref.shape
    flip = mirrored(two)
    pair_weights(w_ref, wt, flip)
    clear_margins(rowbuf)
    decays, scales = load_decays(dec_ref)
    for r in range(height):
        natural = jnp.where(flip == 1, height - 1 - r, r)
        for f in range(frames):
            slot = (r * frames + f) % rowbuf.shape[0]
            x = frames_ref[f, natural]
            rowbuf[slot, 8 : 8 + across, :] = x.astype(F32)
            three_taps(rowbuf, slot, x3, r, f, x)
    first, first_row = (0, 1) if two else (1, 0)
    for p in range(first, height // 2):
        slots = [r if r >= 0 else None for r in range(2 * p - 2, 2 * p + 2)]
        y = pair_dot(x3, slots, wt)
        base = 2 * (p - first)

        def keep(rr, f, s, base=base):
            if base + rr >= first_row:
                p_ref[base + rr - first_row, f] = s

        for rr, s in enumerate(scan_rows(y, decays, scales, across, keep)):
            at = base + rr - first_row
            if at >= 0:
                f_ref[at * across : (at + 1) * across, :] = s.astype(BF16)
    total = decays[0:1]
    for f in range(1, frames):
        total = total * decays[f : f + 1]
    high = total.astype(BF16)
    rest = total - high.astype(F32)
    middle = rest.astype(BF16)
    low = rest - middle.astype(F32)
    row = lax.broadcasted_iota(jnp.int32, (16, chan), 0)
    parts = jnp.where(row == 0, high.astype(F32), jnp.where(row == 1, middle.astype(F32), jnp.where(row == 2, low, 0.0)))
    end = f_ref.shape[0]
    f_ref[end - 16 : end, :] = parts.astype(BF16)


def edge_kernel(
    two, gx, gy, frames_ref, halo_ref, e_ref, l_ref, r_ref, w_ref, dec_ref,
    p_ref, pc_ref, f_ref, wt, rowbuf, x3, xc, yc,
):
    frames, height, across, chan = frames_ref.shape
    flip = mirrored(two)
    x, y_at = lax.axis_index("gx"), lax.axis_index("gy")
    has_left, has_right = (y_at > 0).astype(F32), (y_at < gy - 1).astype(F32)
    has_above, has_below = (x > 0).astype(F32), (x < gx - 1).astype(F32)
    pair_weights(w_ref, wt, flip)
    clear_margins(rowbuf)
    decays, scales = load_decays(dec_ref)
    pairs = [height // 2] if two else [0, height // 2]
    for i, p in enumerate(pairs):
        for k in range(4):
            r = 2 * p - 2 + k
            for f in range(frames):
                slot = (k * frames + f) % rowbuf.shape[0]
                if 0 <= r < height:
                    x = frames_ref[f, jnp.where(flip == 1, height - 1 - r, r)]
                elif two:
                    x = halo_ref[f, jnp.where(flip == 1, 1 - (r - height), r - height)]
                else:
                    x = halo_ref[f, r + 2 if r < 0 else r - height + 2]
                rowbuf[slot, 8 : 8 + across, :] = x.astype(F32)
                three_taps(rowbuf, slot, x3, i * 4 + k, f, x)
        y = pair_dot(x3, [i * 4 + k for k in range(4)], wt)
        inside = 1.0
        if not two:
            inside = has_above if p == 0 else has_below

        def keep(rr, f, s, i=i, p=p, inside=inside):
            border = (rr == 0) if p == 0 else (rr == 1)
            p_ref[2 * i + rr, f] = s * inside if border and not two else s

        for rr, s in enumerate(scan_rows(y, decays, scales, across, keep)):
            border = (rr == 0) if p == 0 else (rr == 1)
            s = s * inside if border and not two else s
            f_ref[(2 * i + rr) * across : (2 * i + rr + 1) * across, :] = s.astype(BF16)

    n_pairs = height // 2 + 1
    for p in range(n_pairs):
        for k in range(4):
            r = 2 * p - 2 + k
            if two:
                at = None if r < 0 else jnp.where(flip == 1, height + 1 - r, r)
            else:
                at = r + 2
            to = slice(p * 4 * frames, (p + 1) * 4 * frames)
            lanes = k * 3 * chan
            if at is None:
                xc[to, lanes : lanes + 3 * chan] = jnp.zeros((4 * frames, 3 * chan), BF16)
                continue
            own = e_ref[at].astype(F32)
            left = l_ref[at].astype(F32)
            right = r_ref[at].astype(F32)
            cols = [left[:frames], left[frames:]] + [own[c * frames : (c + 1) * frames] for c in range(4)]
            cols += [right[:frames], right[frames:]]
            for b in range(3):
                piece = jnp.concatenate([cols[c + b] for c in (0, 1, 4, 5)], axis=0)
                xc[to, lanes + b * chan : lanes + (b + 1) * chan] = piece.astype(BF16)
    edge = jnp.dot(xc[...], wt[...], preferred_element_type=F32)
    for h in range(2):
        yc[h] = edge[:, h * chan : (h + 1) * chan]
    count = n_pairs * 4
    place = lax.broadcasted_iota(jnp.int32, (count, 2 * chan), 0)
    lane = lax.broadcasted_iota(jnp.int32, (count, 2 * chan), 1)
    mask = jnp.where(place % 4 == 0, has_left, jnp.where(place % 4 == 3, has_right, 1.0))
    above = (place < 4) & (lane < chan)
    if two:
        mask = jnp.where(above, 0.0, mask)
    else:
        below = (place >= count - 4) & (lane >= chan)
        mask = jnp.where(above, mask * has_above, mask)
        mask = jnp.where(below, mask * has_below, mask)
    s = None
    for f in range(frames):
        both = [jnp.concatenate([v[f : f + 1]] * 2, axis=1) for v in (decays, scales)]
        halves = [yc[h, pl.ds(f, count, stride=frames), :] for h in range(2)]
        u = both[1] * jnp.concatenate(halves, axis=1) * mask
        s = u if s is None else both[0] * s + u
        for h in range(2):
            pc_ref[h, pl.ds(f, count, stride=frames), :] = s[:, h * chan : (h + 1) * chan]
    base = len(pairs) * 2 * across
    pad = jnp.zeros((32 - count, chan), F32)
    for h in range(2):
        half = jnp.concatenate([s[:, h * chan : (h + 1) * chan], pad], axis=0)
        f_ref[base + 32 * h : base + 32 * (h + 1), :] = half.astype(BF16)


def outer_kernel(
    two, ta, frames_ref, pa_ref, pb_ref, pc_ref, ra_ref, za_ref, rb_ref, zb_ref, w_ref, dec_ref,
    out_ref, wt, rowbuf, x3, sc, ia, ib,
):
    frames, height, across, chan = frames_ref.shape
    flip = mirrored(two)
    pair_weights(w_ref, wt, flip)
    decays = dec_ref[...]
    rows_a = pa_ref.shape[0]
    if ta == 4:
        t = lax.axis_index("ta")
        end = ra_ref.shape[0]
        other = jnp.sum(ra_ref[end - 16 : end, :].astype(F32), axis=0, keepdims=True)
        alpha = ((t == 1) | (t == 3)).astype(F32)
        beta = jnp.where(t == 3, other, (t == 2).astype(F32))
    else:
        alpha, beta = 1.0, 0.0
    ia[...] = alpha * ra_ref[0 : rows_a * across].astype(F32) + beta * za_ref[0 : rows_a * across].astype(F32)
    ib[...] = alpha * rb_ref[...].astype(F32) + beta * zb_ref[...].astype(F32)
    running = [decays[0:1]]
    for f in range(1, frames):
        running.append(running[-1] * decays[f : f + 1])
    count = (height // 2 + 1) * 4
    base = pb_ref.shape[0] * across
    for f in range(frames):
        for h in range(2):
            part = pc_ref[h, pl.ds(f, count, stride=frames), :]
            sc[f, h, 0:count, :] = part + running[f] * ib[base + 32 * h : base + 32 * h + count, :]
    for n in range(height + 2):
        if two and n == 0:
            continue
        if two:
            src, at = ((pa_ref, ia), n - 1) if n < height else ((pb_ref, ib), n - height)
        elif 2 <= n < height:
            src, at = (pa_ref, ia), n - 2
        else:
            src, at = (pb_ref, ib), n if n < 2 else n - height + 2
        incoming = src[1][at * across : (at + 1) * across, :]
        for f in range(frames):
            slot = (n * frames + f) % rowbuf.shape[0]
            rowbuf[slot, 8 : 8 + across, :] = src[0][at, f] + running[f] * incoming
            corner = (n // 2) * 4
            h = n % 2
            rowbuf[slot, 7:8, :] = sc[f, h, corner : corner + 1, :]
            rowbuf[slot, 8:9, :] = sc[f, h, corner + 1 : corner + 2, :]
            rowbuf[slot, 7 + across : 8 + across, :] = sc[f, h, corner + 2 : corner + 3, :]
            rowbuf[slot, 8 + across : 9 + across, :] = sc[f, h, corner + 3 : corner + 4, :]
            three_taps(rowbuf, slot, x3, n, f, rowbuf[slot, 8 : 8 + across, :].astype(BF16))
    for p in range(height // 2):
        slots = [n if n > 0 or not two else None for n in range(2 * p, 2 * p + 4)]
        y = pair_dot(x3, slots, wt)
        for rr in range(2):
            r = 2 * p + rr
            natural = jnp.where(flip == 1, height - 1 - r, r)
            for f in range(frames):
                mixed = y[f * across : (f + 1) * across, rr * chan : (rr + 1) * chan]
                out_ref[f, natural] = (frames_ref[f, natural].astype(F32) + jax.nn.gelu(mixed)).astype(BF16)


def call(body, outs, scratch, flops, args):
    return pl.pallas_call(
        body,
        out_shape=outs,
        in_specs=[VMEM] * len(args),
        out_specs=jax.tree.map(lambda _: VMEM, outs),
        scratch_shapes=scratch,
        compiler_params=pltpu.CompilerParams(vmem_limit_bytes=32 * 2**20),
        cost_estimate=pl.CostEstimate(flops=flops, bytes_accessed=4 * 2**20, transcendentals=0),
    )(*[pltpu.with_memory_space_constraint(a, pltpu.VMEM) for a in args])


def mirrored(two):
    return lax.axis_index("gx") if two else 0


def forward(ends):
    return [(i, i + 1) for i in range(ends - 1)]


def backward(ends):
    return [(i + 1, i) for i in range(ends - 1)]


def carry_general(locals_, total, ta):
    step = 1
    while step < ta:
        pairs = [(i, i + step) for i in range(ta - step)]
        moved = [lax.ppermute(v, "ta", pairs) for v in locals_]
        moved_total = lax.ppermute(total, "ta", pairs)
        has = lax.axis_index("ta") >= step
        locals_ = [(v.astype(F32) + total * m.astype(F32)).astype(BF16) for v, m in zip(locals_, moved)]
        total = jnp.where(has, total * moved_total, total)
        step *= 2
    return [lax.ppermute(v, "ta", forward(ta)) for v in locals_]


def on_device(gx, gy, ta, frames, in_weight, out_weight, decays):
    n_frames, height, across, chan = frames.shape
    two = gx == 2
    x, t = lax.axis_index("gx"), lax.axis_index("ta")

    cols = jnp.concatenate([frames[:, :, :2], frames[:, :, across - 2 :]], axis=2)
    cols = cols.transpose(1, 2, 0, 3).reshape(height, 4 * n_frames, chan)
    if two:
        swap = [(0, 1), (1, 0)]
        start = jnp.where(x == 1, 0, height - 2)
        halo = lax.ppermute(lax.dynamic_slice_in_dim(frames, start, 2, axis=1), "gx", swap)
        corner = lax.ppermute(lax.dynamic_slice_in_dim(cols, start, 2, axis=0), "gx", swap)
        cols = jnp.where(x == 1, jnp.concatenate([corner, cols]), jnp.concatenate([cols, corner]))
    else:
        above = lax.ppermute(frames[:, height - 2 :], "gx", forward(gx))
        below = lax.ppermute(frames[:, :2], "gx", backward(gx))
        halo = jnp.concatenate([above, below], axis=1)
        over = lax.ppermute(cols[height - 2 :], "gx", forward(gx))
        under = lax.ppermute(cols[:2], "gx", backward(gx))
        cols = jnp.concatenate([over, cols, under])

    rows_a = height - 1 if two else height - 2
    rows_b = 2 if two else 4
    wt = pltpu.VMEM((12 * chan, 2 * chan), BF16)
    rowbuf = pltpu.VMEM((16, across + 16, chan), F32)
    cells = n_frames * across
    flops = 2 * 9 * chan * chan * cells
    near_mem = pltpu.VMEM
    pa, fa = call(
        functools.partial(inner_kernel, two),
        (near_mem((rows_a, n_frames, across, chan), F32), near_mem((rows_a * across + 16, chan), BF16)),
        [wt, rowbuf, pltpu.VMEM((height, cells, 3 * chan), BF16)],
        flops * height, [frames, in_weight, decays],
    )

    left = lax.ppermute(cols[:, 2 * n_frames :], "gy", forward(gy))
    right = lax.ppermute(cols[:, : 2 * n_frames], "gy", backward(gy))
    n_cols = (height // 2 + 1) * 4
    pb, pc, fb = call(
        functools.partial(edge_kernel, two, gx, gy),
        (
            near_mem((rows_b, n_frames, across, chan), F32),
            near_mem((2, n_cols * n_frames, chan), F32),
            near_mem((rows_b * across + 64, chan), BF16),
        ),
        [
            wt, rowbuf, pltpu.VMEM((2 * rows_b, cells, 3 * chan), BF16),
            pltpu.VMEM((n_cols * n_frames, 12 * chan), BF16), pltpu.VMEM((2, n_cols * n_frames, chan), F32),
        ],
        flops * rows_b, [frames, halo, cols, left, right, in_weight, decays],
    )

    total = jnp.prod(decays, axis=0)[None]
    if ta == 4:
        near, far = [(0, 1), (1, 0), (2, 3)], [(1, 2), (0, 3)]
        ra = lax.ppermute(fa, "ta", near)
        other = jnp.sum(ra[rows_a * across :].astype(F32), axis=0, keepdims=True)

        def joined(mine, theirs):
            mine, theirs = mine.astype(F32), theirs.astype(F32)
            return jnp.where(t == 0, theirs + other * mine, mine + total * theirs).astype(BF16)

        za = lax.ppermute(joined(fa, ra), "ta", far)
        rb = lax.ppermute(fb, "ta", near)
        zb = lax.ppermute(joined(fb, rb), "ta", far)
    else:
        ra, rb = carry_general([fa, fb], total, ta)
        za, zb = ra, rb

    return call(
        functools.partial(outer_kernel, two, ta),
        jax.ShapeDtypeStruct(frames.shape, BF16),
        [
            wt, rowbuf, pltpu.VMEM((height + 2, cells, 3 * chan), BF16),
            pltpu.VMEM((n_frames, 2, (n_cols + 7) // 8 * 8, chan), F32),
            pltpu.VMEM((rows_a * across, chan), F32), pltpu.VMEM((rows_b * across + 64, chan), F32),
        ],
        flops * height, [frames, pa, pb, pc, ra, za, rb, zb, out_weight, decays],
    )


def solution(mesh):
    sizes = [mesh.shape[a] for a in ("gx", "gy", "ta")]
    placed = (P("ta", "gx", "gy", None), P(), P(), P("ta", None))
    return jax.shard_map(
        functools.partial(on_device, *sizes), mesh=mesh, in_specs=placed,
        out_specs=P("ta", "gx", "gy", None), check_vma=False,
    )
```

```python
import functools

import jax
import jax.numpy as jnp
from jax import lax
from jax.experimental import pallas as pl
from jax.experimental.pallas import tpu as pltpu
from jax.sharding import PartitionSpec as P

F32, BF16 = jnp.float32, jnp.bfloat16
VMEM = pl.BlockSpec(memory_space=pltpu.VMEM)
HBM = pl.BlockSpec(memory_space=pltpu.HBM)


def pair_weights(w_ref, wt, flip):
    chan_in, chan_out = w_ref.shape[2:]
    for k in range(4):
        for b in range(3):
            for rr in range(2):
                at = (k * 3 + b) * chan_in
                a = k - rr
                if 0 <= a <= 2:
                    block = w_ref[jnp.where(flip == 1, 2 - a, a), b]
                else:
                    block = jnp.zeros((chan_in, chan_out), BF16)
                wt[at : at + chan_in, rr * chan_out : (rr + 1) * chan_out] = block


def clear_margins(rowbuf):
    across = rowbuf.shape[1] - 16
    zeros = jnp.zeros((rowbuf.shape[0], 8, rowbuf.shape[2]), F32)
    rowbuf[:, 0:8, :] = zeros
    rowbuf[:, 8 + across : 16 + across, :] = zeros


def three_taps(rowbuf, slot, x3, row, f, middle):
    across = rowbuf.shape[1] - 16
    chan = rowbuf.shape[2]
    at = pl.ds(f * across, across)
    x3[row, at, 0:chan] = rowbuf[slot, 7 : 7 + across, :].astype(BF16)
    x3[row, at, chan : 2 * chan] = middle
    x3[row, at, 2 * chan : 3 * chan] = rowbuf[slot, 9 : 9 + across, :].astype(BF16)


def pair_dot(x3, slots, wt):
    width = x3.shape[2]
    first = next(k for k in range(4) if slots[k] is not None)
    rows = jnp.concatenate([x3[s] for s in slots[first:]], axis=1)
    return jnp.dot(rows, wt[first * width : 4 * width, :], preferred_element_type=F32)


def scan_rows(y, decays, scales, across, keep):
    frames = decays.shape[0]
    chan = decays.shape[1]
    finals = []
    for rr in range(2):
        s = None
        for f in range(frames):
            u = scales[f : f + 1] * y[f * across : (f + 1) * across, rr * chan : (rr + 1) * chan]
            s = u if s is None else decays[f : f + 1] * s + u
            keep(rr, f, s)
        finals.append(s)
    return finals


def load_decays(dec_ref):
    decays = dec_ref[...]
    return decays, jnp.sqrt(1.0 - decays * decays)


def fetch_kernel(frames_hbm, w_in_hbm, w_out_hbm, dec_hbm, frames_ref, w_in_ref, w_out_ref, dec_ref, cols_ref, edge, sems):
    pairs = [(frames_hbm, frames_ref), (dec_hbm, dec_ref), (w_in_hbm, w_in_ref), (w_out_hbm, w_out_ref)]
    copies = [pltpu.make_async_copy(src, dst, sems.at[i]) for i, (src, dst) in enumerate(pairs)]
    for copy in copies:
        copy.start()
    copies[0].wait()
    frames, height, across, chan = frames_ref.shape
    for r in range(height):
        for f in range(frames):
            at = r * 4 * frames + f
            edge[pl.ds(at, 2, stride=frames), :] = frames_ref[f, r, 0:16, :].astype(F32)[0:2]
            last = frames_ref[f, r, across - 16 : across, :].astype(F32)[14:16]
            edge[pl.ds(at + 2 * frames, 2, stride=frames), :] = last
    for r in range(height):
        cols_ref[r] = edge[r * 4 * frames : (r + 1) * 4 * frames, :].astype(BF16)
    for copy in copies[1:]:
        copy.wait()


def inner_kernel(two, frames_ref, w_ref, dec_ref, p_ref, f_ref, wt, rowbuf, x3):
    frames, height, across, chan = frames_ref.shape
    flip = mirrored(two)
    pair_weights(w_ref, wt, flip)
    clear_margins(rowbuf)
    decays, scales = load_decays(dec_ref)
    for r in range(height):
        natural = jnp.where(flip == 1, height - 1 - r, r)
        for f in range(frames):
            slot = (r * frames + f) % rowbuf.shape[0]
            x = frames_ref[f, natural]
            rowbuf[slot, 8 : 8 + across, :] = x.astype(F32)
            three_taps(rowbuf, slot, x3, r, f, x)
    first, first_row = (0, 1) if two else (1, 0)
    for p in range(first, height // 2):
        slots = [r if r >= 0 else None for r in range(2 * p - 2, 2 * p + 2)]
        y = pair_dot(x3, slots, wt)
        base = 2 * (p - first)

        def keep(rr, f, s, base=base):
            if base + rr >= first_row:
                p_ref[base + rr - first_row, f] = s

        for rr, s in enumerate(scan_rows(y, decays, scales, across, keep)):
            at = base + rr - first_row
            if at >= 0:
                f_ref[at * across : (at + 1) * across, :] = s.astype(BF16)
    total = decays[0:1]
    for f in range(1, frames):
        total = total * decays[f : f + 1]
    high = total.astype(BF16)
    rest = total - high.astype(F32)
    middle = rest.astype(BF16)
    low = rest - middle.astype(F32)
    row = lax.broadcasted_iota(jnp.int32, (16, chan), 0)
    parts = jnp.where(row == 0, high.astype(F32), jnp.where(row == 1, middle.astype(F32), jnp.where(row == 2, low, 0.0)))
    end = f_ref.shape[0]
    f_ref[end - 16 : end, :] = parts.astype(BF16)


def edge_kernel(
    two, gx, gy, frames_ref, halo_ref, e_ref, l_ref, r_ref, wt, dec_ref, w_next,
    p_ref, pc_ref, f_ref, wt_next, rowbuf, x3, xc, yc,
):
    frames, height, across, chan = frames_ref.shape
    flip = mirrored(two)
    x, y_at = lax.axis_index("gx"), lax.axis_index("gy")
    has_left, has_right = (y_at > 0).astype(F32), (y_at < gy - 1).astype(F32)
    has_above, has_below = (x > 0).astype(F32), (x < gx - 1).astype(F32)
    pair_weights(w_next, wt_next, flip)
    clear_margins(rowbuf)
    decays, scales = load_decays(dec_ref)
    pairs = [height // 2] if two else [0, height // 2]
    for i, p in enumerate(pairs):
        for k in range(4):
            r = 2 * p - 2 + k
            for f in range(frames):
                slot = (k * frames + f) % rowbuf.shape[0]
                if 0 <= r < height:
                    x = frames_ref[f, jnp.where(flip == 1, height - 1 - r, r)]
                elif two:
                    x = halo_ref[f, jnp.where(flip == 1, 1 - (r - height), r - height)]
                else:
                    x = halo_ref[f, r + 2 if r < 0 else r - height + 2]
                rowbuf[slot, 8 : 8 + across, :] = x.astype(F32)
                three_taps(rowbuf, slot, x3, i * 4 + k, f, x)
        y = pair_dot(x3, [i * 4 + k for k in range(4)], wt)
        inside = 1.0
        if not two:
            inside = has_above if p == 0 else has_below

        def keep(rr, f, s, i=i, p=p, inside=inside):
            border = (rr == 0) if p == 0 else (rr == 1)
            p_ref[2 * i + rr, f] = s * inside if border and not two else s

        for rr, s in enumerate(scan_rows(y, decays, scales, across, keep)):
            border = (rr == 0) if p == 0 else (rr == 1)
            s = s * inside if border and not two else s
            f_ref[(2 * i + rr) * across : (2 * i + rr + 1) * across, :] = s.astype(BF16)

    n_pairs = height // 2 + 1
    for p in range(n_pairs):
        for k in range(4):
            r = 2 * p - 2 + k
            if two:
                at = None if r < 0 else jnp.where(flip == 1, height + 1 - r, r)
            else:
                at = r + 2
            to = slice(p * 4 * frames, (p + 1) * 4 * frames)
            lanes = k * 3 * chan
            if at is None:
                xc[to, lanes : lanes + 3 * chan] = jnp.zeros((4 * frames, 3 * chan), BF16)
                continue
            own = e_ref[at].astype(F32)
            left = l_ref[at].astype(F32)
            right = r_ref[at].astype(F32)
            cols = [left[:frames], left[frames:]] + [own[c * frames : (c + 1) * frames] for c in range(4)]
            cols += [right[:frames], right[frames:]]
            for b in range(3):
                piece = jnp.concatenate([cols[c + b] for c in (0, 1, 4, 5)], axis=0)
                xc[to, lanes + b * chan : lanes + (b + 1) * chan] = piece.astype(BF16)
    edge = jnp.dot(xc[...], wt[...], preferred_element_type=F32)
    for h in range(2):
        yc[h] = edge[:, h * chan : (h + 1) * chan]
    count = n_pairs * 4
    place = lax.broadcasted_iota(jnp.int32, (count, 2 * chan), 0)
    lane = lax.broadcasted_iota(jnp.int32, (count, 2 * chan), 1)
    mask = jnp.where(place % 4 == 0, has_left, jnp.where(place % 4 == 3, has_right, 1.0))
    above = (place < 4) & (lane < chan)
    if two:
        mask = jnp.where(above, 0.0, mask)
    else:
        below = (place >= count - 4) & (lane >= chan)
        mask = jnp.where(above, mask * has_above, mask)
        mask = jnp.where(below, mask * has_below, mask)
    s = None
    for f in range(frames):
        both = [jnp.concatenate([v[f : f + 1]] * 2, axis=1) for v in (decays, scales)]
        halves = [yc[h, pl.ds(f, count, stride=frames), :] for h in range(2)]
        u = both[1] * jnp.concatenate(halves, axis=1) * mask
        s = u if s is None else both[0] * s + u
        for h in range(2):
            pc_ref[h, pl.ds(f, count, stride=frames), :] = s[:, h * chan : (h + 1) * chan]
    base = len(pairs) * 2 * across
    pad = jnp.zeros((32 - count, chan), F32)
    for h in range(2):
        half = jnp.concatenate([s[:, h * chan : (h + 1) * chan], pad], axis=0)
        f_ref[base + 32 * h : base + 32 * (h + 1), :] = half.astype(BF16)


def outer_kernel(
    two, ta, frames_ref, pa_ref, pb_ref, pc_ref, ra_ref, za_ref, rb_ref, zb_ref, wt, dec_ref,
    out_ref, rowbuf, x3, sc, ia, ib, done, sems,
):
    frames, height, across, chan = frames_ref.shape
    flip = mirrored(two)
    decays = dec_ref[...]
    rows_a = pa_ref.shape[0]
    if ta == 4:
        t = lax.axis_index("ta")
        end = ra_ref.shape[0]
        other = jnp.sum(ra_ref[end - 16 : end, :].astype(F32), axis=0, keepdims=True)
        alpha = ((t == 1) | (t == 3)).astype(F32)
        beta = jnp.where(t == 3, other, (t == 2).astype(F32))
    else:
        alpha, beta = 1.0, 0.0
    ia[...] = alpha * ra_ref[0 : rows_a * across].astype(F32) + beta * za_ref[0 : rows_a * across].astype(F32)
    ib[...] = alpha * rb_ref[...].astype(F32) + beta * zb_ref[...].astype(F32)
    running = [decays[0:1]]
    for f in range(1, frames):
        running.append(running[-1] * decays[f : f + 1])
    count = (height // 2 + 1) * 4
    base = pb_ref.shape[0] * across
    for f in range(frames):
        for h in range(2):
            part = pc_ref[h, pl.ds(f, count, stride=frames), :]
            sc[f, h, 0:count, :] = part + running[f] * ib[base + 32 * h : base + 32 * h + count, :]
    for n in range(height + 2):
        if two and n == 0:
            continue
        if two:
            src, at = ((pa_ref, ia), n - 1) if n < height else ((pb_ref, ib), n - height)
        elif 2 <= n < height:
            src, at = (pa_ref, ia), n - 2
        else:
            src, at = (pb_ref, ib), n if n < 2 else n - height + 2
        incoming = src[1][at * across : (at + 1) * across, :]
        for f in range(frames):
            slot = (n * frames + f) % rowbuf.shape[0]
            rowbuf[slot, 8 : 8 + across, :] = src[0][at, f] + running[f] * incoming
            corner = (n // 2) * 4
            h = n % 2
            rowbuf[slot, 7:8, :] = sc[f, h, corner : corner + 1, :]
            rowbuf[slot, 8:9, :] = sc[f, h, corner + 1 : corner + 2, :]
            rowbuf[slot, 7 + across : 8 + across, :] = sc[f, h, corner + 2 : corner + 3, :]
            rowbuf[slot, 8 + across : 9 + across, :] = sc[f, h, corner + 3 : corner + 4, :]
            three_taps(rowbuf, slot, x3, n, f, rowbuf[slot, 8 : 8 + across, :].astype(BF16))
    copies = []
    for p in range(height // 2):
        slots = [n if n > 0 or not two else None for n in range(2 * p, 2 * p + 4)]
        y = pair_dot(x3, slots, wt)
        first = jnp.where(flip == 1, height - 2 - 2 * p, 2 * p)
        for rr in range(2):
            row = jnp.where(flip == 1, 1 - rr, rr)
            for f in range(frames):
                mixed = y[f * across : (f + 1) * across, rr * chan : (rr + 1) * chan]
                frame = frames_ref[f, first + row].astype(F32)
                done[p, f, row] = (frame + jax.nn.gelu(mixed)).astype(BF16)
        copies.append(pltpu.make_async_copy(done.at[p], out_ref.at[:, pl.ds(first, 2)], sems.at[p]))
        copies[-1].start()
    for copy in copies:
        copy.wait()


def call(body, outs, scratch, flops, args, place=(VMEM, VMEM)):
    args = [pltpu.with_memory_space_constraint(a, place[0].memory_space) for a in args]
    return pl.pallas_call(
        body,
        out_shape=outs,
        in_specs=[place[0]] * len(args),
        out_specs=jax.tree.map(lambda _: place[1], outs),
        scratch_shapes=scratch,
        compiler_params=pltpu.CompilerParams(vmem_limit_bytes=32 * 2**20),
        cost_estimate=pl.CostEstimate(flops=flops, bytes_accessed=4 * 2**20, transcendentals=0),
    )(*args)


def mirrored(two):
    return lax.axis_index("gx") if two else 0


def swapped(value, axis, count, odd_first):
    off = 1 if odd_first else 0
    pairs = [((i + off) % count, (i + 1 + off) % count) for i in range(0, count, 2)]
    return lax.ppermute(value, axis, pairs + [(b, a) for a, b in pairs])


def exchange(low, high, axis, count):
    if count % 2:
        up = lax.ppermute(high, axis, [(i, i + 1) for i in range(count - 1)])
        return up, lax.ppermute(low, axis, [(i + 1, i) for i in range(count - 1)])
    at = lax.axis_index(axis)
    odd = at % 2 == 1
    near = swapped(jnp.where(odd, low, high), axis, count, False)
    if count == 2:
        far = jnp.zeros_like(near)
    else:
        far = swapped(jnp.where(odd, high, low), axis, count, True)
        far = jnp.where((at == 0) | (at == count - 1), jnp.zeros_like(far), far)
    return jnp.where(odd, near, far), jnp.where(odd, far, near)


def carry_general(locals_, total, ta):
    t = lax.axis_index("ta")

    def moved(value, step):
        got = lax.ppermute(value, "ta", [(i, (i + step) % ta) for i in range(ta)])
        return jnp.where(t >= step, got, jnp.zeros_like(got))

    step = 1
    while step < ta:
        came = [moved(v, step) for v in locals_]
        locals_ = [(v.astype(F32) + total * m.astype(F32)).astype(BF16) for v, m in zip(locals_, came)]
        total = jnp.where(t >= step, total * moved(total, step), total)
        step *= 2
    return [moved(v, 1) for v in locals_]


def on_device(gx, gy, ta, frames, in_weight, out_weight, decays):
    n_frames, height, across, chan = frames.shape
    two = gx == 2
    x, t = lax.axis_index("gx"), lax.axis_index("ta")
    near_mem = pltpu.VMEM
    frames, in_weight, out_weight, decays, cols = call(
        fetch_kernel,
        (
            near_mem(frames.shape, BF16), near_mem(in_weight.shape, BF16), near_mem(out_weight.shape, BF16),
            near_mem(decays.shape, F32), near_mem((height, 4 * n_frames, chan), BF16),
        ),
        [pltpu.VMEM((height * 4 * n_frames, chan), F32), pltpu.SemaphoreType.DMA((4,))],
        0, [frames, in_weight, out_weight, decays], (HBM, VMEM),
    )
    if two:
        start = jnp.where(x == 1, 0, height - 2)
        corner = swapped(lax.dynamic_slice_in_dim(cols, start, 2, axis=0), "gx", 2, False)
        halo = swapped(lax.dynamic_slice_in_dim(frames, start, 2, axis=1), "gx", 2, False)
        cols = jnp.where(x == 1, jnp.concatenate([corner, cols]), jnp.concatenate([cols, corner]))
    else:
        over, under = exchange(cols[:2], cols[height - 2 :], "gx", gx)
        cols = jnp.concatenate([over, cols, under])
        above, below = exchange(frames[:, :2], frames[:, height - 2 :], "gx", gx)
        halo = jnp.concatenate([above, below], axis=1)

    rows_a = height - 1 if two else height - 2
    rows_b = 2 if two else 4
    wide = (12 * chan, 2 * chan)
    rowbuf = pltpu.VMEM((16, across + 16, chan), F32)
    cells = n_frames * across
    flops = 2 * 9 * chan * chan * cells
    pa, fa, wt_in = call(
        functools.partial(inner_kernel, two),
        (
            near_mem((rows_a, n_frames, across, chan), F32), near_mem((rows_a * across + 16, chan), BF16),
            near_mem(wide, BF16),
        ),
        [rowbuf, pltpu.VMEM((height, cells, 3 * chan), BF16)],
        flops * height, [frames, in_weight, decays],
    )

    cols, fa = lax.optimization_barrier((cols, fa))
    left, right = exchange(cols[:, : 2 * n_frames], cols[:, 2 * n_frames :], "gy", gy)
    total = jnp.prod(decays, axis=0)[None]
    if ta == 4:
        ra = swapped(fa, "ta", ta, False)
        other = jnp.sum(ra[rows_a * across :].astype(F32), axis=0, keepdims=True)

        def joined(mine, theirs):
            mine, theirs = mine.astype(F32), theirs.astype(F32)
            return jnp.where(t == 0, theirs + other * mine, mine + total * theirs).astype(BF16)

        across_two = [(0, 2), (2, 0), (1, 3), (3, 1)]
        left, right, ga = lax.optimization_barrier((left, right, joined(fa, ra)))
        za = lax.ppermute(ga, "ta", across_two)

    n_cols = (height // 2 + 1) * 4
    pb, pc, fb, wt_out = call(
        functools.partial(edge_kernel, two, gx, gy),
        (
            near_mem((rows_b, n_frames, across, chan), F32),
            near_mem((2, n_cols * n_frames, chan), F32),
            near_mem((rows_b * across + 64, chan), BF16),
            near_mem(wide, BF16),
        ),
        [
            rowbuf, pltpu.VMEM((2 * rows_b, cells, 3 * chan), BF16),
            pltpu.VMEM((n_cols * n_frames, 12 * chan), BF16), pltpu.VMEM((2, n_cols * n_frames, chan), F32),
        ],
        flops * rows_b, [frames, halo, cols, left, right, wt_in, decays, out_weight],
    )

    if ta == 4:
        rb = swapped(fb, "ta", ta, False)
        zb = lax.ppermute(joined(fb, rb), "ta", across_two)
    else:
        ra, rb = carry_general([fa, fb], total, ta)
        za, zb = ra, rb

    return call(
        functools.partial(outer_kernel, two, ta),
        jax.ShapeDtypeStruct(frames.shape, BF16),
        [
            rowbuf, pltpu.VMEM((height + 2, cells, 3 * chan), BF16),
            pltpu.VMEM((n_frames, 2, (n_cols + 7) // 8 * 8, chan), F32),
            pltpu.VMEM((rows_a * across, chan), F32), pltpu.VMEM((rows_b * across + 64, chan), F32),
            pltpu.VMEM((height // 2, n_frames, 2, across, chan), BF16), pltpu.SemaphoreType.DMA((height // 2,)),
        ],
        flops * height, [frames, pa, pb, pc, ra, za, rb, zb, wt_out, decays], (VMEM, HBM),
    )


def solution(mesh):
    sizes = [mesh.shape[a] for a in ("gx", "gy", "ta")]
    placed = (P("ta", "gx", "gy", None), P(), P(), P("ta", None))
    return jax.shard_map(
        functools.partial(on_device, *sizes), mesh=mesh, in_specs=placed,
        out_specs=P("ta", "gx", "gy", None), check_vma=False,
    )
```

```python
import functools

import jax
import jax.numpy as jnp
from jax import lax
from jax.experimental import pallas as pl
from jax.experimental.pallas import tpu as pltpu
from jax.sharding import PartitionSpec as P

F32, BF16 = jnp.float32, jnp.bfloat16
VMEM = pl.BlockSpec(memory_space=pltpu.VMEM)
HBM = pl.BlockSpec(memory_space=pltpu.HBM)


def pair_weights(w_ref, wt, flip):
    chan_in, chan_out = w_ref.shape[2:]
    for k in range(4):
        for b in range(3):
            for rr in range(2):
                at = (k * 3 + b) * chan_in
                a = k - rr
                if 0 <= a <= 2:
                    block = w_ref[jnp.where(flip == 1, 2 - a, a), b]
                else:
                    block = jnp.zeros((chan_in, chan_out), BF16)
                wt[at : at + chan_in, rr * chan_out : (rr + 1) * chan_out] = block


def clear_margins(rowbuf):
    across = rowbuf.shape[1] - 16
    zeros = jnp.zeros((rowbuf.shape[0], 8, rowbuf.shape[2]), F32)
    rowbuf[:, 0:8, :] = zeros
    rowbuf[:, 8 + across : 16 + across, :] = zeros


def three_taps(rowbuf, slot, x3, row, f, middle):
    across = rowbuf.shape[1] - 16
    chan = rowbuf.shape[2]
    at = pl.ds(f * across, across)
    x3[row, at, 0:chan] = rowbuf[slot, 7 : 7 + across, :].astype(BF16)
    x3[row, at, chan : 2 * chan] = middle
    x3[row, at, 2 * chan : 3 * chan] = rowbuf[slot, 9 : 9 + across, :].astype(BF16)


def pair_dot(x3, slots, wt):
    width = x3.shape[2]
    first = next(k for k in range(4) if slots[k] is not None)
    rows = jnp.concatenate([x3[s] for s in slots[first:]], axis=1)
    return jnp.dot(rows, wt[first * width : 4 * width, :], preferred_element_type=F32)


def scan_rows(y, decays, scales, across, keep):
    frames = decays.shape[0]
    chan = decays.shape[1]
    finals = []
    for rr in range(2):
        s = None
        for f in range(frames):
            u = scales[f : f + 1] * y[f * across : (f + 1) * across, rr * chan : (rr + 1) * chan]
            s = u if s is None else decays[f : f + 1] * s + u
            keep(rr, f, s)
        finals.append(s)
    return finals


def load_decays(dec_ref):
    decays = dec_ref[...]
    return decays, jnp.sqrt(1.0 - decays * decays)


def gather_edges(src, row, edge, at):
    frames, across = src.shape[0], src.shape[2]
    for f in range(frames):
        edge[pl.ds(at + f, 2, stride=frames), :] = src[f, row, 0:16, :].astype(F32)[0:2]
        last = src[f, row, across - 16 : across, :].astype(F32)[14:16]
        edge[pl.ds(at + f + 2 * frames, 2, stride=frames), :] = last


def fetch_kernel(frames_hbm, w_in_hbm, w_out_hbm, dec_hbm, frames_ref, w_in_ref, w_out_ref, dec_ref, cols_ref, edge, sems):
    pairs = [(frames_hbm, frames_ref), (dec_hbm, dec_ref), (w_in_hbm, w_in_ref), (w_out_hbm, w_out_ref)]
    copies = [pltpu.make_async_copy(src, dst, sems.at[i]) for i, (src, dst) in enumerate(pairs)]
    for copy in copies:
        copy.start()
    copies[0].wait()
    frames, height, across, chan = frames_ref.shape
    for r in range(height):
        gather_edges(frames_ref, r, edge, r * 4 * frames)
    for r in range(height):
        cols_ref[r] = edge[r * 4 * frames : (r + 1) * 4 * frames, :].astype(BF16)
    for copy in copies[1:]:
        copy.wait()


def inner_kernel(two, frames_ref, w_ref, dec_ref, p_ref, f_ref, wt, rowbuf, x3):
    frames, height, across, chan = frames_ref.shape
    flip = mirrored(two)
    pair_weights(w_ref, wt, flip)
    clear_margins(rowbuf)
    decays, scales = load_decays(dec_ref)
    for r in range(height):
        natural = jnp.where(flip == 1, height - 1 - r, r)
        for f in range(frames):
            slot = (r * frames + f) % rowbuf.shape[0]
            x = frames_ref[f, natural]
            rowbuf[slot, 8 : 8 + across, :] = x.astype(F32)
            three_taps(rowbuf, slot, x3, r, f, x)
    first, first_row = (0, 1) if two else (1, 0)
    for p in range(first, height // 2):
        slots = [r if r >= 0 else None for r in range(2 * p - 2, 2 * p + 2)]
        y = pair_dot(x3, slots, wt)
        base = 2 * (p - first)

        def keep(rr, f, s, base=base):
            if base + rr >= first_row:
                p_ref[base + rr - first_row, f] = s

        for rr, s in enumerate(scan_rows(y, decays, scales, across, keep)):
            at = base + rr - first_row
            if at >= 0:
                f_ref[at * across : (at + 1) * across, :] = s.astype(BF16)
    total = decays[0:1]
    for f in range(1, frames):
        total = total * decays[f : f + 1]
    high = total.astype(BF16)
    rest = total - high.astype(F32)
    middle = rest.astype(BF16)
    low = rest - middle.astype(F32)
    row = lax.broadcasted_iota(jnp.int32, (16, chan), 0)
    parts = jnp.where(row == 0, high.astype(F32), jnp.where(row == 1, middle.astype(F32), jnp.where(row == 2, low, 0.0)))
    end = f_ref.shape[0]
    f_ref[end - 16 : end, :] = parts.astype(BF16)


def edge_kernel(two, gx, gy, frames_ref, halo_ref, wt, dec_ref, w_next, e_ref, l_ref, r_ref, *refs):
    *corner_refs, p_ref, pc_ref, f_ref, wt_next, rowbuf, x3, xc, yc, edge = refs
    frames, height, across, chan = frames_ref.shape
    flip = mirrored(two)
    x, y_at = lax.axis_index("gx"), lax.axis_index("gy")
    has_left, has_right = (y_at > 0).astype(F32), (y_at < gy - 1).astype(F32)
    has_above, has_below = (x > 0).astype(F32), (x < gx - 1).astype(F32)
    pair_weights(w_next, wt_next, flip)
    clear_margins(rowbuf)
    decays, scales = load_decays(dec_ref)
    pairs = [height // 2] if two else [0, height // 2]
    for i, p in enumerate(pairs):
        for k in range(4):
            r = 2 * p - 2 + k
            for f in range(frames):
                slot = (k * frames + f) % rowbuf.shape[0]
                if 0 <= r < height:
                    x = frames_ref[f, jnp.where(flip == 1, height - 1 - r, r)]
                elif two:
                    x = halo_ref[f, jnp.where(flip == 1, 1 - (r - height), r - height)]
                else:
                    x = halo_ref[f, r + 2 if r < 0 else r - height + 2]
                rowbuf[slot, 8 : 8 + across, :] = x.astype(F32)
                three_taps(rowbuf, slot, x3, i * 4 + k, f, x)
        y = pair_dot(x3, [i * 4 + k for k in range(4)], wt)
        inside = 1.0
        if not two:
            inside = has_above if p == 0 else has_below

        def keep(rr, f, s, i=i, p=p, inside=inside):
            border = (rr == 0) if p == 0 else (rr == 1)
            p_ref[2 * i + rr, f] = s * inside if border and not two else s

        for rr, s in enumerate(scan_rows(y, decays, scales, across, keep)):
            border = (rr == 0) if p == 0 else (rr == 1)
            s = s * inside if border and not two else s
            f_ref[(2 * i + rr) * across : (2 * i + rr + 1) * across, :] = s.astype(BF16)

    n_pairs = height // 2 + 1
    if two:
        for i in range(2):
            gather_edges(halo_ref, jnp.where(flip == 1, 1 - i, i), edge, i * 4 * frames)
    for p in range(n_pairs):
        for k in range(4):
            r = 2 * p - 2 + k
            to = slice(p * 4 * frames, (p + 1) * 4 * frames)
            lanes = k * 3 * chan
            if two and r < 0:
                xc[to, lanes : lanes + 3 * chan] = jnp.zeros((4 * frames, 3 * chan), BF16)
                continue
            if two and r >= height:
                at = jnp.where(flip == 1, 1 - (r - height), r - height)
                own = edge[(r - height) * 4 * frames : (r - height + 1) * 4 * frames, :]
                left, right = (ref[at].astype(F32) for ref in corner_refs)
            else:
                at = jnp.where(flip == 1, height - 1 - r, r) if two else r + 2
                own, left, right = (ref[at].astype(F32) for ref in (e_ref, l_ref, r_ref))
            cols = [left[:frames], left[frames:]] + [own[c * frames : (c + 1) * frames] for c in range(4)]
            cols += [right[:frames], right[frames:]]
            for b in range(3):
                piece = jnp.concatenate([cols[c + b] for c in (0, 1, 4, 5)], axis=0)
                xc[to, lanes + b * chan : lanes + (b + 1) * chan] = piece.astype(BF16)
    edge = jnp.dot(xc[...], wt[...], preferred_element_type=F32)
    for h in range(2):
        yc[h] = edge[:, h * chan : (h + 1) * chan]
    count = n_pairs * 4
    place = lax.broadcasted_iota(jnp.int32, (count, 2 * chan), 0)
    lane = lax.broadcasted_iota(jnp.int32, (count, 2 * chan), 1)
    mask = jnp.where(place % 4 == 0, has_left, jnp.where(place % 4 == 3, has_right, 1.0))
    above = (place < 4) & (lane < chan)
    if two:
        mask = jnp.where(above, 0.0, mask)
    else:
        below = (place >= count - 4) & (lane >= chan)
        mask = jnp.where(above, mask * has_above, mask)
        mask = jnp.where(below, mask * has_below, mask)
    s = None
    for f in range(frames):
        both = [jnp.concatenate([v[f : f + 1]] * 2, axis=1) for v in (decays, scales)]
        halves = [yc[h, pl.ds(f, count, stride=frames), :] for h in range(2)]
        u = both[1] * jnp.concatenate(halves, axis=1) * mask
        s = u if s is None else both[0] * s + u
        for h in range(2):
            pc_ref[h, pl.ds(f, count, stride=frames), :] = s[:, h * chan : (h + 1) * chan]
    base = len(pairs) * 2 * across
    pad = jnp.zeros((32 - count, chan), F32)
    for h in range(2):
        half = jnp.concatenate([s[:, h * chan : (h + 1) * chan], pad], axis=0)
        f_ref[base + 32 * h : base + 32 * (h + 1), :] = half.astype(BF16)


def outer_kernel(
    two, ta, frames_ref, pa_ref, pb_ref, pc_ref, ra_ref, za_ref, rb_ref, zb_ref, wt, dec_ref,
    out_ref, rowbuf, x3, sc, ia, ib, done, sems,
):
    frames, height, across, chan = frames_ref.shape
    flip = mirrored(two)
    decays = dec_ref[...]
    rows_a = pa_ref.shape[0]
    if ta == 4:
        t = lax.axis_index("ta")
        end = ra_ref.shape[0]
        other = jnp.sum(ra_ref[end - 16 : end, :].astype(F32), axis=0, keepdims=True)
        alpha = ((t == 1) | (t == 3)).astype(F32)
        beta = jnp.where(t == 3, other, (t == 2).astype(F32))
    else:
        alpha, beta = 1.0, 0.0
    ia[...] = alpha * ra_ref[0 : rows_a * across].astype(F32) + beta * za_ref[0 : rows_a * across].astype(F32)
    ib[...] = alpha * rb_ref[...].astype(F32) + beta * zb_ref[...].astype(F32)
    running = [decays[0:1]]
    for f in range(1, frames):
        running.append(running[-1] * decays[f : f + 1])
    count = (height // 2 + 1) * 4
    base = pb_ref.shape[0] * across
    for f in range(frames):
        for h in range(2):
            part = pc_ref[h, pl.ds(f, count, stride=frames), :]
            sc[f, h, 0:count, :] = part + running[f] * ib[base + 32 * h : base + 32 * h + count, :]
    for n in range(height + 2):
        if two and n == 0:
            continue
        if two:
            src, at = ((pa_ref, ia), n - 1) if n < height else ((pb_ref, ib), n - height)
        elif 2 <= n < height:
            src, at = (pa_ref, ia), n - 2
        else:
            src, at = (pb_ref, ib), n if n < 2 else n - height + 2
        incoming = src[1][at * across : (at + 1) * across, :]
        for f in range(frames):
            slot = (n * frames + f) % rowbuf.shape[0]
            rowbuf[slot, 8 : 8 + across, :] = src[0][at, f] + running[f] * incoming
            corner = (n // 2) * 4
            h = n % 2
            rowbuf[slot, 7:8, :] = sc[f, h, corner : corner + 1, :]
            rowbuf[slot, 8:9, :] = sc[f, h, corner + 1 : corner + 2, :]
            rowbuf[slot, 7 + across : 8 + across, :] = sc[f, h, corner + 2 : corner + 3, :]
            rowbuf[slot, 8 + across : 9 + across, :] = sc[f, h, corner + 3 : corner + 4, :]
            three_taps(rowbuf, slot, x3, n, f, rowbuf[slot, 8 : 8 + across, :].astype(BF16))
    copies = []
    for p in range(height // 2):
        slots = [n if n > 0 or not two else None for n in range(2 * p, 2 * p + 4)]
        y = pair_dot(x3, slots, wt)
        first = jnp.where(flip == 1, height - 2 - 2 * p, 2 * p)
        for rr in range(2):
            row = jnp.where(flip == 1, 1 - rr, rr)
            for f in range(frames):
                mixed = y[f * across : (f + 1) * across, rr * chan : (rr + 1) * chan]
                frame = frames_ref[f, first + row].astype(F32)
                done[p, f, row] = (frame + jax.nn.gelu(mixed)).astype(BF16)
        copies.append(pltpu.make_async_copy(done.at[p], out_ref.at[:, pl.ds(first, 2)], sems.at[p]))
        copies[-1].start()
    for copy in copies:
        copy.wait()


def call(body, outs, scratch, flops, args, place=(VMEM, VMEM)):
    args = [pltpu.with_memory_space_constraint(a, place[0].memory_space) for a in args]
    return pl.pallas_call(
        body,
        out_shape=outs,
        in_specs=[place[0]] * len(args),
        out_specs=jax.tree.map(lambda _: place[1], outs),
        scratch_shapes=scratch,
        compiler_params=pltpu.CompilerParams(vmem_limit_bytes=32 * 2**20),
        cost_estimate=pl.CostEstimate(flops=flops, bytes_accessed=4 * 2**20, transcendentals=0),
    )(*args)


def mirrored(two):
    return lax.axis_index("gx") if two else 0


def swapped(value, axis, count, odd_first=False, mirror=None):
    off = 1 if odd_first else 0
    pairs = [((i + off) % count, (i + 1 + off) % count) for i in range(0, count, 2)]
    pairs += [(b, a) for a, b in pairs]
    if mirror is None:
        return lax.ppermute(value, axis, pairs)
    both = [(m * count + a, (1 - m) * count + b) for m in range(2) for a, b in pairs]
    return lax.ppermute(value, (mirror, axis), both)


def exchange(low, high, axis, count, mirror=None):
    at = lax.axis_index(axis)
    odd = at % 2 == 1
    if count % 2:
        ups, downs = [(i, i + 1) for i in range(count - 1)], [(i + 1, i) for i in range(count - 1)]
        if mirror is not None:
            high, low = (lax.ppermute(v, mirror, [(0, 1), (1, 0)]) for v in (high, low))
        return lax.ppermute(high, axis, ups), lax.ppermute(low, axis, downs)
    near = swapped(jnp.where(odd, low, high), axis, count, False, mirror)
    if count == 2:
        far = jnp.zeros_like(near)
    else:
        far = swapped(jnp.where(odd, high, low), axis, count, True, mirror)
        far = jnp.where((at == 0) | (at == count - 1), jnp.zeros_like(far), far)
    return jnp.where(odd, near, far), jnp.where(odd, far, near)


def carry_general(locals_, total, ta):
    t = lax.axis_index("ta")

    def moved(value, step):
        got = lax.ppermute(value, "ta", [(i, (i + step) % ta) for i in range(ta)])
        return jnp.where(t >= step, got, jnp.zeros_like(got))

    step = 1
    while step < ta:
        came = [moved(v, step) for v in locals_]
        locals_ = [(v.astype(F32) + total * m.astype(F32)).astype(BF16) for v, m in zip(locals_, came)]
        total = jnp.where(t >= step, total * moved(total, step), total)
        step *= 2
    return [moved(v, 1) for v in locals_]


def on_device(gx, gy, ta, frames, in_weight, out_weight, decays):
    n_frames, height, across, chan = frames.shape
    two = gx == 2
    x, t = lax.axis_index("gx"), lax.axis_index("ta")
    near_mem = pltpu.VMEM
    frames, in_weight, out_weight, decays, cols = call(
        fetch_kernel,
        (
            near_mem(frames.shape, BF16), near_mem(in_weight.shape, BF16), near_mem(out_weight.shape, BF16),
            near_mem(decays.shape, F32), near_mem((height, 4 * n_frames, chan), BF16),
        ),
        [pltpu.VMEM((height * 4 * n_frames, chan), F32), pltpu.SemaphoreType.DMA((4,))],
        0, [frames, in_weight, out_weight, decays], (HBM, VMEM),
    )
    low, high = cols[:, : 2 * n_frames], cols[:, 2 * n_frames :]
    if two:
        start = jnp.where(x == 1, 0, height - 2)
        halo = lax.ppermute(lax.dynamic_slice_in_dim(frames, start, 2, axis=1), "gx", [(0, 1), (1, 0)])
        left, right = exchange(low, high, "gy", gy)
        facing = [lax.dynamic_slice_in_dim(v, start, 2, axis=0) for v in (low, high)]
        sides = [cols, left, right, *exchange(*facing, "gy", gy, "gx")]
    else:
        above, below = exchange(frames[:, :2], frames[:, height - 2 :], "gx", gx)
        halo = jnp.concatenate([above, below], axis=1)
        over, under = exchange(cols[:2], cols[height - 2 :], "gx", gx)
        cols = jnp.concatenate([over, cols, under])
        sides = [cols, *exchange(cols[:, : 2 * n_frames], cols[:, 2 * n_frames :], "gy", gy)]

    rows_a = height - 1 if two else height - 2
    rows_b = 2 if two else 4
    wide = (12 * chan, 2 * chan)
    rowbuf = pltpu.VMEM((16, across + 16, chan), F32)
    cells = n_frames * across
    flops = 2 * 9 * chan * chan * cells
    pa, fa, wt_in = call(
        functools.partial(inner_kernel, two),
        (
            near_mem((rows_a, n_frames, across, chan), F32), near_mem((rows_a * across + 16, chan), BF16),
            near_mem(wide, BF16),
        ),
        [rowbuf, pltpu.VMEM((height, cells, 3 * chan), BF16)],
        flops * height, [frames, in_weight, decays],
    )

    total = jnp.prod(decays, axis=0)[None]
    if ta == 4:
        ra = swapped(fa, "ta", ta, False)
        other = jnp.sum(ra[rows_a * across :].astype(F32), axis=0, keepdims=True)

        def joined(mine, theirs):
            mine, theirs = mine.astype(F32), theirs.astype(F32)
            return jnp.where(t == 0, theirs + other * mine, mine + total * theirs).astype(BF16)

        across_two = [(0, 2), (2, 0), (1, 3), (3, 1)]
        za = lax.ppermute(joined(fa, ra), "ta", across_two)

    n_cols = (height // 2 + 1) * 4
    pb, pc, fb, wt_out = call(
        functools.partial(edge_kernel, two, gx, gy),
        (
            near_mem((rows_b, n_frames, across, chan), F32),
            near_mem((2, n_cols * n_frames, chan), F32),
            near_mem((rows_b * across + 64, chan), BF16),
            near_mem(wide, BF16),
        ),
        [
            rowbuf, pltpu.VMEM((2 * rows_b, cells, 3 * chan), BF16),
            pltpu.VMEM((n_cols * n_frames, 12 * chan), BF16), pltpu.VMEM((2, n_cols * n_frames, chan), F32),
            pltpu.VMEM((8 * n_frames, chan), F32),
        ],
        flops * rows_b, [frames, halo, wt_in, decays, out_weight, *sides],
    )

    if ta == 4:
        rb = swapped(fb, "ta", ta, False)
        zb = lax.ppermute(joined(fb, rb), "ta", across_two)
    else:
        ra, rb = carry_general([fa, fb], total, ta)
        za, zb = ra, rb

    return call(
        functools.partial(outer_kernel, two, ta),
        jax.ShapeDtypeStruct(frames.shape, BF16),
        [
            rowbuf, pltpu.VMEM((height + 2, cells, 3 * chan), BF16),
            pltpu.VMEM((n_frames, 2, (n_cols + 7) // 8 * 8, chan), F32),
            pltpu.VMEM((rows_a * across, chan), F32), pltpu.VMEM((rows_b * across + 64, chan), F32),
            pltpu.VMEM((height // 2, n_frames, 2, across, chan), BF16), pltpu.SemaphoreType.DMA((height // 2,)),
        ],
        flops * height, [frames, pa, pb, pc, ra, za, rb, zb, wt_out, decays], (VMEM, HBM),
    )


def solution(mesh):
    sizes = [mesh.shape[a] for a in ("gx", "gy", "ta")]
    placed = (P("ta", "gx", "gy", None), P(), P(), P("ta", None))
    return jax.shard_map(
        functools.partial(on_device, *sizes), mesh=mesh, in_specs=placed,
        out_specs=P("ta", "gx", "gy", None), check_vma=False,
    )
```

```python
import functools

import jax
import jax.numpy as jnp
from jax import lax
from jax.experimental import pallas as pl
from jax.experimental.pallas import tpu as pltpu
from jax.sharding import PartitionSpec as P

F32, BF16 = jnp.float32, jnp.bfloat16
VMEM = pl.BlockSpec(memory_space=pltpu.VMEM)
HBM = pl.BlockSpec(memory_space=pltpu.HBM)


def pair_weights(w_ref, wt, flip):
    chan_in, chan_out = w_ref.shape[2:]
    for k in range(4):
        for b in range(3):
            for rr in range(2):
                at = (k * 3 + b) * chan_in
                a = k - rr
                if 0 <= a <= 2:
                    block = w_ref[jnp.where(flip == 1, 2 - a, a), b]
                else:
                    block = jnp.zeros((chan_in, chan_out), BF16)
                wt[at : at + chan_in, rr * chan_out : (rr + 1) * chan_out] = block


def clear_margins(rowbuf):
    across = rowbuf.shape[1] - 16
    zeros = jnp.zeros((rowbuf.shape[0], 8, rowbuf.shape[2]), F32)
    rowbuf[:, 0:8, :] = zeros
    rowbuf[:, 8 + across : 16 + across, :] = zeros


def three_taps(rowbuf, slot, x3, row, f, middle):
    across = rowbuf.shape[1] - 16
    chan = rowbuf.shape[2]
    at = pl.ds(f * across, across)
    x3[row, at, 0:chan] = rowbuf[slot, 7 : 7 + across, :].astype(BF16)
    x3[row, at, chan : 2 * chan] = middle
    x3[row, at, 2 * chan : 3 * chan] = rowbuf[slot, 9 : 9 + across, :].astype(BF16)


def pair_dot(x3, slots, wt):
    width = x3.shape[2]
    first = next(k for k in range(4) if slots[k] is not None)
    rows = jnp.concatenate([x3[s] for s in slots[first:]], axis=1)
    return jnp.dot(rows, wt[first * width : 4 * width, :], preferred_element_type=F32)


def scan_rows(y, decays, scales, across, keep):
    frames = decays.shape[0]
    chan = decays.shape[1]
    finals = []
    for rr in range(2):
        s = None
        for f in range(frames):
            u = scales[f : f + 1] * y[f * across : (f + 1) * across, rr * chan : (rr + 1) * chan]
            s = u if s is None else decays[f : f + 1] * s + u
            keep(rr, f, s)
        finals.append(s)
    return finals


def load_decays(dec_ref):
    decays = dec_ref[...]
    return decays, jnp.sqrt(1.0 - decays * decays)


def gather_edges(src, row, edge, at):
    frames, across = src.shape[0], src.shape[2]
    for f in range(frames):
        edge[pl.ds(at + f, 2, stride=frames), :] = src[f, row, 0:16, :].astype(F32)[0:2]
        last = src[f, row, across - 16 : across, :].astype(F32)[14:16]
        edge[pl.ds(at + f + 2 * frames, 2, stride=frames), :] = last


def fetch_kernel(two, frames_hbm, dec_hbm, w_hbm, frames_ref, dec_ref, w_ref, cols_ref, *refs):
    *sent, edge, sems = refs
    pairs = [(frames_hbm, frames_ref), (dec_hbm, dec_ref), (w_hbm, w_ref)]
    copies = [pltpu.make_async_copy(src, dst, sems.at[i]) for i, (src, dst) in enumerate(pairs)]
    for copy in copies:
        copy.start()
    copies[0].wait()
    frames, height, across, chan = frames_ref.shape
    for r in range(height):
        gather_edges(frames_ref, r, edge, r * 4 * frames)
    for r in range(height):
        cols_ref[r] = edge[r * 4 * frames : (r + 1) * 4 * frames, :].astype(BF16)
    if two:
        halo_ref, near_ref, far_ref, near_corner, far_corner = sent
        odd = lax.axis_index("gy") % 2 == 1
        start = jnp.where(lax.axis_index("gx") == 1, 0, height - 2)
        halo_ref[...] = frames_ref[:, pl.ds(start, 2)]
        half = 2 * frames
        for refs, rows in (((near_ref, far_ref), range(height)), ((near_corner, far_corner), (start, start + 1))):
            for i, r in enumerate(rows):
                at = pl.multiple_of(r * 2 * half, 2 * half)
                low, high = edge[pl.ds(at, half), :], edge[pl.ds(at + half, half), :]
                refs[0][i] = jnp.where(odd, low, high).astype(BF16)
                refs[1][i] = jnp.where(odd, high, low).astype(BF16)
    for copy in copies[1:]:
        copy.wait()


def inner_kernel(two, frames_ref, dec_ref, w_ref, p_ref, f_ref, wt, rowbuf, x3):
    frames, height, across, chan = frames_ref.shape
    flip = mirrored(two)
    pair_weights(w_ref, wt, flip)
    clear_margins(rowbuf)
    decays, scales = load_decays(dec_ref)
    for r in range(height):
        natural = jnp.where(flip == 1, height - 1 - r, r)
        for f in range(frames):
            slot = (r * frames + f) % rowbuf.shape[0]
            x = frames_ref[f, natural]
            rowbuf[slot, 8 : 8 + across, :] = x.astype(F32)
            three_taps(rowbuf, slot, x3, r, f, x)
    first, first_row = (0, 1) if two else (1, 0)
    for p in range(first, height // 2):
        slots = [r if r >= 0 else None for r in range(2 * p - 2, 2 * p + 2)]
        y = pair_dot(x3, slots, wt)
        base = 2 * (p - first)

        def keep(rr, f, s, base=base):
            if base + rr >= first_row:
                p_ref[base + rr - first_row, f] = s

        for rr, s in enumerate(scan_rows(y, decays, scales, across, keep)):
            at = base + rr - first_row
            if at >= 0:
                f_ref[at * across : (at + 1) * across, :] = s.astype(BF16)
    total = decays[0:1]
    for f in range(1, frames):
        total = total * decays[f : f + 1]
    high = total.astype(BF16)
    rest = total - high.astype(F32)
    middle = rest.astype(BF16)
    low = rest - middle.astype(F32)
    row = lax.broadcasted_iota(jnp.int32, (16, chan), 0)
    parts = jnp.where(row == 0, high.astype(F32), jnp.where(row == 1, middle.astype(F32), jnp.where(row == 2, low, 0.0)))
    end = f_ref.shape[0]
    f_ref[end - 16 : end, :] = parts.astype(BF16)


def edge_kernel(two, gx, gy, own_ref, dec_ref, w_ref, halo_ref, e_ref, *refs):
    *sides, next_hbm, p_ref, pc_ref, f_ref, next_ref, wt, rowbuf, x3, xc, yc, edge, sem = refs
    fetch = pltpu.make_async_copy(next_hbm, next_ref, sem)
    fetch.start()
    frames, across, chan = own_ref.shape[0], *own_ref.shape[2:]
    height = e_ref.shape[0] if two else own_ref.shape[1]
    flip = mirrored(two)
    x, y_at = lax.axis_index("gx"), lax.axis_index("gy")
    has_left, has_right = (y_at > 0).astype(F32), (y_at < gy - 1).astype(F32)
    has_above, has_below = (x > 0).astype(F32), (x < gx - 1).astype(F32)
    pair_weights(w_ref, wt, flip)
    clear_margins(rowbuf)
    decays, scales = load_decays(dec_ref)
    pairs = [height // 2] if two else [0, height // 2]
    for i, p in enumerate(pairs):
        for k in range(4):
            r = 2 * p - 2 + k
            for f in range(frames):
                slot = (k * frames + f) % rowbuf.shape[0]
                if two and r < height:
                    x = own_ref[f, jnp.where(flip == 1, height - 1 - r, r - height + 2)]
                elif 0 <= r < height:
                    x = own_ref[f, r]
                elif two:
                    x = halo_ref[f, jnp.where(flip == 1, 1 - (r - height), r - height)]
                else:
                    x = halo_ref[f, r + 2 if r < 0 else r - height + 2]
                rowbuf[slot, 8 : 8 + across, :] = x.astype(F32)
                three_taps(rowbuf, slot, x3, i * 4 + k, f, x)
    odd = y_at % 2 == 1

    def beside(at, first, second):
        first, second = first[at].astype(F32), second[at].astype(F32)
        if not two:
            return first, second
        second = jnp.where((y_at == 0) | (y_at == gy - 1), 0.0, second)
        return jnp.where(odd, first, second), jnp.where(odd, second, first)

    n_pairs = height // 2 + 1
    if two:
        for i in range(2):
            gather_edges(halo_ref, jnp.where(flip == 1, 1 - i, i), edge, i * 4 * frames)
    for p in range(n_pairs):
        for k in range(4):
            r = 2 * p - 2 + k
            to = slice(p * 4 * frames, (p + 1) * 4 * frames)
            lanes = k * 3 * chan
            if two and r < 0:
                xc[to, lanes : lanes + 3 * chan] = jnp.zeros((4 * frames, 3 * chan), BF16)
                continue
            if two and r >= height:
                at = jnp.where(flip == 1, 1 - (r - height), r - height)
                own = edge[(r - height) * 4 * frames : (r - height + 1) * 4 * frames, :]
                left, right = beside(at, *sides[2:])
            else:
                at = jnp.where(flip == 1, height - 1 - r, r) if two else r + 2
                own = e_ref[at].astype(F32)
                left, right = beside(at, *sides[:2])
            cols = [left[:frames], left[frames:]] + [own[c * frames : (c + 1) * frames] for c in range(4)]
            cols += [right[:frames], right[frames:]]
            for b in range(3):
                piece = jnp.concatenate([cols[c + b] for c in (0, 1, 4, 5)], axis=0)
                xc[to, lanes + b * chan : lanes + (b + 1) * chan] = piece.astype(BF16)
    for i, p in enumerate(pairs):
        y = pair_dot(x3, [i * 4 + k for k in range(4)], wt)
        inside = 1.0
        if not two:
            inside = has_above if p == 0 else has_below

        def keep(rr, f, s, i=i, p=p, inside=inside):
            border = (rr == 0) if p == 0 else (rr == 1)
            p_ref[2 * i + rr, f] = s * inside if border and not two else s

        for rr, s in enumerate(scan_rows(y, decays, scales, across, keep)):
            border = (rr == 0) if p == 0 else (rr == 1)
            s = s * inside if border and not two else s
            f_ref[(2 * i + rr) * across : (2 * i + rr + 1) * across, :] = s.astype(BF16)

    wide = jnp.dot(xc[...], wt[...], preferred_element_type=F32)
    for h in range(2):
        yc[h] = wide[:, h * chan : (h + 1) * chan]
    count = n_pairs * 4
    place = lax.broadcasted_iota(jnp.int32, (count, 2 * chan), 0)
    lane = lax.broadcasted_iota(jnp.int32, (count, 2 * chan), 1)
    mask = jnp.where(place % 4 == 0, has_left, jnp.where(place % 4 == 3, has_right, 1.0))
    above = (place < 4) & (lane < chan)
    if two:
        mask = jnp.where(above, 0.0, mask)
    else:
        below = (place >= count - 4) & (lane >= chan)
        mask = jnp.where(above, mask * has_above, mask)
        mask = jnp.where(below, mask * has_below, mask)
    s = None
    for f in range(frames):
        both = [jnp.concatenate([v[f : f + 1]] * 2, axis=1) for v in (decays, scales)]
        halves = [yc[h, pl.ds(f, count, stride=frames), :] for h in range(2)]
        u = both[1] * jnp.concatenate(halves, axis=1) * mask
        s = u if s is None else both[0] * s + u
        for h in range(2):
            pc_ref[h, pl.ds(f, count, stride=frames), :] = s[:, h * chan : (h + 1) * chan]
    base = len(pairs) * 2 * across
    pad = jnp.zeros((32 - count, chan), F32)
    for h in range(2):
        half = jnp.concatenate([s[:, h * chan : (h + 1) * chan], pad], axis=0)
        f_ref[base + 32 * h : base + 32 * (h + 1), :] = half.astype(BF16)
    fetch.wait()


def outer_kernel(
    two, ta, pa_ref, pb_ref, pc_ref, ra_ref, za_ref, rb_ref, zb_ref, dec_ref, w_ref, frames_hbm,
    out_ref, frames_ref, wt, rowbuf, x3, sc, ia, ib, done, sems,
):
    frames, height, across, chan = frames_ref.shape
    fetch = pltpu.make_async_copy(frames_hbm, frames_ref, sems.at[0])
    fetch.start()
    flip = mirrored(two)
    pair_weights(w_ref, wt, flip)
    decays = dec_ref[...]
    rows_a = pa_ref.shape[0]
    if ta == 4:
        t = lax.axis_index("ta")
        end = ra_ref.shape[0]
        other = jnp.sum(ra_ref[end - 16 : end, :].astype(F32), axis=0, keepdims=True)
        alpha = ((t == 1) | (t == 3)).astype(F32)
        beta = jnp.where(t == 3, other, (t == 2).astype(F32))
    else:
        alpha, beta = 1.0, 0.0
    ia[...] = alpha * ra_ref[0 : rows_a * across].astype(F32) + beta * za_ref[0 : rows_a * across].astype(F32)
    ib[...] = alpha * rb_ref[...].astype(F32) + beta * zb_ref[...].astype(F32)
    running = [decays[0:1]]
    for f in range(1, frames):
        running.append(running[-1] * decays[f : f + 1])
    count = (height // 2 + 1) * 4
    base = pb_ref.shape[0] * across
    for f in range(frames):
        for h in range(2):
            part = pc_ref[h, pl.ds(f, count, stride=frames), :]
            sc[f, h, 0:count, :] = part + running[f] * ib[base + 32 * h : base + 32 * h + count, :]
    def build(n):
        if two and n == 0:
            return
        if two:
            src, at = ((pa_ref, ia), n - 1) if n < height else ((pb_ref, ib), n - height)
        elif 2 <= n < height:
            src, at = (pa_ref, ia), n - 2
        else:
            src, at = (pb_ref, ib), n if n < 2 else n - height + 2
        incoming = src[1][at * across : (at + 1) * across, :]
        for f in range(frames):
            slot = (n * frames + f) % rowbuf.shape[0]
            rowbuf[slot, 8 : 8 + across, :] = src[0][at, f] + running[f] * incoming
            corner = (n // 2) * 4
            h = n % 2
            rowbuf[slot, 7:8, :] = sc[f, h, corner : corner + 1, :]
            rowbuf[slot, 8:9, :] = sc[f, h, corner + 1 : corner + 2, :]
            rowbuf[slot, 7 + across : 8 + across, :] = sc[f, h, corner + 2 : corner + 3, :]
            rowbuf[slot, 8 + across : 9 + across, :] = sc[f, h, corner + 3 : corner + 4, :]
            three_taps(rowbuf, slot, x3, n, f, rowbuf[slot, 8 : 8 + across, :].astype(BF16))

    def finish(p, y):
        first = jnp.where(flip == 1, height - 2 - 2 * p, 2 * p)
        for rr in range(2):
            row = jnp.where(flip == 1, 1 - rr, rr)
            for f in range(frames):
                mixed = y[f * across : (f + 1) * across, rr * chan : (rr + 1) * chan]
                frame = frames_ref[f, first + row].astype(F32)
                done[p, f, row] = (frame + jax.nn.gelu(mixed)).astype(BF16)
        copy = pltpu.make_async_copy(done.at[p], out_ref.at[:, pl.ds(first, 2)], sems.at[1 + p])
        copy.start()
        return copy

    copies, waiting = [], []
    for n in range(2):
        build(n)
    for p in range(height // 2):
        build(2 * p + 2)
        build(2 * p + 3)
        slots = [n if n > 0 or not two else None for n in range(2 * p, 2 * p + 4)]
        waiting.append((p, pair_dot(x3, slots, wt)))
        if p == 1:
            fetch.wait()
        if p >= 1:
            copies += [finish(*w) for w in waiting]
            waiting = []
    for copy in copies:
        copy.wait()


def call(body, outs, scratch, flops, near, far=(), out_place=VMEM):
    near = [pltpu.with_memory_space_constraint(a, pltpu.VMEM) for a in near]
    far = [pltpu.with_memory_space_constraint(a, pltpu.HBM) for a in far]
    return pl.pallas_call(
        body,
        out_shape=outs,
        in_specs=[VMEM] * len(near) + [HBM] * len(far),
        out_specs=jax.tree.map(lambda _: out_place, outs),
        scratch_shapes=scratch,
        compiler_params=pltpu.CompilerParams(vmem_limit_bytes=24 * 2**20),
        cost_estimate=pl.CostEstimate(flops=flops, bytes_accessed=4 * 2**20, transcendentals=0),
    )(*near, *far)


def mirrored(two):
    return lax.axis_index("gx") if two else 0


def swapped(value, axis, count, odd_first=False, mirror=None):
    off = 1 if odd_first else 0
    pairs = [((i + off) % count, (i + 1 + off) % count) for i in range(0, count, 2)]
    pairs += [(b, a) for a, b in pairs]
    if mirror is None:
        return lax.ppermute(value, axis, pairs)
    both = [(m * count + a, (1 - m) * count + b) for m in range(2) for a, b in pairs]
    return lax.ppermute(value, (mirror, axis), both)


def exchange(low, high, axis, count, mirror=None):
    at = lax.axis_index(axis)
    odd = at % 2 == 1
    if count % 2:
        ups, downs = [(i, i + 1) for i in range(count - 1)], [(i + 1, i) for i in range(count - 1)]
        if mirror is not None:
            high, low = (lax.ppermute(v, mirror, [(0, 1), (1, 0)]) for v in (high, low))
        return lax.ppermute(high, axis, ups), lax.ppermute(low, axis, downs)
    near = swapped(jnp.where(odd, low, high), axis, count, False, mirror)
    if count == 2:
        far = jnp.zeros_like(near)
    else:
        far = swapped(jnp.where(odd, high, low), axis, count, True, mirror)
        far = jnp.where((at == 0) | (at == count - 1), jnp.zeros_like(far), far)
    return jnp.where(odd, near, far), jnp.where(odd, far, near)


def carry_general(locals_, total, ta):
    t = lax.axis_index("ta")

    def moved(value, step):
        got = lax.ppermute(value, "ta", [(i, (i + step) % ta) for i in range(ta)])
        return jnp.where(t >= step, got, jnp.zeros_like(got))

    step = 1
    while step < ta:
        came = [moved(v, step) for v in locals_]
        locals_ = [(v.astype(F32) + total * m.astype(F32)).astype(BF16) for v, m in zip(locals_, came)]
        total = jnp.where(t >= step, total * moved(total, step), total)
        step *= 2
    return [moved(v, 1) for v in locals_]


def on_device(gx, gy, ta, frames_far, in_weight, out_weight, decays_far):
    n_frames, height, across, chan = frames_far.shape
    two = gx == 2 and gy > 2 and gy % 2 == 0
    t = lax.axis_index("ta")
    near_mem = pltpu.VMEM
    sent = []
    if two:
        side, corner = (height, 2 * n_frames, chan), (2, 2 * n_frames, chan)
        sent = [near_mem(s, BF16) for s in ((n_frames, 2, across, chan), side, side, corner, corner)]
    frames, decays, w_in, cols, *sent = call(
        functools.partial(fetch_kernel, two),
        [
            near_mem(frames_far.shape, BF16), near_mem(decays_far.shape, F32), near_mem(in_weight.shape, BF16),
            near_mem((height, 4 * n_frames, chan), BF16), *sent,
        ],
        [pltpu.VMEM((height * 4 * n_frames, chan), F32), pltpu.SemaphoreType.DMA((3,))],
        0, [], [frames_far, decays_far, in_weight],
    )
    if two:
        halo = lax.ppermute(sent[0], "gx", [(0, 1), (1, 0)])
        sides = [swapped(v, "gy", gy, i % 2 == 1, "gx" if i > 1 else None) for i, v in enumerate(sent[1:])]
    else:
        above, below = exchange(frames[:, :2], frames[:, height - 2 :], "gx", gx)
        halo = jnp.concatenate([above, below], axis=1)
        over, under = exchange(cols[:2], cols[height - 2 :], "gx", gx)
        cols = jnp.concatenate([over, cols, under])
        sides = exchange(cols[:, : 2 * n_frames], cols[:, 2 * n_frames :], "gy", gy)

    rows_a = height - 1 if two else height - 2
    rows_b = 2 if two else 4
    wt = pltpu.VMEM((12 * chan, 2 * chan), BF16)
    rowbuf = pltpu.VMEM((16, across + 16, chan), F32)
    cells = n_frames * across
    flops = 2 * 9 * chan * chan * cells
    pa, fa = call(
        functools.partial(inner_kernel, two),
        (near_mem((rows_a, n_frames, across, chan), F32), near_mem((rows_a * across + 16, chan), BF16)),
        [wt, rowbuf, pltpu.VMEM((height, cells, 3 * chan), BF16)],
        flops * height, [frames, decays, w_in],
    )

    if two:
        fa, *sides = lax.optimization_barrier((fa, *sides))
    total = jnp.prod(decays, axis=0)[None]
    if ta == 4:
        ra = swapped(fa, "ta", ta, False)
        other = jnp.sum(ra[rows_a * across :].astype(F32), axis=0, keepdims=True)

        def joined(mine, theirs):
            mine, theirs = mine.astype(F32), theirs.astype(F32)
            return jnp.where(t == 0, theirs + other * mine, mine + total * theirs).astype(BF16)

        across_two = [(0, 2), (2, 0), (1, 3), (3, 1)]
        za = lax.ppermute(joined(fa, ra), "ta", across_two)

    n_cols = (height // 2 + 1) * 4
    pb, pc, fb, w_out = call(
        functools.partial(edge_kernel, two, gx, gy),
        (
            near_mem((rows_b, n_frames, across, chan), F32),
            near_mem((2, n_cols * n_frames, chan), F32),
            near_mem((rows_b * across + 64, chan), BF16),
            near_mem(out_weight.shape, BF16),
        ),
        [
            wt, rowbuf, pltpu.VMEM((2 * rows_b, cells, 3 * chan), BF16),
            pltpu.VMEM((n_cols * n_frames, 12 * chan), BF16), pltpu.VMEM((2, n_cols * n_frames, chan), F32),
            pltpu.VMEM((8 * n_frames, chan), F32), pltpu.SemaphoreType.DMA,
        ],
        flops * rows_b, [sent[0] if two else frames, decays, w_in, halo, cols, *sides], [out_weight],
    )
    if ta == 4:
        rb = swapped(fb, "ta", ta, False)
        zb = lax.ppermute(joined(fb, rb), "ta", across_two)
    else:
        ra, rb = carry_general([fa, fb], total, ta)
        za, zb = ra, rb

    return call(
        functools.partial(outer_kernel, two, ta),
        jax.ShapeDtypeStruct(frames.shape, BF16),
        [
            pltpu.VMEM(frames.shape, BF16), wt, rowbuf, pltpu.VMEM((height + 2, cells, 3 * chan), BF16),
            pltpu.VMEM((n_frames, 2, (n_cols + 7) // 8 * 8, chan), F32),
            pltpu.VMEM((rows_a * across, chan), F32), pltpu.VMEM((rows_b * across + 64, chan), F32),
            pltpu.VMEM((height // 2, n_frames, 2, across, chan), BF16), pltpu.SemaphoreType.DMA((1 + height // 2,)),
        ],
        flops * height, [pa, pb, pc, ra, za, rb, zb, decays, w_out], [frames_far], HBM,
    )


def solution(mesh):
    sizes = [mesh.shape[a] for a in ("gx", "gy", "ta")]
    placed = (P("ta", "gx", "gy", None), P(), P(), P("ta", None))
    return jax.shard_map(
        functools.partial(on_device, *sizes), mesh=mesh, in_specs=placed,
        out_specs=P("ta", "gx", "gy", None), check_vma=False,
    )
```

```python
import functools

import jax
import jax.numpy as jnp
from jax import lax
from jax.experimental import pallas as pl
from jax.experimental.pallas import tpu as pltpu
from jax.sharding import PartitionSpec as P

F32, BF16 = jnp.float32, jnp.bfloat16
VMEM = pl.BlockSpec(memory_space=pltpu.VMEM)
HBM = pl.BlockSpec(memory_space=pltpu.HBM)


def pair_weights(w_ref, wt, flip):
    chan_in, chan_out = w_ref.shape[2:]
    for k in range(4):
        for b in range(3):
            for rr in range(2):
                at = (k * 3 + b) * chan_in
                a = k - rr
                if 0 <= a <= 2:
                    block = w_ref[jnp.where(flip == 1, 2 - a, a), b]
                else:
                    block = jnp.zeros((chan_in, chan_out), BF16)
                wt[at : at + chan_in, rr * chan_out : (rr + 1) * chan_out] = block


def clear_margins(rowbuf):
    across = rowbuf.shape[1] - 16
    zeros = jnp.zeros((rowbuf.shape[0], 8, rowbuf.shape[2]), F32)
    rowbuf[:, 0:8, :] = zeros
    rowbuf[:, 8 + across : 16 + across, :] = zeros


def three_taps(rowbuf, slot, x3, row, f, middle):
    across = rowbuf.shape[1] - 16
    chan = rowbuf.shape[2]
    at = pl.ds(f * across, across)
    x3[row, at, 0:chan] = rowbuf[slot, 7 : 7 + across, :].astype(BF16)
    x3[row, at, chan : 2 * chan] = middle
    x3[row, at, 2 * chan : 3 * chan] = rowbuf[slot, 9 : 9 + across, :].astype(BF16)


def pair_dot(x3, slots, wt):
    width = x3.shape[2]
    first = next(k for k in range(4) if slots[k] is not None)
    rows = jnp.concatenate([x3[s] for s in slots[first:]], axis=1)
    return jnp.dot(rows, wt[first * width : 4 * width, :], preferred_element_type=F32)


def scan_rows(y, decays, scales, across, keep):
    frames = decays.shape[0]
    chan = decays.shape[1]
    finals = []
    for rr in range(2):
        s = None
        for f in range(frames):
            u = scales[f : f + 1] * y[f * across : (f + 1) * across, rr * chan : (rr + 1) * chan]
            s = u if s is None else decays[f : f + 1] * s + u
            keep(rr, f, s)
        finals.append(s)
    return finals


def load_decays(dec_ref):
    decays = dec_ref[...]
    return decays, jnp.sqrt(1.0 - decays * decays)


def gather_edges(src, row, edge, at):
    frames, across = src.shape[0], src.shape[2]
    for f in range(frames):
        edge[pl.ds(at + f, 2, stride=frames), :] = src[f, row, 0:16, :].astype(F32)[0:2]
        last = src[f, row, across - 16 : across, :].astype(F32)[14:16]
        edge[pl.ds(at + f + 2 * frames, 2, stride=frames), :] = last


def fetch_kernel(two, frames_hbm, dec_hbm, w_hbm, frames_ref, dec_ref, w_ref, cols_ref, *refs):
    *sent, edge, sems = refs
    pairs = [(frames_hbm, frames_ref), (dec_hbm, dec_ref), (w_hbm, w_ref)]
    copies = [pltpu.make_async_copy(src, dst, sems.at[i]) for i, (src, dst) in enumerate(pairs)]
    for copy in copies:
        copy.start()
    copies[0].wait()
    frames, height, across, chan = frames_ref.shape
    for r in range(height):
        gather_edges(frames_ref, r, edge, r * 4 * frames)
    for r in range(height):
        cols_ref[r] = edge[r * 4 * frames : (r + 1) * 4 * frames, :].astype(BF16)
    if two:
        corner_ref, halo_ref, near_ref, far_ref = sent
        odd = lax.axis_index("gy") % 2 == 1
        start = jnp.where(lax.axis_index("gx") == 1, 0, height - 2)
        halo_ref[...] = frames_ref[:, pl.ds(start, 2)]
        half = 2 * frames
        for r in range(height):
            low, high = edge[r * 2 * half : r * 2 * half + half, :], edge[r * 2 * half + half : (r + 1) * 2 * half, :]
            near_ref[r] = jnp.where(odd, low, high).astype(BF16)
            far_ref[r] = jnp.where(odd, high, low).astype(BF16)
        for i in range(2):
            corner_ref[i] = edge[pl.ds(pl.multiple_of((start + i) * 2 * half, 2 * half), 2 * half), :].astype(BF16)
    for copy in copies[1:]:
        copy.wait()


def inner_kernel(two, frames_ref, dec_ref, w_ref, p_ref, f_ref, wt, rowbuf, x3):
    frames, height, across, chan = frames_ref.shape
    flip = mirrored(two)
    pair_weights(w_ref, wt, flip)
    clear_margins(rowbuf)
    decays, scales = load_decays(dec_ref)
    for r in range(height):
        natural = jnp.where(flip == 1, height - 1 - r, r)
        for f in range(frames):
            slot = (r * frames + f) % rowbuf.shape[0]
            x = frames_ref[f, natural]
            rowbuf[slot, 8 : 8 + across, :] = x.astype(F32)
            three_taps(rowbuf, slot, x3, r, f, x)
    first, first_row = (0, 1) if two else (1, 0)
    for p in range(first, height // 2):
        slots = [r if r >= 0 else None for r in range(2 * p - 2, 2 * p + 2)]
        y = pair_dot(x3, slots, wt)
        base = 2 * (p - first)

        def keep(rr, f, s, base=base):
            if base + rr >= first_row:
                p_ref[base + rr - first_row, f] = s

        for rr, s in enumerate(scan_rows(y, decays, scales, across, keep)):
            at = base + rr - first_row
            if at >= 0:
                f_ref[at * across : (at + 1) * across, :] = s.astype(BF16)
    total = decays[0:1]
    for f in range(1, frames):
        total = total * decays[f : f + 1]
    high = total.astype(BF16)
    rest = total - high.astype(F32)
    middle = rest.astype(BF16)
    low = rest - middle.astype(F32)
    row = lax.broadcasted_iota(jnp.int32, (16, chan), 0)
    parts = jnp.where(row == 0, high.astype(F32), jnp.where(row == 1, middle.astype(F32), jnp.where(row == 2, low, 0.0)))
    end = f_ref.shape[0]
    f_ref[end - 16 : end, :] = parts.astype(BF16)


def edge_kernel(two, gx, gy, own_ref, dec_ref, w_ref, halo_ref, e_ref, corner_ref, *refs):
    *sides, next_hbm, p_ref, pc_ref, f_ref, next_ref, wt, rowbuf, x3, xc, yc, sem = refs
    fetch = pltpu.make_async_copy(next_hbm, next_ref, sem)
    fetch.start()
    frames, across, chan = own_ref.shape[0], *own_ref.shape[2:]
    height = e_ref.shape[0] if two else own_ref.shape[1]
    flip = mirrored(two)
    x, y_at = lax.axis_index("gx"), lax.axis_index("gy")
    has_left, has_right = (y_at > 0).astype(F32), (y_at < gy - 1).astype(F32)
    has_above, has_below = (x > 0).astype(F32), (x < gx - 1).astype(F32)
    pair_weights(w_ref, wt, flip)
    clear_margins(rowbuf)
    decays, scales = load_decays(dec_ref)
    pairs = [height // 2] if two else [0, height // 2]
    for i, p in enumerate(pairs):
        for k in range(4):
            r = 2 * p - 2 + k
            for f in range(frames):
                slot = (k * frames + f) % rowbuf.shape[0]
                if two and r < height:
                    x = own_ref[f, jnp.where(flip == 1, height - 1 - r, r - height + 2)]
                elif 0 <= r < height:
                    x = own_ref[f, r]
                elif two:
                    x = halo_ref[f, jnp.where(flip == 1, 1 - (r - height), r - height)]
                else:
                    x = halo_ref[f, r + 2 if r < 0 else r - height + 2]
                rowbuf[slot, 8 : 8 + across, :] = x.astype(F32)
                three_taps(rowbuf, slot, x3, i * 4 + k, f, x)
    odd = y_at % 2 == 1

    def beside(at, first, second):
        first, second = first[at].astype(F32), second[at].astype(F32)
        if not two:
            return first, second
        second = jnp.where((y_at == 0) | (y_at == gy - 1), 0.0, second)
        return jnp.where(odd, first, second), jnp.where(odd, second, first)

    n_pairs = height // 2 + 1
    for p in range(n_pairs):
        for k in range(4):
            r = 2 * p - 2 + k
            to = slice(p * 4 * frames, (p + 1) * 4 * frames)
            lanes = k * 3 * chan
            if two and r < 0:
                xc[to, lanes : lanes + 3 * chan] = jnp.zeros((4 * frames, 3 * chan), BF16)
                continue
            if two and r >= height:
                at = jnp.where(flip == 1, 1 - (r - height), r - height)
                own = corner_ref[at].astype(F32)
                left, right = beside(height + at, *sides)
            else:
                at = jnp.where(flip == 1, height - 1 - r, r) if two else r + 2
                own = e_ref[at].astype(F32)
                left, right = beside(at, *sides)
            cols = [left[:frames], left[frames:]] + [own[c * frames : (c + 1) * frames] for c in range(4)]
            cols += [right[:frames], right[frames:]]
            for b in range(3):
                piece = jnp.concatenate([cols[c + b] for c in (0, 1, 4, 5)], axis=0)
                xc[to, lanes + b * chan : lanes + (b + 1) * chan] = piece.astype(BF16)
    for i, p in enumerate(pairs):
        y = pair_dot(x3, [i * 4 + k for k in range(4)], wt)
        inside = 1.0
        if not two:
            inside = has_above if p == 0 else has_below

        def keep(rr, f, s, i=i, p=p, inside=inside):
            border = (rr == 0) if p == 0 else (rr == 1)
            p_ref[2 * i + rr, f] = s * inside if border and not two else s

        for rr, s in enumerate(scan_rows(y, decays, scales, across, keep)):
            border = (rr == 0) if p == 0 else (rr == 1)
            s = s * inside if border and not two else s
            f_ref[(2 * i + rr) * across : (2 * i + rr + 1) * across, :] = s.astype(BF16)

    wide = jnp.dot(xc[...], wt[...], preferred_element_type=F32)
    for h in range(2):
        yc[h] = wide[:, h * chan : (h + 1) * chan]
    count = n_pairs * 4
    place = lax.broadcasted_iota(jnp.int32, (count, 2 * chan), 0)
    lane = lax.broadcasted_iota(jnp.int32, (count, 2 * chan), 1)
    mask = jnp.where(place % 4 == 0, has_left, jnp.where(place % 4 == 3, has_right, 1.0))
    above = (place < 4) & (lane < chan)
    if two:
        mask = jnp.where(above, 0.0, mask)
    else:
        below = (place >= count - 4) & (lane >= chan)
        mask = jnp.where(above, mask * has_above, mask)
        mask = jnp.where(below, mask * has_below, mask)
    s = None
    for f in range(frames):
        both = [jnp.concatenate([v[f : f + 1]] * 2, axis=1) for v in (decays, scales)]
        halves = [yc[h, pl.ds(f, count, stride=frames), :] for h in range(2)]
        u = both[1] * jnp.concatenate(halves, axis=1) * mask
        s = u if s is None else both[0] * s + u
        for h in range(2):
            pc_ref[h, pl.ds(f, count, stride=frames), :] = s[:, h * chan : (h + 1) * chan]
    base = len(pairs) * 2 * across
    pad = jnp.zeros((32 - count, chan), F32)
    for h in range(2):
        half = jnp.concatenate([s[:, h * chan : (h + 1) * chan], pad], axis=0)
        f_ref[base + 32 * h : base + 32 * (h + 1), :] = half.astype(BF16)
    fetch.wait()


def outer_kernel(
    two, ta, pa_ref, pb_ref, pc_ref, ra_ref, za_ref, rb_ref, zb_ref, dec_ref, w_ref, frames_hbm,
    out_ref, frames_ref, wt, rowbuf, x3, sc, ia, ib, done, sems,
):
    frames, height, across, chan = frames_ref.shape
    fetch = pltpu.make_async_copy(frames_hbm, frames_ref, sems.at[0])
    fetch.start()
    flip = mirrored(two)
    pair_weights(w_ref, wt, flip)
    decays = dec_ref[...]
    rows_a = pa_ref.shape[0]
    if ta == 4:
        t = lax.axis_index("ta")
        end = ra_ref.shape[0]
        other = jnp.sum(ra_ref[end - 16 : end, :].astype(F32), axis=0, keepdims=True)
        alpha = ((t == 1) | (t == 3)).astype(F32)
        beta = jnp.where(t == 3, other, (t == 2).astype(F32))
    else:
        alpha, beta = 1.0, 0.0
    ia[...] = alpha * ra_ref[0 : rows_a * across].astype(F32) + beta * za_ref[0 : rows_a * across].astype(F32)
    ib[...] = alpha * rb_ref[...].astype(F32) + beta * zb_ref[...].astype(F32)
    running = [decays[0:1]]
    for f in range(1, frames):
        running.append(running[-1] * decays[f : f + 1])
    count = (height // 2 + 1) * 4
    base = pb_ref.shape[0] * across
    for f in range(frames):
        for h in range(2):
            part = pc_ref[h, pl.ds(f, count, stride=frames), :]
            sc[f, h, 0:count, :] = part + running[f] * ib[base + 32 * h : base + 32 * h + count, :]
    def build(n):
        if two and n == 0:
            return
        if two:
            src, at = ((pa_ref, ia), n - 1) if n < height else ((pb_ref, ib), n - height)
        elif 2 <= n < height:
            src, at = (pa_ref, ia), n - 2
        else:
            src, at = (pb_ref, ib), n if n < 2 else n - height + 2
        incoming = src[1][at * across : (at + 1) * across, :]
        for f in range(frames):
            slot = (n * frames + f) % rowbuf.shape[0]
            rowbuf[slot, 8 : 8 + across, :] = src[0][at, f] + running[f] * incoming
            corner = (n // 2) * 4
            h = n % 2
            rowbuf[slot, 7:8, :] = sc[f, h, corner : corner + 1, :]
            rowbuf[slot, 8:9, :] = sc[f, h, corner + 1 : corner + 2, :]
            rowbuf[slot, 7 + across : 8 + across, :] = sc[f, h, corner + 2 : corner + 3, :]
            rowbuf[slot, 8 + across : 9 + across, :] = sc[f, h, corner + 3 : corner + 4, :]
            three_taps(rowbuf, slot, x3, n, f, rowbuf[slot, 8 : 8 + across, :].astype(BF16))

    def finish(p, y):
        first = jnp.where(flip == 1, height - 2 - 2 * p, 2 * p)
        for rr in range(2):
            row = jnp.where(flip == 1, 1 - rr, rr)
            for f in range(frames):
                mixed = y[f * across : (f + 1) * across, rr * chan : (rr + 1) * chan]
                frame = frames_ref[f, first + row].astype(F32)
                done[p, f, row] = (frame + jax.nn.gelu(mixed)).astype(BF16)
        copy = pltpu.make_async_copy(done.at[p], out_ref.at[:, pl.ds(first, 2)], sems.at[1 + p])
        copy.start()
        return copy

    copies, waiting = [], []
    for n in range(2):
        build(n)
    for p in range(height // 2):
        build(2 * p + 2)
        build(2 * p + 3)
        slots = [n if n > 0 or not two else None for n in range(2 * p, 2 * p + 4)]
        waiting.append((p, pair_dot(x3, slots, wt)))
        if p == 1:
            fetch.wait()
        if p >= 1:
            copies += [finish(*w) for w in waiting]
            waiting = []
    for copy in copies:
        copy.wait()


def call(body, outs, scratch, flops, near, far=(), out_place=VMEM):
    near = [pltpu.with_memory_space_constraint(a, pltpu.VMEM) for a in near]
    far = [pltpu.with_memory_space_constraint(a, pltpu.HBM) for a in far]
    return pl.pallas_call(
        body,
        out_shape=outs,
        in_specs=[VMEM] * len(near) + [HBM] * len(far),
        out_specs=jax.tree.map(lambda _: out_place, outs),
        scratch_shapes=scratch,
        compiler_params=pltpu.CompilerParams(vmem_limit_bytes=24 * 2**20),
        cost_estimate=pl.CostEstimate(flops=flops, bytes_accessed=4 * 2**20, transcendentals=0),
    )(*near, *far)


def mirrored(two):
    return lax.axis_index("gx") if two else 0


def swapped(value, axis, count, odd_first):
    off = 1 if odd_first else 0
    pairs = [((i + off) % count, (i + 1 + off) % count) for i in range(0, count, 2)]
    return lax.ppermute(value, axis, pairs + [(b, a) for a, b in pairs])


def exchange(low, high, axis, count):
    at = lax.axis_index(axis)
    odd = at % 2 == 1
    if count % 2:
        ups, downs = [(i, i + 1) for i in range(count - 1)], [(i + 1, i) for i in range(count - 1)]
        return lax.ppermute(high, axis, ups), lax.ppermute(low, axis, downs)
    near = swapped(jnp.where(odd, low, high), axis, count, False)
    if count == 2:
        far = jnp.zeros_like(near)
    else:
        far = swapped(jnp.where(odd, high, low), axis, count, True)
        far = jnp.where((at == 0) | (at == count - 1), jnp.zeros_like(far), far)
    return jnp.where(odd, near, far), jnp.where(odd, far, near)


def carry_general(locals_, total, ta):
    t = lax.axis_index("ta")

    def moved(value, step):
        got = lax.ppermute(value, "ta", [(i, (i + step) % ta) for i in range(ta)])
        return jnp.where(t >= step, got, jnp.zeros_like(got))

    step = 1
    while step < ta:
        came = [moved(v, step) for v in locals_]
        locals_ = [(v.astype(F32) + total * m.astype(F32)).astype(BF16) for v, m in zip(locals_, came)]
        total = jnp.where(t >= step, total * moved(total, step), total)
        step *= 2
    return [moved(v, 1) for v in locals_]


def on_device(gx, gy, ta, frames_far, in_weight, out_weight, decays_far):
    n_frames, height, across, chan = frames_far.shape
    two = gx == 2 and gy > 2 and gy % 2 == 0
    t = lax.axis_index("ta")
    near_mem = pltpu.VMEM
    sent = []
    if two:
        side = (height, 2 * n_frames, chan)
        sent = [near_mem(s, BF16) for s in ((2, 4 * n_frames, chan), (n_frames, 2, across, chan), side, side)]
    frames, decays, w_in, cols, *sent = call(
        functools.partial(fetch_kernel, two),
        [
            near_mem(frames_far.shape, BF16), near_mem(decays_far.shape, F32), near_mem(in_weight.shape, BF16),
            near_mem((height, 4 * n_frames, chan), BF16), *sent,
        ],
        [pltpu.VMEM((height * 4 * n_frames, chan), F32), pltpu.SemaphoreType.DMA((3,))],
        0, [], [frames_far, decays_far, in_weight],
    )
    if two:
        facing = [(0, 1), (1, 0)]
        corner = lax.ppermute(sent[0], "gx", facing)
        halo = lax.ppermute(sent[1], "gx", facing)
    else:
        above, below = exchange(frames[:, :2], frames[:, height - 2 :], "gx", gx)
        halo = jnp.concatenate([above, below], axis=1)
        over, under = exchange(cols[:2], cols[height - 2 :], "gx", gx)
        cols = jnp.concatenate([over, cols, under])
        sides = exchange(cols[:, : 2 * n_frames], cols[:, 2 * n_frames :], "gy", gy)
        corner = cols[:2]

    rows_a = height - 1 if two else height - 2
    rows_b = 2 if two else 4
    wt = pltpu.VMEM((12 * chan, 2 * chan), BF16)
    rowbuf = pltpu.VMEM((16, across + 16, chan), F32)
    cells = n_frames * across
    flops = 2 * 9 * chan * chan * cells
    pa, fa = call(
        functools.partial(inner_kernel, two),
        (near_mem((rows_a, n_frames, across, chan), F32), near_mem((rows_a * across + 16, chan), BF16)),
        [wt, rowbuf, pltpu.VMEM((height, cells, 3 * chan), BF16)],
        flops * height, [frames, decays, w_in],
    )

    if two:
        fa, corner = lax.optimization_barrier((fa, corner))
        odd = lax.axis_index("gy") % 2 == 1
        low, high = corner[:, : 2 * n_frames], corner[:, 2 * n_frames :]
        near = jnp.concatenate([sent[2], jnp.where(odd, low, high)])
        far = jnp.concatenate([sent[3], jnp.where(odd, high, low)])
        sides = [swapped(near, "gy", gy, False), swapped(far, "gy", gy, True)]
    total = jnp.prod(decays, axis=0)[None]
    if ta == 4:
        ra = swapped(fa, "ta", ta, False)
        other = jnp.sum(ra[rows_a * across :].astype(F32), axis=0, keepdims=True)

        def joined(mine, theirs):
            mine, theirs = mine.astype(F32), theirs.astype(F32)
            return jnp.where(t == 0, theirs + other * mine, mine + total * theirs).astype(BF16)

        across_two = [(0, 2), (2, 0), (1, 3), (3, 1)]
        ga = joined(fa, ra)
        za = lax.ppermute(ga, "ta", across_two)
        _, *sides = lax.optimization_barrier((ga, *sides))

    n_cols = (height // 2 + 1) * 4
    pb, pc, fb, w_out = call(
        functools.partial(edge_kernel, two, gx, gy),
        (
            near_mem((rows_b, n_frames, across, chan), F32),
            near_mem((2, n_cols * n_frames, chan), F32),
            near_mem((rows_b * across + 64, chan), BF16),
            near_mem(out_weight.shape, BF16),
        ),
        [
            wt, rowbuf, pltpu.VMEM((2 * rows_b, cells, 3 * chan), BF16),
            pltpu.VMEM((n_cols * n_frames, 12 * chan), BF16), pltpu.VMEM((2, n_cols * n_frames, chan), F32),
            pltpu.SemaphoreType.DMA,
        ],
        flops * rows_b, [sent[1] if two else frames, decays, w_in, halo, cols, corner, *sides], [out_weight],
    )
    if ta == 4:
        za, rb = lax.optimization_barrier((za, swapped(fb, "ta", ta, False)))
        zb = lax.ppermute(joined(fb, rb), "ta", across_two)
    else:
        ra, rb = carry_general([fa, fb], total, ta)
        za, zb = ra, rb

    return call(
        functools.partial(outer_kernel, two, ta),
        jax.ShapeDtypeStruct(frames.shape, BF16),
        [
            pltpu.VMEM(frames.shape, BF16), wt, rowbuf, pltpu.VMEM((height + 2, cells, 3 * chan), BF16),
            pltpu.VMEM((n_frames, 2, (n_cols + 7) // 8 * 8, chan), F32),
            pltpu.VMEM((rows_a * across, chan), F32), pltpu.VMEM((rows_b * across + 64, chan), F32),
            pltpu.VMEM((height // 2, n_frames, 2, across, chan), BF16), pltpu.SemaphoreType.DMA((1 + height // 2,)),
        ],
        flops * height, [pa, pb, pc, ra, za, rb, zb, decays, w_out], [frames_far], HBM,
    )


def solution(mesh):
    sizes = [mesh.shape[a] for a in ("gx", "gy", "ta")]
    placed = (P("ta", "gx", "gy", None), P(), P(), P("ta", None))
    return jax.shard_map(
        functools.partial(on_device, *sizes), mesh=mesh, in_specs=placed,
        out_specs=P("ta", "gx", "gy", None), check_vma=False,
    )
```

```python
import functools

import jax
import jax.numpy as jnp
from jax import lax
from jax.experimental import pallas as pl
from jax.experimental.pallas import tpu as pltpu
from jax.sharding import PartitionSpec as P

F32, BF16 = jnp.float32, jnp.bfloat16
VMEM = pl.BlockSpec(memory_space=pltpu.VMEM)
HBM = pl.BlockSpec(memory_space=pltpu.HBM)


def pair_weights(w_ref, wt, flip):
    chan_in, chan_out = w_ref.shape[2:]
    for k in range(4):
        for b in range(3):
            for rr in range(2):
                at = (k * 3 + b) * chan_in
                a = k - rr
                if 0 <= a <= 2:
                    block = w_ref[jnp.where(flip == 1, 2 - a, a), b]
                else:
                    block = jnp.zeros((chan_in, chan_out), BF16)
                wt[at : at + chan_in, rr * chan_out : (rr + 1) * chan_out] = block


def clear_margins(rowbuf):
    across = rowbuf.shape[1] - 16
    zeros = jnp.zeros((rowbuf.shape[0], 8, rowbuf.shape[2]), F32)
    rowbuf[:, 0:8, :] = zeros
    rowbuf[:, 8 + across : 16 + across, :] = zeros


def three_taps(rowbuf, slot, x3, row, f, middle):
    across = rowbuf.shape[1] - 16
    chan = rowbuf.shape[2]
    at = pl.ds(f * across, across)
    x3[row, at, 0:chan] = rowbuf[slot, 7 : 7 + across, :].astype(BF16)
    x3[row, at, chan : 2 * chan] = middle
    x3[row, at, 2 * chan : 3 * chan] = rowbuf[slot, 9 : 9 + across, :].astype(BF16)


def pair_dot(x3, slots, wt):
    width = x3.shape[2]
    first = next(k for k in range(4) if slots[k] is not None)
    rows = jnp.concatenate([x3[s] for s in slots[first:]], axis=1)
    return jnp.dot(rows, wt[first * width : 4 * width, :], preferred_element_type=F32)


def scan_rows(y, decays, scales, across, keep):
    frames = decays.shape[0]
    chan = decays.shape[1]
    finals = []
    for rr in range(2):
        s = None
        for f in range(frames):
            u = scales[f : f + 1] * y[f * across : (f + 1) * across, rr * chan : (rr + 1) * chan]
            s = u if s is None else decays[f : f + 1] * s + u
            keep(rr, f, s)
        finals.append(s)
    return finals


def load_decays(dec_ref):
    decays = dec_ref[...]
    return decays, jnp.sqrt(1.0 - decays * decays)


def gather_edges(src, row, edge, at):
    frames, across = src.shape[0], src.shape[2]
    for f in range(frames):
        edge[pl.ds(at + f, 2, stride=frames), :] = src[f, row, 0:16, :].astype(F32)[0:2]
        last = src[f, row, across - 16 : across, :].astype(F32)[14:16]
        edge[pl.ds(at + f + 2 * frames, 2, stride=frames), :] = last


def fetch_kernel(two, frames_hbm, dec_hbm, w_hbm, frames_ref, dec_ref, w_ref, cols_ref, *refs):
    *sent, edge, sems = refs
    pairs = [(frames_hbm, frames_ref), (dec_hbm, dec_ref), (w_hbm, w_ref)]
    copies = [pltpu.make_async_copy(src, dst, sems.at[i]) for i, (src, dst) in enumerate(pairs)]
    for copy in copies:
        copy.start()
    copies[0].wait()
    frames, height, across, chan = frames_ref.shape
    for r in range(height):
        gather_edges(frames_ref, r, edge, r * 4 * frames)
    for r in range(height):
        cols_ref[r] = edge[r * 4 * frames : (r + 1) * 4 * frames, :].astype(BF16)
    if two:
        corner_ref, halo_ref, near_ref, far_ref = sent
        odd = lax.axis_index("gy") % 2 == 1
        start = jnp.where(lax.axis_index("gx") == 1, 0, height - 2)
        halo_ref[...] = frames_ref[:, pl.ds(start, 2)]
        half = 2 * frames
        for r in range(height):
            low, high = edge[r * 2 * half : r * 2 * half + half, :], edge[r * 2 * half + half : (r + 1) * 2 * half, :]
            near_ref[r] = jnp.where(odd, low, high).astype(BF16)
            far_ref[r] = jnp.where(odd, high, low).astype(BF16)
        for i in range(2):
            corner_ref[i] = edge[pl.ds(pl.multiple_of((start + i) * 2 * half, 2 * half), 2 * half), :].astype(BF16)
    for copy in copies[1:]:
        copy.wait()


def addends(decays, rows):
    total = decays[0:1]
    for f in range(1, decays.shape[0]):
        total = total * decays[f : f + 1]
    high = total.astype(BF16).astype(F32)
    middle = (total - high).astype(BF16).astype(F32)
    low = total - high - middle
    row = lax.broadcasted_iota(jnp.int32, (rows, decays.shape[1]), 0)
    return jnp.where(row == 0, high, jnp.where(row == 1, middle, jnp.where(row == 2, low, 0.0)))


def inner_kernel(two, frames_ref, dec_ref, w_ref, p_ref, f_ref, wt, rowbuf, x3):
    frames, height, across, chan = frames_ref.shape
    flip = mirrored(two)
    pair_weights(w_ref, wt, flip)
    clear_margins(rowbuf)
    decays, scales = load_decays(dec_ref)
    for r in range(height):
        natural = jnp.where(flip == 1, height - 1 - r, r)
        for f in range(frames):
            slot = (r * frames + f) % rowbuf.shape[0]
            x = frames_ref[f, natural]
            rowbuf[slot, 8 : 8 + across, :] = x.astype(F32)
            three_taps(rowbuf, slot, x3, r, f, x)
    first, first_row = (0, 1) if two else (1, 0)
    for p in range(first, height // 2):
        slots = [r if r >= 0 else None for r in range(2 * p - 2, 2 * p + 2)]
        y = pair_dot(x3, slots, wt)
        base = 2 * (p - first)

        def keep(rr, f, s, base=base):
            if base + rr >= first_row:
                p_ref[base + rr - first_row, f] = s

        for rr, s in enumerate(scan_rows(y, decays, scales, across, keep)):
            at = base + rr - first_row
            if at >= 0:
                f_ref[at * across : (at + 1) * across, :] = s.astype(BF16)
    end = f_ref.shape[0]
    f_ref[end - 16 : end, :] = addends(decays, 16).astype(BF16)


def edge_kernel(two, gx, gy, own_ref, dec_ref, w_ref, halo_ref, e_ref, corner_ref, *refs):
    *sides, next_hbm, p_ref, pc_ref, f_ref, next_ref, wt, rowbuf, x3, xc, yc, sem = refs
    fetch = pltpu.make_async_copy(next_hbm, next_ref, sem)
    fetch.start()
    frames, across, chan = own_ref.shape[0], *own_ref.shape[2:]
    height = e_ref.shape[0] if two else own_ref.shape[1]
    flip = mirrored(two)
    x, y_at = lax.axis_index("gx"), lax.axis_index("gy")
    has_left, has_right = (y_at > 0).astype(F32), (y_at < gy - 1).astype(F32)
    has_above, has_below = (x > 0).astype(F32), (x < gx - 1).astype(F32)
    pair_weights(w_ref, wt, flip)
    clear_margins(rowbuf)
    decays, scales = load_decays(dec_ref)
    pairs = [height // 2] if two else [0, height // 2]
    for i, p in enumerate(pairs):
        for k in range(4):
            r = 2 * p - 2 + k
            for f in range(frames):
                slot = (k * frames + f) % rowbuf.shape[0]
                if two and r < height:
                    x = own_ref[f, jnp.where(flip == 1, height - 1 - r, r - height + 2)]
                elif 0 <= r < height:
                    x = own_ref[f, r]
                elif two:
                    x = halo_ref[f, jnp.where(flip == 1, 1 - (r - height), r - height)]
                else:
                    x = halo_ref[f, r + 2 if r < 0 else r - height + 2]
                rowbuf[slot, 8 : 8 + across, :] = x.astype(F32)
                three_taps(rowbuf, slot, x3, i * 4 + k, f, x)
    odd = y_at % 2 == 1

    def beside(at, first, second):
        first, second = first[at].astype(F32), second[at].astype(F32)
        if not two:
            return first, second
        second = jnp.where((y_at == 0) | (y_at == gy - 1), 0.0, second)
        return jnp.where(odd, first, second), jnp.where(odd, second, first)

    n_pairs = height // 2 + 1
    for p in range(n_pairs):
        for k in range(4):
            r = 2 * p - 2 + k
            to = slice(p * 4 * frames, (p + 1) * 4 * frames)
            lanes = k * 3 * chan
            if two and r < 0:
                xc[to, lanes : lanes + 3 * chan] = jnp.zeros((4 * frames, 3 * chan), BF16)
                continue
            if two and r >= height:
                at = jnp.where(flip == 1, 1 - (r - height), r - height)
                own = corner_ref[at].astype(F32)
                left, right = beside(height + at, *sides)
            else:
                at = jnp.where(flip == 1, height - 1 - r, r) if two else r + 2
                own = e_ref[at].astype(F32)
                left, right = beside(at, *sides)
            cols = [left[:frames], left[frames:]] + [own[c * frames : (c + 1) * frames] for c in range(4)]
            cols += [right[:frames], right[frames:]]
            for b in range(3):
                piece = jnp.concatenate([cols[c + b] for c in (0, 1, 4, 5)], axis=0)
                xc[to, lanes + b * chan : lanes + (b + 1) * chan] = piece.astype(BF16)
    for i, p in enumerate(pairs):
        y = pair_dot(x3, [i * 4 + k for k in range(4)], wt)
        inside = 1.0
        if not two:
            inside = has_above if p == 0 else has_below

        def keep(rr, f, s, i=i, p=p, inside=inside):
            border = (rr == 0) if p == 0 else (rr == 1)
            p_ref[2 * i + rr, f] = s * inside if border and not two else s

        for rr, s in enumerate(scan_rows(y, decays, scales, across, keep)):
            border = (rr == 0) if p == 0 else (rr == 1)
            s = s * inside if border and not two else s
            f_ref[(2 * i + rr) * across : (2 * i + rr + 1) * across, :] = s.astype(BF16)

    wide = jnp.dot(xc[...], wt[...], preferred_element_type=F32)
    for h in range(2):
        yc[h] = wide[:, h * chan : (h + 1) * chan]
    count = n_pairs * 4
    place = lax.broadcasted_iota(jnp.int32, (count, 2 * chan), 0)
    lane = lax.broadcasted_iota(jnp.int32, (count, 2 * chan), 1)
    mask = jnp.where(place % 4 == 0, has_left, jnp.where(place % 4 == 3, has_right, 1.0))
    above = (place < 4) & (lane < chan)
    if two:
        mask = jnp.where(above, 0.0, mask)
    else:
        below = (place >= count - 4) & (lane >= chan)
        mask = jnp.where(above, mask * has_above, mask)
        mask = jnp.where(below, mask * has_below, mask)
    s = None
    for f in range(frames):
        both = [jnp.concatenate([v[f : f + 1]] * 2, axis=1) for v in (decays, scales)]
        halves = [yc[h, pl.ds(f, count, stride=frames), :] for h in range(2)]
        u = both[1] * jnp.concatenate(halves, axis=1) * mask
        s = u if s is None else both[0] * s + u
        for h in range(2):
            pc_ref[h, pl.ds(f, count, stride=frames), :] = s[:, h * chan : (h + 1) * chan]
    base = len(pairs) * 2 * across
    pad = jnp.concatenate([jnp.zeros((24 - count, chan), F32), addends(decays, 8)], axis=0)
    for h in range(2):
        half = jnp.concatenate([s[:, h * chan : (h + 1) * chan], pad], axis=0)
        f_ref[base + 32 * h : base + 32 * (h + 1), :] = half.astype(BF16)
    fetch.wait()


def outer_kernel(
    two, ta, pa_ref, pb_ref, pc_ref, ra_ref, za_ref, b1_ref, b2_ref, b3_ref, dec_ref, w_ref, frames_hbm,
    out_ref, frames_ref, wt, rowbuf, x3, sc, ia, ib, done, sems,
):
    frames, height, across, chan = frames_ref.shape
    fetch = pltpu.make_async_copy(frames_hbm, frames_ref, sems.at[0])
    fetch.start()
    flip = mirrored(two)
    pair_weights(w_ref, wt, flip)
    decays = dec_ref[...]
    rows_a = pa_ref.shape[0]
    base = pb_ref.shape[0] * across

    def product(ref, at):
        return jnp.sum(ref[at : at + 16, :].astype(F32)[8:16], axis=0, keepdims=True)

    if ta == 4:
        t = lax.axis_index("ta")
        end = ra_ref.shape[0]
        other = jnp.sum(ra_ref[end - 16 : end, :].astype(F32), axis=0, keepdims=True)
        last = (t == 3).astype(F32)
        one, two_on = ((t == 1) | (t == 3)).astype(F32), (t == 2).astype(F32)
        from_a = one, two_on + last * other
        d1, d2, d3 = (product(ref, base + 16) for ref in (b1_ref, b2_ref, b3_ref))
        from_b = one, two_on * d3 + last * d1, two_on + last * d1 * d2
    else:
        from_a, from_b = (1.0, 0.0), (1.0, 0.0, 0.0)
    ia[...] = sum(c * ref[0 : rows_a * across].astype(F32) for c, ref in zip(from_a, (ra_ref, za_ref)))
    ib[...] = sum(c * ref[...].astype(F32) for c, ref in zip(from_b, (b1_ref, b2_ref, b3_ref)))
    running = [decays[0:1]]
    for f in range(1, frames):
        running.append(running[-1] * decays[f : f + 1])
    count = (height // 2 + 1) * 4
    for f in range(frames):
        for h in range(2):
            part = pc_ref[h, pl.ds(f, count, stride=frames), :]
            sc[f, h, 0:count, :] = part + running[f] * ib[base + 32 * h : base + 32 * h + count, :]
    def build(n):
        if two and n == 0:
            return
        if two:
            src, at = ((pa_ref, ia), n - 1) if n < height else ((pb_ref, ib), n - height)
        elif 2 <= n < height:
            src, at = (pa_ref, ia), n - 2
        else:
            src, at = (pb_ref, ib), n if n < 2 else n - height + 2
        incoming = src[1][at * across : (at + 1) * across, :]
        for f in range(frames):
            slot = (n * frames + f) % rowbuf.shape[0]
            rowbuf[slot, 8 : 8 + across, :] = src[0][at, f] + running[f] * incoming
            corner = (n // 2) * 4
            h = n % 2
            rowbuf[slot, 7:8, :] = sc[f, h, corner : corner + 1, :]
            rowbuf[slot, 8:9, :] = sc[f, h, corner + 1 : corner + 2, :]
            rowbuf[slot, 7 + across : 8 + across, :] = sc[f, h, corner + 2 : corner + 3, :]
            rowbuf[slot, 8 + across : 9 + across, :] = sc[f, h, corner + 3 : corner + 4, :]
            three_taps(rowbuf, slot, x3, n, f, rowbuf[slot, 8 : 8 + across, :].astype(BF16))

    def finish(p, y):
        first = jnp.where(flip == 1, height - 2 - 2 * p, 2 * p)
        for rr in range(2):
            row = jnp.where(flip == 1, 1 - rr, rr)
            for f in range(frames):
                mixed = y[f * across : (f + 1) * across, rr * chan : (rr + 1) * chan]
                frame = frames_ref[f, first + row].astype(F32)
                done[p, f, row] = (frame + jax.nn.gelu(mixed)).astype(BF16)
        copy = pltpu.make_async_copy(done.at[p], out_ref.at[:, pl.ds(first, 2)], sems.at[1 + p])
        copy.start()
        return copy

    copies, waiting = [], []
    for n in range(2):
        build(n)
    for p in range(height // 2):
        build(2 * p + 2)
        build(2 * p + 3)
        slots = [n if n > 0 or not two else None for n in range(2 * p, 2 * p + 4)]
        waiting.append((p, pair_dot(x3, slots, wt)))
        if p == 1:
            fetch.wait()
        if p >= 1:
            copies += [finish(*w) for w in waiting]
            waiting = []
    for copy in copies:
        copy.wait()


def call(body, outs, scratch, flops, near, far=(), out_place=VMEM):
    near = [pltpu.with_memory_space_constraint(a, pltpu.VMEM) for a in near]
    far = [pltpu.with_memory_space_constraint(a, pltpu.HBM) for a in far]
    return pl.pallas_call(
        body,
        out_shape=outs,
        in_specs=[VMEM] * len(near) + [HBM] * len(far),
        out_specs=jax.tree.map(lambda _: out_place, outs),
        scratch_shapes=scratch,
        compiler_params=pltpu.CompilerParams(vmem_limit_bytes=24 * 2**20),
        cost_estimate=pl.CostEstimate(flops=flops, bytes_accessed=4 * 2**20, transcendentals=0),
    )(*near, *far)


def mirrored(two):
    return lax.axis_index("gx") if two else 0


def swapped(value, axis, count, odd_first):
    off = 1 if odd_first else 0
    pairs = [((i + off) % count, (i + 1 + off) % count) for i in range(0, count, 2)]
    return lax.ppermute(value, axis, pairs + [(b, a) for a, b in pairs])


def exchange(low, high, axis, count):
    at = lax.axis_index(axis)
    odd = at % 2 == 1
    if count % 2:
        ups, downs = [(i, i + 1) for i in range(count - 1)], [(i + 1, i) for i in range(count - 1)]
        return lax.ppermute(high, axis, ups), lax.ppermute(low, axis, downs)
    near = swapped(jnp.where(odd, low, high), axis, count, False)
    if count == 2:
        far = jnp.zeros_like(near)
    else:
        far = swapped(jnp.where(odd, high, low), axis, count, True)
        far = jnp.where((at == 0) | (at == count - 1), jnp.zeros_like(far), far)
    return jnp.where(odd, near, far), jnp.where(odd, far, near)


def carry_general(locals_, total, ta):
    t = lax.axis_index("ta")

    def moved(value, step):
        got = lax.ppermute(value, "ta", [(i, (i + step) % ta) for i in range(ta)])
        return jnp.where(t >= step, got, jnp.zeros_like(got))

    step = 1
    while step < ta:
        came = [moved(v, step) for v in locals_]
        locals_ = [(v.astype(F32) + total * m.astype(F32)).astype(BF16) for v, m in zip(locals_, came)]
        total = jnp.where(t >= step, total * moved(total, step), total)
        step *= 2
    return [moved(v, 1) for v in locals_]


def on_device(gx, gy, ta, frames_far, in_weight, out_weight, decays_far):
    n_frames, height, across, chan = frames_far.shape
    two = gx == 2 and gy > 2 and gy % 2 == 0
    t = lax.axis_index("ta")
    near_mem = pltpu.VMEM
    sent = []
    if two:
        side = (height, 2 * n_frames, chan)
        sent = [near_mem(s, BF16) for s in ((2, 4 * n_frames, chan), (n_frames, 2, across, chan), side, side)]
    frames, decays, w_in, cols, *sent = call(
        functools.partial(fetch_kernel, two),
        [
            near_mem(frames_far.shape, BF16), near_mem(decays_far.shape, F32), near_mem(in_weight.shape, BF16),
            near_mem((height, 4 * n_frames, chan), BF16), *sent,
        ],
        [pltpu.VMEM((height * 4 * n_frames, chan), F32), pltpu.SemaphoreType.DMA((3,))],
        0, [], [frames_far, decays_far, in_weight],
    )
    if two:
        facing = [(0, 1), (1, 0)]
        corner = lax.ppermute(sent[0], "gx", facing)
        halo = lax.ppermute(sent[1], "gx", facing)
    else:
        above, below = exchange(frames[:, :2], frames[:, height - 2 :], "gx", gx)
        halo = jnp.concatenate([above, below], axis=1)
        over, under = exchange(cols[:2], cols[height - 2 :], "gx", gx)
        cols = jnp.concatenate([over, cols, under])
        sides = exchange(cols[:, : 2 * n_frames], cols[:, 2 * n_frames :], "gy", gy)
        corner = cols[:2]

    rows_a = height - 1 if two else height - 2
    rows_b = 2 if two else 4
    wt = pltpu.VMEM((12 * chan, 2 * chan), BF16)
    rowbuf = pltpu.VMEM((16, across + 16, chan), F32)
    cells = n_frames * across
    flops = 2 * 9 * chan * chan * cells
    pa, fa = call(
        functools.partial(inner_kernel, two),
        (near_mem((rows_a, n_frames, across, chan), F32), near_mem((rows_a * across + 16, chan), BF16)),
        [wt, rowbuf, pltpu.VMEM((height, cells, 3 * chan), BF16)],
        flops * height, [frames, decays, w_in],
    )

    if two:
        fa, corner = lax.optimization_barrier((fa, corner))
        odd = lax.axis_index("gy") % 2 == 1
        low, high = corner[:, : 2 * n_frames], corner[:, 2 * n_frames :]
        near = jnp.concatenate([sent[2], jnp.where(odd, low, high)])
        far = jnp.concatenate([sent[3], jnp.where(odd, high, low)])
        sides = [swapped(near, "gy", gy, False), swapped(far, "gy", gy, True)]
    total = jnp.prod(decays, axis=0)[None]
    if ta == 4:
        ra = swapped(fa, "ta", ta, False)
        other = jnp.sum(ra[rows_a * across :].astype(F32), axis=0, keepdims=True)

        def joined(mine, theirs):
            mine, theirs = mine.astype(F32), theirs.astype(F32)
            return jnp.where(t == 0, theirs + other * mine, mine + total * theirs).astype(BF16)

        across_two = [(0, 2), (2, 0), (1, 3), (3, 1)]
        ga = joined(fa, ra)
        za = lax.ppermute(ga, "ta", across_two)
        _, *sides = lax.optimization_barrier((ga, *sides))

    n_cols = (height // 2 + 1) * 4
    pb, pc, fb, w_out = call(
        functools.partial(edge_kernel, two, gx, gy),
        (
            near_mem((rows_b, n_frames, across, chan), F32),
            near_mem((2, n_cols * n_frames, chan), F32),
            near_mem((rows_b * across + 64, chan), BF16),
            near_mem(out_weight.shape, BF16),
        ),
        [
            wt, rowbuf, pltpu.VMEM((2 * rows_b, cells, 3 * chan), BF16),
            pltpu.VMEM((n_cols * n_frames, 12 * chan), BF16), pltpu.VMEM((2, n_cols * n_frames, chan), F32),
            pltpu.SemaphoreType.DMA,
        ],
        flops * rows_b, [sent[1] if two else frames, decays, w_in, halo, cols, corner, *sides], [out_weight],
    )
    if ta == 4:
        edges = [swapped(fb, "ta", ta, False), lax.ppermute(fb, "ta", across_two), swapped(fb, "ta", ta, True)]
    else:
        ra, rb = carry_general([fa, fb], total, ta)
        za, edges = ra, [rb] * 3

    return call(
        functools.partial(outer_kernel, two, ta),
        jax.ShapeDtypeStruct(frames.shape, BF16),
        [
            pltpu.VMEM(frames.shape, BF16), wt, rowbuf, pltpu.VMEM((height + 2, cells, 3 * chan), BF16),
            pltpu.VMEM((n_frames, 2, (n_cols + 7) // 8 * 8, chan), F32),
            pltpu.VMEM((rows_a * across, chan), F32), pltpu.VMEM((rows_b * across + 64, chan), F32),
            pltpu.VMEM((height // 2, n_frames, 2, across, chan), BF16), pltpu.SemaphoreType.DMA((1 + height // 2,)),
        ],
        flops * height, [pa, pb, pc, ra, za, *edges, decays, w_out], [frames_far], HBM,
    )


def solution(mesh):
    sizes = [mesh.shape[a] for a in ("gx", "gy", "ta")]
    placed = (P("ta", "gx", "gy", None), P(), P(), P("ta", None))
    return jax.shard_map(
        functools.partial(on_device, *sizes), mesh=mesh, in_specs=placed,
        out_specs=P("ta", "gx", "gy", None), check_vma=False,
    )
```

```python
import functools

import jax
import jax.numpy as jnp
from jax import lax
from jax.experimental import pallas as pl
from jax.experimental.pallas import tpu as pltpu
from jax.sharding import PartitionSpec as P

F32, BF16 = jnp.float32, jnp.bfloat16
VMEM = pl.BlockSpec(memory_space=pltpu.VMEM)
HBM = pl.BlockSpec(memory_space=pltpu.HBM)


def pair_weights(w_ref, wt, flip):
    chan_in, chan_out = w_ref.shape[2:]
    for k in range(4):
        for b in range(3):
            for rr in range(2):
                at = (k * 3 + b) * chan_in
                a = k - rr
                if 0 <= a <= 2:
                    block = w_ref[jnp.where(flip == 1, 2 - a, a), b]
                else:
                    block = jnp.zeros((chan_in, chan_out), BF16)
                wt[at : at + chan_in, rr * chan_out : (rr + 1) * chan_out] = block


def clear_margins(rowbuf):
    across = rowbuf.shape[1] - 16
    zeros = jnp.zeros((rowbuf.shape[0], 8, rowbuf.shape[2]), F32)
    rowbuf[:, 0:8, :] = zeros
    rowbuf[:, 8 + across : 16 + across, :] = zeros


def three_taps(rowbuf, slot, x3, row, f, middle):
    across = rowbuf.shape[1] - 16
    chan = rowbuf.shape[2]
    at = pl.ds(f * across, across)
    x3[row, at, 0:chan] = rowbuf[slot, 7 : 7 + across, :].astype(BF16)
    x3[row, at, chan : 2 * chan] = middle
    x3[row, at, 2 * chan : 3 * chan] = rowbuf[slot, 9 : 9 + across, :].astype(BF16)


def pair_dot(x3, slots, wt):
    width = x3.shape[2]
    first = next(k for k in range(4) if slots[k] is not None)
    rows = jnp.concatenate([x3[s] for s in slots[first:]], axis=1)
    return jnp.dot(rows, wt[first * width : 4 * width, :], preferred_element_type=F32)


def scan_rows(y, decays, scales, across, keep):
    frames = decays.shape[0]
    chan = decays.shape[1]
    finals = []
    for rr in range(2):
        s = None
        for f in range(frames):
            u = scales[f : f + 1] * y[f * across : (f + 1) * across, rr * chan : (rr + 1) * chan]
            s = u if s is None else decays[f : f + 1] * s + u
            keep(rr, f, s)
        finals.append(s)
    return finals


def load_decays(dec_ref):
    decays = dec_ref[...]
    return decays, jnp.sqrt(1.0 - decays * decays)


def gather_edges(src, row, edge, at):
    frames, across = src.shape[0], src.shape[2]
    for f in range(frames):
        edge[pl.ds(at + f, 2, stride=frames), :] = src[f, row, 0:16, :].astype(F32)[0:2]
        last = src[f, row, across - 16 : across, :].astype(F32)[14:16]
        edge[pl.ds(at + f + 2 * frames, 2, stride=frames), :] = last


def fetch_kernel(two, frames_hbm, dec_hbm, w_hbm, frames_ref, dec_ref, w_ref, cols_ref, *refs):
    *sent, edge, sems = refs
    pairs = [(frames_hbm, frames_ref), (dec_hbm, dec_ref), (w_hbm, w_ref)]
    copies = [pltpu.make_async_copy(src, dst, sems.at[i]) for i, (src, dst) in enumerate(pairs)]
    for copy in copies:
        copy.start()
    copies[0].wait()
    frames, height, across, chan = frames_ref.shape
    for r in range(height):
        gather_edges(frames_ref, r, edge, r * 4 * frames)
    for r in range(height):
        cols_ref[r] = edge[r * 4 * frames : (r + 1) * 4 * frames, :].astype(BF16)
    if two:
        corner_ref, halo_ref, near_ref, far_ref = sent
        odd = lax.axis_index("gy") % 2 == 1
        start = jnp.where(lax.axis_index("gx") == 1, 0, height - 2)
        halo_ref[...] = frames_ref[:, pl.ds(start, 2)]
        half = 2 * frames
        for r in range(height):
            low, high = edge[r * 2 * half : r * 2 * half + half, :], edge[r * 2 * half + half : (r + 1) * 2 * half, :]
            near_ref[r] = jnp.where(odd, low, high).astype(BF16)
            far_ref[r] = jnp.where(odd, high, low).astype(BF16)
        for i in range(2):
            corner_ref[i] = edge[pl.ds(pl.multiple_of((start + i) * 2 * half, 2 * half), 2 * half), :].astype(BF16)
    for copy in copies[1:]:
        copy.wait()


def addends(decays, rows):
    total = decays[0:1]
    for f in range(1, decays.shape[0]):
        total = total * decays[f : f + 1]
    high = total.astype(BF16).astype(F32)
    middle = (total - high).astype(BF16).astype(F32)
    low = total - high - middle
    row = lax.broadcasted_iota(jnp.int32, (rows, decays.shape[1]), 0)
    return jnp.where(row == 0, high, jnp.where(row == 1, middle, jnp.where(row == 2, low, 0.0)))


def inner_kernel(two, frames_ref, dec_ref, w_ref, p_ref, f_ref, wt, rowbuf, x3):
    frames, height, across, chan = frames_ref.shape
    flip = mirrored(two)
    pair_weights(w_ref, wt, flip)
    clear_margins(rowbuf)
    decays, scales = load_decays(dec_ref)
    for r in range(height):
        natural = jnp.where(flip == 1, height - 1 - r, r)
        for f in range(frames):
            slot = (r * frames + f) % rowbuf.shape[0]
            x = frames_ref[f, natural]
            rowbuf[slot, 8 : 8 + across, :] = x.astype(F32)
            three_taps(rowbuf, slot, x3, r, f, x)
    first, first_row = (0, 1) if two else (1, 0)
    for p in range(first, height // 2):
        slots = [r if r >= 0 else None for r in range(2 * p - 2, 2 * p + 2)]
        y = pair_dot(x3, slots, wt)
        base = 2 * (p - first)

        def keep(rr, f, s, base=base):
            if base + rr >= first_row:
                p_ref[base + rr - first_row, f] = s.astype(BF16)

        for rr, s in enumerate(scan_rows(y, decays, scales, across, keep)):
            at = base + rr - first_row
            if at >= 0:
                f_ref[at * across : (at + 1) * across, :] = s.astype(BF16)
    end = f_ref.shape[0]
    f_ref[end - 16 : end, :] = addends(decays, 16).astype(BF16)


def edge_kernel(two, gx, gy, own_ref, dec_ref, w_ref, halo_ref, e_ref, corner_ref, *refs):
    *sides, next_hbm, p_ref, pc_ref, f_ref, next_wt, next_w, wt, rowbuf, x3, xc, yc, sem = refs
    fetch = pltpu.make_async_copy(next_hbm, next_w, sem)
    fetch.start()
    frames, across, chan = own_ref.shape[0], *own_ref.shape[2:]
    height = e_ref.shape[0] if two else own_ref.shape[1]
    flip = mirrored(two)
    x, y_at = lax.axis_index("gx"), lax.axis_index("gy")
    has_left, has_right = (y_at > 0).astype(F32), (y_at < gy - 1).astype(F32)
    has_above, has_below = (x > 0).astype(F32), (x < gx - 1).astype(F32)
    pair_weights(w_ref, wt, flip)
    clear_margins(rowbuf)
    decays, scales = load_decays(dec_ref)
    pairs = [height // 2] if two else [0, height // 2]
    for i, p in enumerate(pairs):
        for k in range(4):
            r = 2 * p - 2 + k
            for f in range(frames):
                slot = (k * frames + f) % rowbuf.shape[0]
                if two and r < height:
                    x = own_ref[f, jnp.where(flip == 1, height - 1 - r, r - height + 2)]
                elif 0 <= r < height:
                    x = own_ref[f, r]
                elif two:
                    x = halo_ref[f, jnp.where(flip == 1, 1 - (r - height), r - height)]
                else:
                    x = halo_ref[f, r + 2 if r < 0 else r - height + 2]
                rowbuf[slot, 8 : 8 + across, :] = x.astype(F32)
                three_taps(rowbuf, slot, x3, i * 4 + k, f, x)
    odd = y_at % 2 == 1

    def beside(at, first, second):
        first, second = first[at].astype(F32), second[at].astype(F32)
        if not two:
            return first, second
        second = jnp.where((y_at == 0) | (y_at == gy - 1), 0.0, second)
        return jnp.where(odd, first, second), jnp.where(odd, second, first)

    n_pairs = height // 2 + 1
    for p in range(n_pairs):
        for k in range(4):
            r = 2 * p - 2 + k
            to = slice(p * 4 * frames, (p + 1) * 4 * frames)
            lanes = k * 3 * chan
            if two and r < 0:
                xc[to, lanes : lanes + 3 * chan] = jnp.zeros((4 * frames, 3 * chan), BF16)
                continue
            if two and r >= height:
                at = jnp.where(flip == 1, 1 - (r - height), r - height)
                own = corner_ref[at].astype(F32)
                left, right = beside(height + at, *sides)
            else:
                at = jnp.where(flip == 1, height - 1 - r, r) if two else r + 2
                own = e_ref[at].astype(F32)
                left, right = beside(at, *sides)
            cols = [left[:frames], left[frames:]] + [own[c * frames : (c + 1) * frames] for c in range(4)]
            cols += [right[:frames], right[frames:]]
            for b in range(3):
                piece = jnp.concatenate([cols[c + b] for c in (0, 1, 4, 5)], axis=0)
                xc[to, lanes + b * chan : lanes + (b + 1) * chan] = piece.astype(BF16)
    for i, p in enumerate(pairs):
        y = pair_dot(x3, [i * 4 + k for k in range(4)], wt)
        inside = 1.0
        if not two:
            inside = has_above if p == 0 else has_below

        def keep(rr, f, s, i=i, p=p, inside=inside):
            border = (rr == 0) if p == 0 else (rr == 1)
            p_ref[2 * i + rr, f] = s * inside if border and not two else s

        for rr, s in enumerate(scan_rows(y, decays, scales, across, keep)):
            border = (rr == 0) if p == 0 else (rr == 1)
            s = s * inside if border and not two else s
            f_ref[(2 * i + rr) * across : (2 * i + rr + 1) * across, :] = s.astype(BF16)

    wide = jnp.dot(xc[...], wt[...], preferred_element_type=F32)
    for h in range(2):
        yc[h] = wide[:, h * chan : (h + 1) * chan]
    count = n_pairs * 4
    place = lax.broadcasted_iota(jnp.int32, (count, 2 * chan), 0)
    lane = lax.broadcasted_iota(jnp.int32, (count, 2 * chan), 1)
    mask = jnp.where(place % 4 == 0, has_left, jnp.where(place % 4 == 3, has_right, 1.0))
    above = (place < 4) & (lane < chan)
    if two:
        mask = jnp.where(above, 0.0, mask)
    else:
        below = (place >= count - 4) & (lane >= chan)
        mask = jnp.where(above, mask * has_above, mask)
        mask = jnp.where(below, mask * has_below, mask)
    s = None
    for f in range(frames):
        both = [jnp.concatenate([v[f : f + 1]] * 2, axis=1) for v in (decays, scales)]
        halves = [yc[h, pl.ds(f, count, stride=frames), :] for h in range(2)]
        u = both[1] * jnp.concatenate(halves, axis=1) * mask
        s = u if s is None else both[0] * s + u
        for h in range(2):
            pc_ref[h, pl.ds(f, count, stride=frames), :] = s[:, h * chan : (h + 1) * chan]
    base = len(pairs) * 2 * across
    pad = jnp.concatenate([jnp.zeros((24 - count, chan), F32), addends(decays, 8)], axis=0)
    for h in range(2):
        half = jnp.concatenate([s[:, h * chan : (h + 1) * chan], pad], axis=0)
        f_ref[base + 32 * h : base + 32 * (h + 1), :] = half.astype(BF16)
    fetch.wait()
    pair_weights(next_w, next_wt, flip)


def outer_kernel(
    two, ta, pa_ref, pb_ref, pc_ref, ra_ref, za_ref, b1_ref, b2_ref, b3_ref, dec_ref, wt, frames_ref,
    out_ref, rowbuf, x3, sc, ia, ib, done, sems,
):
    frames, height, across, chan = frames_ref.shape
    flip = mirrored(two)
    decays = dec_ref[...]
    rows_a = pa_ref.shape[0]
    base = pb_ref.shape[0] * across

    def product(ref, at):
        return jnp.sum(ref[at : at + 16, :].astype(F32)[8:16], axis=0, keepdims=True)

    if ta == 4:
        t = lax.axis_index("ta")
        end = ra_ref.shape[0]
        other = jnp.sum(ra_ref[end - 16 : end, :].astype(F32), axis=0, keepdims=True)
        last = (t == 3).astype(F32)
        one, two_on = ((t == 1) | (t == 3)).astype(F32), (t == 2).astype(F32)
        from_a = one, two_on + last * other
        d1, d2, d3 = (product(ref, base + 16) for ref in (b1_ref, b2_ref, b3_ref))
        from_b = one, two_on * d3 + last * d1, two_on + last * d1 * d2
    else:
        from_a, from_b = (1.0, 0.0), (1.0, 0.0, 0.0)
    ia[...] = sum(c * ref[0 : rows_a * across].astype(F32) for c, ref in zip(from_a, (ra_ref, za_ref)))
    ib[...] = sum(c * ref[...].astype(F32) for c, ref in zip(from_b, (b1_ref, b2_ref, b3_ref)))
    running = [decays[0:1]]
    for f in range(1, frames):
        running.append(running[-1] * decays[f : f + 1])
    count = (height // 2 + 1) * 4
    for f in range(frames):
        for h in range(2):
            part = pc_ref[h, pl.ds(f, count, stride=frames), :]
            sc[f, h, 0:count, :] = part + running[f] * ib[base + 32 * h : base + 32 * h + count, :]
    def build(n):
        if two and n == 0:
            return
        if two:
            src, at = ((pa_ref, ia), n - 1) if n < height else ((pb_ref, ib), n - height)
        elif 2 <= n < height:
            src, at = (pa_ref, ia), n - 2
        else:
            src, at = (pb_ref, ib), n if n < 2 else n - height + 2
        incoming = src[1][at * across : (at + 1) * across, :]
        for f in range(frames):
            slot = (n * frames + f) % rowbuf.shape[0]
            rowbuf[slot, 8 : 8 + across, :] = src[0][at, f].astype(F32) + running[f] * incoming
            corner = (n // 2) * 4
            h = n % 2
            rowbuf[slot, 7:9, :] = sc[f, h, corner : corner + 2, :]
            rowbuf[slot, 7 + across : 9 + across, :] = sc[f, h, corner + 2 : corner + 4, :]
            three_taps(rowbuf, slot, x3, n, f, rowbuf[slot, 8 : 8 + across, :].astype(BF16))

    def finish(p, y):
        first = jnp.where(flip == 1, height - 2 - 2 * p, 2 * p)
        for rr in range(2):
            row = jnp.where(flip == 1, 1 - rr, rr)
            for f in range(frames):
                mixed = y[f * across : (f + 1) * across, rr * chan : (rr + 1) * chan]
                frame = frames_ref[f, first + row].astype(F32)
                done[p, f, row] = (frame + jax.nn.gelu(mixed)).astype(BF16)
        copy = pltpu.make_async_copy(done.at[p], out_ref.at[:, pl.ds(first, 2)], sems.at[p])
        copy.start()
        return copy

    copies = []
    for n in range(2):
        build(n)
    for p in range(height // 2):
        build(2 * p + 2)
        build(2 * p + 3)
        slots = [n if n > 0 or not two else None for n in range(2 * p, 2 * p + 4)]
        copies.append(finish(p, pair_dot(x3, slots, wt)))
    for copy in copies:
        copy.wait()


def call(body, outs, scratch, flops, near, far=(), out_place=VMEM):
    near = [pltpu.with_memory_space_constraint(a, pltpu.VMEM) for a in near]
    far = [pltpu.with_memory_space_constraint(a, pltpu.HBM) for a in far]
    return pl.pallas_call(
        body,
        out_shape=outs,
        in_specs=[VMEM] * len(near) + [HBM] * len(far),
        out_specs=jax.tree.map(lambda _: out_place, outs),
        scratch_shapes=scratch,
        compiler_params=pltpu.CompilerParams(vmem_limit_bytes=24 * 2**20),
        cost_estimate=pl.CostEstimate(flops=flops, bytes_accessed=4 * 2**20, transcendentals=0),
    )(*near, *far)


def mirrored(two):
    return lax.axis_index("gx") if two else 0


def swapped(value, axis, count, odd_first):
    off = 1 if odd_first else 0
    pairs = [((i + off) % count, (i + 1 + off) % count) for i in range(0, count, 2)]
    return lax.ppermute(value, axis, pairs + [(b, a) for a, b in pairs])


def exchange(low, high, axis, count):
    at = lax.axis_index(axis)
    odd = at % 2 == 1
    if count % 2:
        ups, downs = [(i, i + 1) for i in range(count - 1)], [(i + 1, i) for i in range(count - 1)]
        return lax.ppermute(high, axis, ups), lax.ppermute(low, axis, downs)
    near = swapped(jnp.where(odd, low, high), axis, count, False)
    if count == 2:
        far = jnp.zeros_like(near)
    else:
        far = swapped(jnp.where(odd, high, low), axis, count, True)
        far = jnp.where((at == 0) | (at == count - 1), jnp.zeros_like(far), far)
    return jnp.where(odd, near, far), jnp.where(odd, far, near)


def carry_general(locals_, total, ta):
    t = lax.axis_index("ta")

    def moved(value, step):
        got = lax.ppermute(value, "ta", [(i, (i + step) % ta) for i in range(ta)])
        return jnp.where(t >= step, got, jnp.zeros_like(got))

    step = 1
    while step < ta:
        came = [moved(v, step) for v in locals_]
        locals_ = [(v.astype(F32) + total * m.astype(F32)).astype(BF16) for v, m in zip(locals_, came)]
        total = jnp.where(t >= step, total * moved(total, step), total)
        step *= 2
    return [moved(v, 1) for v in locals_]


def on_device(gx, gy, ta, frames_far, in_weight, out_weight, decays_far):
    n_frames, height, across, chan = frames_far.shape
    two = gx == 2 and gy > 2 and gy % 2 == 0
    t = lax.axis_index("ta")
    near_mem = pltpu.VMEM
    sent = []
    if two:
        side = (height, 2 * n_frames, chan)
        sent = [near_mem(s, BF16) for s in ((2, 4 * n_frames, chan), (n_frames, 2, across, chan), side, side)]
    frames, decays, w_in, cols, *sent = call(
        functools.partial(fetch_kernel, two),
        [
            near_mem(frames_far.shape, BF16), near_mem(decays_far.shape, F32), near_mem(in_weight.shape, BF16),
            near_mem((height, 4 * n_frames, chan), BF16), *sent,
        ],
        [pltpu.VMEM((height * 4 * n_frames, chan), F32), pltpu.SemaphoreType.DMA((3,))],
        0, [], [frames_far, decays_far, in_weight],
    )
    if two:
        facing = [(0, 1), (1, 0)]
        corner = lax.ppermute(sent[0], "gx", facing)
        halo = lax.ppermute(sent[1], "gx", facing)
    else:
        above, below = exchange(frames[:, :2], frames[:, height - 2 :], "gx", gx)
        halo = jnp.concatenate([above, below], axis=1)
        over, under = exchange(cols[:2], cols[height - 2 :], "gx", gx)
        cols = jnp.concatenate([over, cols, under])
        sides = exchange(cols[:, : 2 * n_frames], cols[:, 2 * n_frames :], "gy", gy)
        corner = cols[:2]

    rows_a = height - 1 if two else height - 2
    rows_b = 2 if two else 4
    wt = pltpu.VMEM((12 * chan, 2 * chan), BF16)
    rowbuf = pltpu.VMEM((16, across + 16, chan), F32)
    cells = n_frames * across
    flops = 2 * 9 * chan * chan * cells
    pa, fa = call(
        functools.partial(inner_kernel, two),
        (near_mem((rows_a, n_frames, across, chan), BF16), near_mem((rows_a * across + 16, chan), BF16)),
        [wt, rowbuf, pltpu.VMEM((height, cells, 3 * chan), BF16)],
        flops * height, [frames, decays, w_in],
    )

    if two:
        fa, corner = lax.optimization_barrier((fa, corner))
        odd = lax.axis_index("gy") % 2 == 1
        low, high = corner[:, : 2 * n_frames], corner[:, 2 * n_frames :]
        near = jnp.concatenate([sent[2], jnp.where(odd, low, high)])
        far = jnp.concatenate([sent[3], jnp.where(odd, high, low)])
        sides = [swapped(near, "gy", gy, False), swapped(far, "gy", gy, True)]
    total = jnp.prod(decays, axis=0)[None]
    if ta == 4:
        ra = swapped(fa, "ta", ta, False)
        other = jnp.sum(ra[rows_a * across :].astype(F32), axis=0, keepdims=True)

        def joined(mine, theirs):
            mine, theirs = mine.astype(F32), theirs.astype(F32)
            return jnp.where(t == 0, theirs + other * mine, mine + total * theirs).astype(BF16)

        across_two = [(0, 2), (2, 0), (1, 3), (3, 1)]
        ga = joined(fa, ra)
        za = lax.ppermute(ga, "ta", across_two)
        _, *sides = lax.optimization_barrier((ga, *sides))

    n_cols = (height // 2 + 1) * 4
    pb, pc, fb, wt_out = call(
        functools.partial(edge_kernel, two, gx, gy),
        (
            near_mem((rows_b, n_frames, across, chan), F32),
            near_mem((2, n_cols * n_frames, chan), F32),
            near_mem((rows_b * across + 64, chan), BF16),
            near_mem((12 * chan, 2 * chan), BF16),
        ),
        [
            pltpu.VMEM(out_weight.shape, BF16), wt, rowbuf, pltpu.VMEM((2 * rows_b, cells, 3 * chan), BF16),
            pltpu.VMEM((n_cols * n_frames, 12 * chan), BF16), pltpu.VMEM((2, n_cols * n_frames, chan), F32),
            pltpu.SemaphoreType.DMA,
        ],
        flops * rows_b, [sent[1] if two else frames, decays, w_in, halo, cols, corner, *sides], [out_weight],
    )
    if ta == 4:
        edges = [swapped(fb, "ta", ta, False), lax.ppermute(fb, "ta", across_two), swapped(fb, "ta", ta, True)]
    else:
        ra, rb = carry_general([fa, fb], total, ta)
        za, edges = ra, [rb] * 3

    return call(
        functools.partial(outer_kernel, two, ta),
        jax.ShapeDtypeStruct(frames.shape, BF16),
        [
            rowbuf, pltpu.VMEM((height + 2, cells, 3 * chan), BF16),
            pltpu.VMEM((n_frames, 2, (n_cols + 7) // 8 * 8, chan), F32),
            pltpu.VMEM((rows_a * across, chan), F32), pltpu.VMEM((rows_b * across + 64, chan), F32),
            pltpu.VMEM((height // 2, n_frames, 2, across, chan), BF16), pltpu.SemaphoreType.DMA((height // 2,)),
        ],
        flops * height, [pa, pb, pc, ra, za, *edges, decays, wt_out, frames], out_place=HBM,
    )


def solution(mesh):
    sizes = [mesh.shape[a] for a in ("gx", "gy", "ta")]
    placed = (P("ta", "gx", "gy", None), P(), P(), P("ta", None))
    return jax.shard_map(
        functools.partial(on_device, *sizes), mesh=mesh, in_specs=placed,
        out_specs=P("ta", "gx", "gy", None), check_vma=False,
    )
```

```python
import functools

import jax
import jax.numpy as jnp
from jax import lax
from jax.experimental import pallas as pl
from jax.experimental.pallas import tpu as pltpu
from jax.sharding import PartitionSpec as P

F32, BF16 = jnp.float32, jnp.bfloat16
VMEM = pl.BlockSpec(memory_space=pltpu.VMEM)
HBM = pl.BlockSpec(memory_space=pltpu.HBM)


def pair_weights(w_ref, wt, flip):
    chan_in, chan_out = w_ref.shape[2:]
    for k in range(4):
        for b in range(3):
            for rr in range(2):
                at = (k * 3 + b) * chan_in
                a = k - rr
                if 0 <= a <= 2:
                    block = w_ref[jnp.where(flip == 1, 2 - a, a), b]
                else:
                    block = jnp.zeros((chan_in, chan_out), BF16)
                wt[at : at + chan_in, rr * chan_out : (rr + 1) * chan_out] = block


def clear_margins(rowbuf):
    across = rowbuf.shape[1] - 16
    zeros = jnp.zeros((rowbuf.shape[0], 8, rowbuf.shape[2]), F32)
    rowbuf[:, 0:8, :] = zeros
    rowbuf[:, 8 + across : 16 + across, :] = zeros


def three_taps(rowbuf, slot, x3, row, f, middle):
    across = rowbuf.shape[1] - 16
    chan = rowbuf.shape[2]
    at = pl.ds(f * across, across)
    x3[row, at, 0:chan] = rowbuf[slot, 7 : 7 + across, :].astype(BF16)
    x3[row, at, chan : 2 * chan] = middle
    x3[row, at, 2 * chan : 3 * chan] = rowbuf[slot, 9 : 9 + across, :].astype(BF16)


def pair_dot(x3, slots, wt, lo=0, hi=None):
    width = x3.shape[2]
    first = next(k for k in range(4) if slots[k] is not None)
    hi = hi or x3.shape[1]
    rows = jnp.concatenate([x3[s, lo:hi, :] for s in slots[first:]], axis=1)
    return jnp.dot(rows, wt[first * width : 4 * width, :], preferred_element_type=F32)


def scan_rows(y, decays, scales, across, keep):
    frames = decays.shape[0]
    chan = decays.shape[1]
    finals = []
    for rr in range(2):
        s = None
        for f in range(frames):
            u = scales[f : f + 1] * y[f * across : (f + 1) * across, rr * chan : (rr + 1) * chan]
            s = u if s is None else decays[f : f + 1] * s + u
            keep(rr, f, s)
        finals.append(s)
    return finals


def load_decays(dec_ref):
    decays = dec_ref[...]
    return decays, jnp.sqrt(1.0 - decays * decays)


def gather_edges(src, row, edge, at):
    frames, across = src.shape[0], src.shape[2]
    for f in range(frames):
        edge[pl.ds(at + f, 2, stride=frames), :] = src[f, row, 0:16, :].astype(F32)[0:2]
        last = src[f, row, across - 16 : across, :].astype(F32)[14:16]
        edge[pl.ds(at + f + 2 * frames, 2, stride=frames), :] = last


def fetch_kernel(two, frames_hbm, dec_hbm, w_hbm, frames_ref, dec_ref, w_ref, cols_ref, *refs):
    *sent, edge, sems = refs
    pairs = [(frames_hbm, frames_ref), (dec_hbm, dec_ref), (w_hbm, w_ref)]
    copies = [pltpu.make_async_copy(src, dst, sems.at[i]) for i, (src, dst) in enumerate(pairs)]
    for copy in copies:
        copy.start()
    copies[0].wait()
    frames, height, across, chan = frames_ref.shape
    for r in range(height):
        gather_edges(frames_ref, r, edge, r * 4 * frames)
    for r in range(height):
        cols_ref[r] = edge[r * 4 * frames : (r + 1) * 4 * frames, :].astype(BF16)
    if two:
        corner_ref, halo_ref, near_ref, far_ref = sent
        odd = lax.axis_index("gy") % 2 == 1
        start = jnp.where(lax.axis_index("gx") == 1, 0, height - 2)
        halo_ref[...] = frames_ref[:, pl.ds(start, 2)]
        half = 2 * frames
        for r in range(height):
            low, high = edge[r * 2 * half : r * 2 * half + half, :], edge[r * 2 * half + half : (r + 1) * 2 * half, :]
            near_ref[r] = jnp.where(odd, low, high).astype(BF16)
            far_ref[r] = jnp.where(odd, high, low).astype(BF16)
        for i in range(2):
            corner_ref[i] = edge[pl.ds(pl.multiple_of((start + i) * 2 * half, 2 * half), 2 * half), :].astype(BF16)
    for copy in copies[1:]:
        copy.wait()


def addends(decays, rows):
    total = decays[0:1]
    for f in range(1, decays.shape[0]):
        total = total * decays[f : f + 1]
    high = total.astype(BF16).astype(F32)
    middle = (total - high).astype(BF16).astype(F32)
    low = total - high - middle
    row = lax.broadcasted_iota(jnp.int32, (rows, decays.shape[1]), 0)
    return jnp.where(row == 0, high, jnp.where(row == 1, middle, jnp.where(row == 2, low, 0.0)))


def inner_kernel(two, frames_ref, dec_ref, w_ref, p_ref, f_ref, wt, rowbuf, x3):
    frames, height, across, chan = frames_ref.shape
    flip = mirrored(two)
    pair_weights(w_ref, wt, flip)
    clear_margins(rowbuf)
    decays, scales = load_decays(dec_ref)
    def build(r):
        natural = jnp.where(flip == 1, height - 1 - r, r)
        for f in range(frames):
            slot = (r * frames + f) % rowbuf.shape[0]
            x = frames_ref[f, natural]
            rowbuf[slot, 8 : 8 + across, :] = x.astype(F32)
            three_taps(rowbuf, slot, x3, r, f, x)

    first, first_row = (0, 1) if two else (1, 0)
    for r in range(2 * first):
        build(r)
    for p in range(first, height // 2):
        build(2 * p)
        build(2 * p + 1)
        slots = [r if r >= 0 else None for r in range(2 * p - 2, 2 * p + 2)]
        y = pair_dot(x3, slots, wt)
        base = 2 * (p - first)

        def keep(rr, f, s, base=base):
            if base + rr >= first_row:
                p_ref[base + rr - first_row, f] = s.astype(BF16)

        for rr, s in enumerate(scan_rows(y, decays, scales, across, keep)):
            at = base + rr - first_row
            if at >= 0:
                f_ref[at * across : (at + 1) * across, :] = s.astype(BF16)
    end = f_ref.shape[0]
    f_ref[end - 16 : end, :] = addends(decays, 16).astype(BF16)


def edge_kernel(two, gx, gy, own_ref, dec_ref, w_ref, halo_ref, e_ref, corner_ref, *refs):
    *sides, next_hbm, p_ref, pc_ref, f_ref, next_wt, next_w, wt, rowbuf, x3, xc, yc, sem = refs
    fetch = pltpu.make_async_copy(next_hbm, next_w, sem)
    fetch.start()
    frames, across, chan = own_ref.shape[0], *own_ref.shape[2:]
    height = e_ref.shape[0] if two else own_ref.shape[1]
    flip = mirrored(two)
    x, y_at = lax.axis_index("gx"), lax.axis_index("gy")
    has_left, has_right = (y_at > 0).astype(F32), (y_at < gy - 1).astype(F32)
    has_above, has_below = (x > 0).astype(F32), (x < gx - 1).astype(F32)
    pair_weights(w_ref, wt, flip)
    clear_margins(rowbuf)
    decays, scales = load_decays(dec_ref)
    pairs = [height // 2] if two else [0, height // 2]
    for i, p in enumerate(pairs):
        for k in range(4):
            r = 2 * p - 2 + k
            for f in range(frames):
                slot = (k * frames + f) % rowbuf.shape[0]
                if two and r < height:
                    x = own_ref[f, jnp.where(flip == 1, height - 1 - r, r - height + 2)]
                elif 0 <= r < height:
                    x = own_ref[f, r]
                elif two:
                    x = halo_ref[f, jnp.where(flip == 1, 1 - (r - height), r - height)]
                else:
                    x = halo_ref[f, r + 2 if r < 0 else r - height + 2]
                rowbuf[slot, 8 : 8 + across, :] = x.astype(F32)
                three_taps(rowbuf, slot, x3, i * 4 + k, f, x)
    odd = y_at % 2 == 1

    def beside(at, first, second):
        first, second = first[at].astype(F32), second[at].astype(F32)
        if not two:
            return first, second
        second = jnp.where((y_at == 0) | (y_at == gy - 1), 0.0, second)
        return jnp.where(odd, first, second), jnp.where(odd, second, first)

    n_pairs = height // 2 + 1
    for p in range(n_pairs):
        for k in range(4):
            r = 2 * p - 2 + k
            to = slice(p * 4 * frames, (p + 1) * 4 * frames)
            lanes = k * 3 * chan
            if two and r < 0:
                xc[to, lanes : lanes + 3 * chan] = jnp.zeros((4 * frames, 3 * chan), BF16)
                continue
            if two and r >= height:
                at = jnp.where(flip == 1, 1 - (r - height), r - height)
                own = corner_ref[at].astype(F32)
                left, right = beside(height + at, *sides)
            else:
                at = jnp.where(flip == 1, height - 1 - r, r) if two else r + 2
                own = e_ref[at].astype(F32)
                left, right = beside(at, *sides)
            cols = [left[:frames], left[frames:]] + [own[c * frames : (c + 1) * frames] for c in range(4)]
            cols += [right[:frames], right[frames:]]
            for b in range(3):
                piece = jnp.concatenate([cols[c + b] for c in (0, 1, 4, 5)], axis=0)
                xc[to, lanes + b * chan : lanes + (b + 1) * chan] = piece.astype(BF16)
    for i, p in enumerate(pairs):
        y = pair_dot(x3, [i * 4 + k for k in range(4)], wt)
        inside = 1.0
        if not two:
            inside = has_above if p == 0 else has_below

        def keep(rr, f, s, i=i, p=p, inside=inside):
            border = (rr == 0) if p == 0 else (rr == 1)
            p_ref[2 * i + rr, f] = s * inside if border and not two else s

        for rr, s in enumerate(scan_rows(y, decays, scales, across, keep)):
            border = (rr == 0) if p == 0 else (rr == 1)
            s = s * inside if border and not two else s
            f_ref[(2 * i + rr) * across : (2 * i + rr + 1) * across, :] = s.astype(BF16)

    wide = jnp.dot(xc[...], wt[...], preferred_element_type=F32)
    for h in range(2):
        yc[h] = wide[:, h * chan : (h + 1) * chan]
    count = n_pairs * 4
    place = lax.broadcasted_iota(jnp.int32, (count, 2 * chan), 0)
    lane = lax.broadcasted_iota(jnp.int32, (count, 2 * chan), 1)
    mask = jnp.where(place % 4 == 0, has_left, jnp.where(place % 4 == 3, has_right, 1.0))
    above = (place < 4) & (lane < chan)
    if two:
        mask = jnp.where(above, 0.0, mask)
    else:
        below = (place >= count - 4) & (lane >= chan)
        mask = jnp.where(above, mask * has_above, mask)
        mask = jnp.where(below, mask * has_below, mask)
    s = None
    for f in range(frames):
        both = [jnp.concatenate([v[f : f + 1]] * 2, axis=1) for v in (decays, scales)]
        halves = [yc[h, pl.ds(f, count, stride=frames), :] for h in range(2)]
        u = both[1] * jnp.concatenate(halves, axis=1) * mask
        s = u if s is None else both[0] * s + u
        for h in range(2):
            pc_ref[h, pl.ds(f, count, stride=frames), :] = s[:, h * chan : (h + 1) * chan]
    base = len(pairs) * 2 * across
    gap = (-2 * count - 8) % 16
    tail = [s[:, :chan], s[:, chan:]] + ([jnp.zeros((gap, chan), F32)] if gap else [])
    f_ref[base:, :] = jnp.concatenate(tail + [addends(decays, 8)], axis=0).astype(BF16)
    fetch.wait()
    pair_weights(next_w, next_wt, flip)


def outer_kernel(
    two, ta, pa_ref, pb_ref, pc_ref, ra_ref, za_ref, b1_ref, b2_ref, b3_ref, dec_ref, wt, frames_ref,
    out_ref, rowbuf, x3, sc, ia, ib, done, sems,
):
    frames, height, across, chan = frames_ref.shape
    flip = mirrored(two)
    decays = dec_ref[...]
    rows_a = pa_ref.shape[0]
    base = pb_ref.shape[0] * across

    def product(ref):
        end = ref.shape[0]
        return jnp.sum(ref[end - 16 : end, :].astype(F32)[8:16], axis=0, keepdims=True)

    if ta == 4:
        t = lax.axis_index("ta")
        end = ra_ref.shape[0]
        other = jnp.sum(ra_ref[end - 16 : end, :].astype(F32), axis=0, keepdims=True)
        last = (t == 3).astype(F32)
        one, two_on = ((t == 1) | (t == 3)).astype(F32), (t == 2).astype(F32)
        from_a = one, two_on + last * other
        d1, d2, d3 = (product(ref) for ref in (b1_ref, b2_ref, b3_ref))
        from_b = one, two_on * d3 + last * d1, two_on + last * d1 * d2
    else:
        from_a, from_b = (1.0, 0.0), (1.0, 0.0, 0.0)
    ia[...] = sum(c * ref[0 : rows_a * across].astype(F32) for c, ref in zip(from_a, (ra_ref, za_ref)))
    ib[...] = sum(c * ref[...].astype(F32) for c, ref in zip(from_b, (b1_ref, b2_ref, b3_ref)))
    running = [decays[0:1]]
    for f in range(1, frames):
        running.append(running[-1] * decays[f : f + 1])
    count = (height // 2 + 1) * 4
    for f in range(frames):
        for h in range(2):
            part = pc_ref[h, pl.ds(f, count, stride=frames), :]
            sc[f, h, 0:count, :] = part + running[f] * ib[base + count * h : base + count * (h + 1), :]
    def build(n, fs):
        if two and n == 0:
            return
        if two:
            src, at = ((pa_ref, ia), n - 1) if n < height else ((pb_ref, ib), n - height)
        elif 2 <= n < height:
            src, at = (pa_ref, ia), n - 2
        else:
            src, at = (pb_ref, ib), n if n < 2 else n - height + 2
        incoming = src[1][at * across : (at + 1) * across, :]
        for f in fs:
            slot = (n * frames + f) % rowbuf.shape[0]
            rowbuf[slot, 8 : 8 + across, :] = src[0][at, f].astype(F32) + running[f] * incoming
            corner = (n // 2) * 4
            h = n % 2
            rowbuf[slot, 7:9, :] = sc[f, h, corner : corner + 2, :]
            rowbuf[slot, 7 + across : 9 + across, :] = sc[f, h, corner + 2 : corner + 4, :]
            three_taps(rowbuf, slot, x3, n, f, rowbuf[slot, 8 : 8 + across, :].astype(BF16))

    def finish(p, fs, y):
        for rr in range(2):
            natural = jnp.where(flip == 1, height - 1 - (2 * p + rr), 2 * p + rr)
            for i, f in enumerate(fs):
                mixed = y[i * across : (i + 1) * across, rr * chan : (rr + 1) * chan]
                frame = frames_ref[f, natural].astype(F32)
                done[2 * p + rr, f] = (frame + jax.nn.gelu(mixed)).astype(BF16)
            if fs[-1] == frames - 1:
                copy = pltpu.make_async_copy(done.at[2 * p + rr], out_ref.at[:, natural], sems.at[2 * p + rr])
                copy.start()
                copies.append(copy)

    copies, waiting = [], None
    parts = [range(i, i + 4) for i in range(0, frames, 4)]
    for fs in parts:
        for n in range(4):
            build(n, fs)
    for p in range(height // 2):
        slots = [n if n > 0 or not two else None for n in range(2 * p, 2 * p + 4)]
        for fs in parts:
            y = pair_dot(x3, slots, wt, fs[0] * across, (fs[-1] + 1) * across)
            if waiting:
                finish(*waiting)
            waiting = (p, fs, y)
            for n in (2 * p + 4, 2 * p + 5):
                if n < height + 2:
                    build(n, fs)
    finish(*waiting)
    for copy in copies:
        copy.wait()


def call(body, outs, scratch, flops, near, far=(), out_place=VMEM):
    near = [pltpu.with_memory_space_constraint(a, pltpu.VMEM) for a in near]
    far = [pltpu.with_memory_space_constraint(a, pltpu.HBM) for a in far]
    return pl.pallas_call(
        body,
        out_shape=outs,
        in_specs=[VMEM] * len(near) + [HBM] * len(far),
        out_specs=jax.tree.map(lambda _: out_place, outs),
        scratch_shapes=scratch,
        compiler_params=pltpu.CompilerParams(vmem_limit_bytes=24 * 2**20),
        cost_estimate=pl.CostEstimate(flops=flops, bytes_accessed=4 * 2**20, transcendentals=0),
    )(*near, *far)


def mirrored(two):
    return lax.axis_index("gx") if two else 0


def swapped(value, axis, count, odd_first):
    off = 1 if odd_first else 0
    pairs = [((i + off) % count, (i + 1 + off) % count) for i in range(0, count, 2)]
    return lax.ppermute(value, axis, pairs + [(b, a) for a, b in pairs])


def exchange(low, high, axis, count):
    at = lax.axis_index(axis)
    odd = at % 2 == 1
    if count % 2:
        ups, downs = [(i, i + 1) for i in range(count - 1)], [(i + 1, i) for i in range(count - 1)]
        return lax.ppermute(high, axis, ups), lax.ppermute(low, axis, downs)
    near = swapped(jnp.where(odd, low, high), axis, count, False)
    if count == 2:
        far = jnp.zeros_like(near)
    else:
        far = swapped(jnp.where(odd, high, low), axis, count, True)
        far = jnp.where((at == 0) | (at == count - 1), jnp.zeros_like(far), far)
    return jnp.where(odd, near, far), jnp.where(odd, far, near)


def carry_general(locals_, total, ta):
    t = lax.axis_index("ta")

    def moved(value, step):
        got = lax.ppermute(value, "ta", [(i, (i + step) % ta) for i in range(ta)])
        return jnp.where(t >= step, got, jnp.zeros_like(got))

    step = 1
    while step < ta:
        came = [moved(v, step) for v in locals_]
        locals_ = [(v.astype(F32) + total * m.astype(F32)).astype(BF16) for v, m in zip(locals_, came)]
        total = jnp.where(t >= step, total * moved(total, step), total)
        step *= 2
    return [moved(v, 1) for v in locals_]


def on_device(gx, gy, ta, frames_far, in_weight, out_weight, decays_far):
    n_frames, height, across, chan = frames_far.shape
    two = gx == 2 and gy > 2 and gy % 2 == 0
    t = lax.axis_index("ta")
    near_mem = pltpu.VMEM
    sent = []
    if two:
        side = (height, 2 * n_frames, chan)
        sent = [near_mem(s, BF16) for s in ((2, 4 * n_frames, chan), (n_frames, 2, across, chan), side, side)]
    frames, decays, w_in, cols, *sent = call(
        functools.partial(fetch_kernel, two),
        [
            near_mem(frames_far.shape, BF16), near_mem(decays_far.shape, F32), near_mem(in_weight.shape, BF16),
            near_mem((height, 4 * n_frames, chan), BF16), *sent,
        ],
        [pltpu.VMEM((height * 4 * n_frames, chan), F32), pltpu.SemaphoreType.DMA((3,))],
        0, [], [frames_far, decays_far, in_weight],
    )
    if two:
        facing = [(0, 1), (1, 0)]
        corner = lax.ppermute(sent[0], "gx", facing)
        halo = lax.ppermute(sent[1], "gx", facing)
    else:
        above, below = exchange(frames[:, :2], frames[:, height - 2 :], "gx", gx)
        halo = jnp.concatenate([above, below], axis=1)
        over, under = exchange(cols[:2], cols[height - 2 :], "gx", gx)
        cols = jnp.concatenate([over, cols, under])
        sides = exchange(cols[:, : 2 * n_frames], cols[:, 2 * n_frames :], "gy", gy)
        corner = cols[:2]

    rows_a = height - 1 if two else height - 2
    rows_b = 2 if two else 4
    wt = pltpu.VMEM((12 * chan, 2 * chan), BF16)
    rowbuf = pltpu.VMEM((16, across + 16, chan), F32)
    cells = n_frames * across
    flops = 2 * 9 * chan * chan * cells
    pa, fa = call(
        functools.partial(inner_kernel, two),
        (near_mem((rows_a, n_frames, across, chan), BF16), near_mem((rows_a * across + 16, chan), BF16)),
        [wt, rowbuf, pltpu.VMEM((height, cells, 3 * chan), BF16)],
        flops * height, [frames, decays, w_in],
    )

    if two:
        fa, corner = lax.optimization_barrier((fa, corner))
        odd = lax.axis_index("gy") % 2 == 1
        low, high = corner[:, : 2 * n_frames], corner[:, 2 * n_frames :]
        near = jnp.concatenate([sent[2]] + [jnp.where(odd, low, high)] * 2)
        far = jnp.concatenate([sent[3]] + [jnp.where(odd, high, low)] * 2)
        sides = [swapped(near, "gy", gy, False), swapped(far, "gy", gy, True)]
    total = jnp.prod(decays, axis=0)[None]
    if ta == 4:
        ra = swapped(fa, "ta", ta, False)
        other = jnp.sum(ra[rows_a * across :].astype(F32), axis=0, keepdims=True)

        def joined(mine, theirs):
            mine, theirs = mine.astype(F32), theirs.astype(F32)
            return jnp.where(t == 0, theirs + other * mine, mine + total * theirs).astype(BF16)

        across_two = [(0, 2), (2, 0), (1, 3), (3, 1)]
        ga = joined(fa, ra)
        za = lax.ppermute(ga, "ta", across_two)
        _, *sides = lax.optimization_barrier((ga, *sides))

    n_cols = (height // 2 + 1) * 4
    tail_rows = (2 * n_cols + 8 + 15) // 16 * 16
    pb, pc, fb, wt_out = call(
        functools.partial(edge_kernel, two, gx, gy),
        (
            near_mem((rows_b, n_frames, across, chan), F32),
            near_mem((2, n_cols * n_frames, chan), F32),
            near_mem((rows_b * across + tail_rows, chan), BF16),
            near_mem((12 * chan, 2 * chan), BF16),
        ),
        [
            pltpu.VMEM(out_weight.shape, BF16), wt, rowbuf, pltpu.VMEM((2 * rows_b, cells, 3 * chan), BF16),
            pltpu.VMEM((n_cols * n_frames, 12 * chan), BF16), pltpu.VMEM((2, n_cols * n_frames, chan), F32),
            pltpu.SemaphoreType.DMA,
        ],
        flops * rows_b, [sent[1] if two else frames, decays, w_in, halo, cols, corner, *sides], [out_weight],
    )
    if ta == 4:
        edges = [swapped(fb, "ta", ta, False), lax.ppermute(fb, "ta", across_two), swapped(fb, "ta", ta, True)]
    else:
        ra, rb = carry_general([fa, fb], total, ta)
        za, edges = ra, [rb] * 3

    return call(
        functools.partial(outer_kernel, two, ta),
        jax.ShapeDtypeStruct(frames.shape, BF16),
        [
            rowbuf, pltpu.VMEM((height + 2, cells, 3 * chan), BF16),
            pltpu.VMEM((n_frames, 2, (n_cols + 7) // 8 * 8, chan), F32),
            pltpu.VMEM((rows_a * across, chan), F32), pltpu.VMEM((rows_b * across + tail_rows, chan), F32),
            pltpu.VMEM((height, n_frames, across, chan), BF16), pltpu.SemaphoreType.DMA((height,)),
        ],
        flops * height, [pa, pb, pc, ra, za, *edges, decays, wt_out, frames], out_place=HBM,
    )


def solution(mesh):
    sizes = [mesh.shape[a] for a in ("gx", "gy", "ta")]
    placed = (P("ta", "gx", "gy", None), P(), P(), P("ta", None))
    return jax.shard_map(
        functools.partial(on_device, *sizes), mesh=mesh, in_specs=placed,
        out_specs=P("ta", "gx", "gy", None), check_vma=False,
    )
```

```python
import functools

import jax
import jax.numpy as jnp
from jax import lax
from jax.experimental import pallas as pl
from jax.experimental.pallas import tpu as pltpu
from jax.sharding import PartitionSpec as P

F32, BF16 = jnp.float32, jnp.bfloat16
VMEM = pl.BlockSpec(memory_space=pltpu.VMEM)
HBM = pl.BlockSpec(memory_space=pltpu.HBM)


def pair_weights(w_ref, wt, flip):
    chan_in, chan_out = w_ref.shape[2:]
    for k in range(4):
        for b in range(3):
            for rr in range(2):
                at = (k * 3 + b) * chan_in
                a = k - rr
                if 0 <= a <= 2:
                    block = w_ref[jnp.where(flip == 1, 2 - a, a), b]
                else:
                    block = jnp.zeros((chan_in, chan_out), BF16)
                wt[at : at + chan_in, rr * chan_out : (rr + 1) * chan_out] = block


def clear_margins(rowbuf):
    across = rowbuf.shape[1] - 16
    zeros = jnp.zeros((rowbuf.shape[0], 8, rowbuf.shape[2]), F32)
    rowbuf[:, 0:8, :] = zeros
    rowbuf[:, 8 + across : 16 + across, :] = zeros


def three_taps(rowbuf, slot, x3, row, f, middle):
    across = rowbuf.shape[1] - 16
    chan = rowbuf.shape[2]
    at = pl.ds(f * across, across)
    x3[row, at, 0:chan] = rowbuf[slot, 7 : 7 + across, :].astype(BF16)
    x3[row, at, chan : 2 * chan] = middle
    x3[row, at, 2 * chan : 3 * chan] = rowbuf[slot, 9 : 9 + across, :].astype(BF16)


def pair_dot(x3, slots, wt, lo=0, hi=None):
    width = x3.shape[2]
    first = next(k for k in range(4) if slots[k] is not None)
    hi = hi or x3.shape[1]
    rows = jnp.concatenate([x3[s, lo:hi, :] for s in slots[first:]], axis=1)
    return jnp.dot(rows, wt[first * width : 4 * width, :], preferred_element_type=F32)


def scan_rows(y, decays, scales, across, keep):
    frames = decays.shape[0]
    chan = decays.shape[1]
    finals = []
    for rr in range(2):
        s = None
        for f in range(frames):
            u = scales[f : f + 1] * y[f * across : (f + 1) * across, rr * chan : (rr + 1) * chan]
            s = u if s is None else decays[f : f + 1] * s + u
            keep(rr, f, s)
        finals.append(s)
    return finals


def load_decays(dec_ref):
    decays = dec_ref[...]
    return decays, jnp.sqrt(1.0 - decays * decays)


def gather_edges(src, row, edge, at):
    frames, across = src.shape[0], src.shape[2]
    for f in range(frames):
        edge[pl.ds(at + f, 2, stride=frames), :] = src[f, row, 0:16, :].astype(F32)[0:2]
        last = src[f, row, across - 16 : across, :].astype(F32)[14:16]
        edge[pl.ds(at + f + 2 * frames, 2, stride=frames), :] = last


def fetch_kernel(two, frames_hbm, dec_hbm, w_hbm, frames_ref, dec_ref, w_ref, cols_ref, *refs):
    *sent, edge, sems = refs
    pairs = [(frames_hbm, frames_ref), (dec_hbm, dec_ref), (w_hbm, w_ref)]
    copies = [pltpu.make_async_copy(src, dst, sems.at[i]) for i, (src, dst) in enumerate(pairs)]
    for copy in copies:
        copy.start()
    copies[0].wait()
    frames, height, across, chan = frames_ref.shape
    for r in range(height):
        gather_edges(frames_ref, r, edge, r * 4 * frames)
    for r in range(height):
        cols_ref[r] = edge[r * 4 * frames : (r + 1) * 4 * frames, :].astype(BF16)
    if two:
        corner_ref, halo_ref, near_ref, far_ref = sent
        odd = lax.axis_index("gy") % 2 == 1
        start = jnp.where(lax.axis_index("gx") == 1, 0, height - 2)
        halo_ref[...] = frames_ref[:, pl.ds(start, 2)]
        half = 2 * frames
        for r in range(height):
            low, high = edge[r * 2 * half : r * 2 * half + half, :], edge[r * 2 * half + half : (r + 1) * 2 * half, :]
            near_ref[r] = jnp.where(odd, low, high).astype(BF16)
            far_ref[r] = jnp.where(odd, high, low).astype(BF16)
        for i in range(2):
            corner_ref[i] = edge[pl.ds(pl.multiple_of((start + i) * 2 * half, 2 * half), 2 * half), :].astype(BF16)
    for copy in copies[1:]:
        copy.wait()


def addends(decays, rows):
    total = decays[0:1]
    for f in range(1, decays.shape[0]):
        total = total * decays[f : f + 1]
    high = total.astype(BF16).astype(F32)
    middle = (total - high).astype(BF16).astype(F32)
    low = total - high - middle
    row = lax.broadcasted_iota(jnp.int32, (rows, decays.shape[1]), 0)
    return jnp.where(row == 0, high, jnp.where(row == 1, middle, jnp.where(row == 2, low, 0.0)))


def inner_kernel(two, frames_ref, dec_ref, w_ref, p_ref, f_ref, wt, rowbuf, x3):
    frames, height, across, chan = frames_ref.shape
    flip = mirrored(two)
    pair_weights(w_ref, wt, flip)
    clear_margins(rowbuf)
    decays, scales = load_decays(dec_ref)
    def build(r):
        natural = jnp.where(flip == 1, height - 1 - r, r)
        for f in range(frames):
            slot = (r * frames + f) % rowbuf.shape[0]
            x = frames_ref[f, natural]
            rowbuf[slot, 8 : 8 + across, :] = x.astype(F32)
            three_taps(rowbuf, slot, x3, r, f, x)

    first, first_row = (0, 1) if two else (1, 0)
    for r in range(2 * first):
        build(r)
    for p in range(first, height // 2):
        build(2 * p)
        build(2 * p + 1)
        slots = [r if r >= 0 else None for r in range(2 * p - 2, 2 * p + 2)]
        y = pair_dot(x3, slots, wt)
        base = 2 * (p - first)

        def keep(rr, f, s, base=base):
            if base + rr >= first_row:
                p_ref[base + rr - first_row, f] = s.astype(BF16)

        for rr, s in enumerate(scan_rows(y, decays, scales, across, keep)):
            at = base + rr - first_row
            if at >= 0:
                f_ref[at * across : (at + 1) * across, :] = s.astype(BF16)
    end = f_ref.shape[0]
    f_ref[end - 16 : end, :] = addends(decays, 16).astype(BF16)


def edge_kernel(two, gx, gy, own_ref, dec_ref, w_ref, halo_ref, e_ref, corner_ref, *refs):
    *sides, next_hbm, p_ref, pc_ref, f_ref, next_wt, next_w, wt, rowbuf, x3, xc, yc, sem = refs
    fetch = pltpu.make_async_copy(next_hbm, next_w, sem)
    fetch.start()
    frames, across, chan = own_ref.shape[0], *own_ref.shape[2:]
    height = e_ref.shape[0] if two else own_ref.shape[1]
    flip = mirrored(two)
    x, y_at = lax.axis_index("gx"), lax.axis_index("gy")
    has_left, has_right = (y_at > 0).astype(F32), (y_at < gy - 1).astype(F32)
    has_above, has_below = (x > 0).astype(F32), (x < gx - 1).astype(F32)
    pair_weights(w_ref, wt, flip)
    clear_margins(rowbuf)
    decays, scales = load_decays(dec_ref)
    pairs = [height // 2] if two else [0, height // 2]
    for i, p in enumerate(pairs):
        for k in range(4):
            r = 2 * p - 2 + k
            for f in range(frames):
                slot = (k * frames + f) % rowbuf.shape[0]
                if two and r < height:
                    x = own_ref[f, jnp.where(flip == 1, height - 1 - r, r - height + 2)]
                elif 0 <= r < height:
                    x = own_ref[f, r]
                elif two:
                    x = halo_ref[f, jnp.where(flip == 1, 1 - (r - height), r - height)]
                else:
                    x = halo_ref[f, r + 2 if r < 0 else r - height + 2]
                rowbuf[slot, 8 : 8 + across, :] = x.astype(F32)
                three_taps(rowbuf, slot, x3, i * 4 + k, f, x)
    odd = y_at % 2 == 1

    def beside(at, first, second):
        first, second = first[at].astype(F32), second[at].astype(F32)
        if not two:
            return first, second
        second = jnp.where((y_at == 0) | (y_at == gy - 1), 0.0, second)
        return jnp.where(odd, first, second), jnp.where(odd, second, first)

    n_pairs = height // 2 + 1
    for p in range(n_pairs):
        for k in range(4):
            r = 2 * p - 2 + k
            to = slice(p * 4 * frames, (p + 1) * 4 * frames)
            lanes = k * 3 * chan
            if two and r < 0:
                xc[to, lanes : lanes + 3 * chan] = jnp.zeros((4 * frames, 3 * chan), BF16)
                continue
            if two and r >= height:
                at = jnp.where(flip == 1, 1 - (r - height), r - height)
                own = corner_ref[at].astype(F32)
                left, right = beside(height + at, *sides)
            else:
                at = jnp.where(flip == 1, height - 1 - r, r) if two else r + 2
                own = e_ref[at].astype(F32)
                left, right = beside(at, *sides)
            cols = [left[:frames], left[frames:]] + [own[c * frames : (c + 1) * frames] for c in range(4)]
            cols += [right[:frames], right[frames:]]
            for b in range(3):
                piece = jnp.concatenate([cols[c + b] for c in (0, 1, 4, 5)], axis=0)
                xc[to, lanes + b * chan : lanes + (b + 1) * chan] = piece.astype(BF16)
    for i, p in enumerate(pairs):
        y = pair_dot(x3, [i * 4 + k for k in range(4)], wt)
        inside = 1.0
        if not two:
            inside = has_above if p == 0 else has_below

        def keep(rr, f, s, i=i, p=p, inside=inside):
            border = (rr == 0) if p == 0 else (rr == 1)
            p_ref[2 * i + rr, f] = s * inside if border and not two else s

        for rr, s in enumerate(scan_rows(y, decays, scales, across, keep)):
            border = (rr == 0) if p == 0 else (rr == 1)
            s = s * inside if border and not two else s
            f_ref[(2 * i + rr) * across : (2 * i + rr + 1) * across, :] = s.astype(BF16)

    wide = jnp.dot(xc[...], wt[...], preferred_element_type=F32)
    for h in range(2):
        yc[h] = wide[:, h * chan : (h + 1) * chan]
    count = n_pairs * 4
    place = lax.broadcasted_iota(jnp.int32, (count, 2 * chan), 0)
    lane = lax.broadcasted_iota(jnp.int32, (count, 2 * chan), 1)
    mask = jnp.where(place % 4 == 0, has_left, jnp.where(place % 4 == 3, has_right, 1.0))
    above = (place < 4) & (lane < chan)
    if two:
        mask = jnp.where(above, 0.0, mask)
    else:
        below = (place >= count - 4) & (lane >= chan)
        mask = jnp.where(above, mask * has_above, mask)
        mask = jnp.where(below, mask * has_below, mask)
    s = None
    for f in range(frames):
        both = [jnp.concatenate([v[f : f + 1]] * 2, axis=1) for v in (decays, scales)]
        halves = [yc[h, pl.ds(f, count, stride=frames), :] for h in range(2)]
        u = both[1] * jnp.concatenate(halves, axis=1) * mask
        s = u if s is None else both[0] * s + u
        for h in range(2):
            pc_ref[h, pl.ds(f, count, stride=frames), :] = s[:, h * chan : (h + 1) * chan]
    base = len(pairs) * 2 * across
    gap = (-2 * count - 8) % 16
    tail = [s[:, :chan], s[:, chan:]] + ([jnp.zeros((gap, chan), F32)] if gap else [])
    f_ref[base:, :] = jnp.concatenate(tail + [addends(decays, 8)], axis=0).astype(BF16)
    fetch.wait()
    pair_weights(next_w, next_wt, flip)


def outer_kernel(two, ta, early, n_in, *refs):
    pa_ref, pb_ref, pc_ref, dec_ref, wt, frames_ref, *others = refs[:n_in]
    out_ref, *scratch = refs[n_in:]
    if ta != 4:
        finish_frames(two, ta, early, pa_ref, pb_ref, pc_ref, dec_ref, wt, frames_ref, others, out_ref, *scratch)
        return
    here = lax.axis_index("ta") == 0 if early else lax.axis_index("ta") > 0

    @pl.when(here)
    def _():
        finish_frames(two, ta, early, pa_ref, pb_ref, pc_ref, dec_ref, wt, frames_ref, others, out_ref, *scratch)


def finish_frames(
    two, ta, early, pa_ref, pb_ref, pc_ref, dec_ref, wt, frames_ref, others,
    out_ref, rowbuf, x3, sc, ia, ib, done, sems,
):
    frames, height, across, chan = frames_ref.shape
    flip = mirrored(two)
    decays = dec_ref[...]
    rows_a = pa_ref.shape[0]
    base = pb_ref.shape[0] * across

    def product(ref):
        end = ref.shape[0]
        return jnp.sum(ref[end - 16 : end, :].astype(F32)[8:16], axis=0, keepdims=True)

    t = lax.axis_index("ta")
    if early:
        ia[...] = jnp.zeros_like(ia)
        ib[...] = jnp.zeros_like(ib)
    elif ta != 4:
        ia[...] = others[0][0 : rows_a * across].astype(F32)
        ib[...] = others[1][...].astype(F32)
    else:
        ra_ref, b1_ref, b2_ref, b3_ref, za_ref = others[:5]
        end = ra_ref.shape[0]
        other = jnp.sum(ra_ref[end - 16 : end, :].astype(F32), axis=0, keepdims=True)
        last = (t == 3).astype(F32)
        one, two_on = (t == 1).astype(F32) + last, (t == 2).astype(F32)
        from_a = one, two_on + last * other
        d1, d2, d3 = (product(ref) for ref in (b1_ref, b2_ref, b3_ref))
        from_b = one, two_on * d3 + last * d1, two_on + last * d1 * d2
        ia[...] = sum(c * ref[0 : rows_a * across].astype(F32) for c, ref in zip(from_a, (ra_ref, za_ref)))
        ib[...] = sum(c * ref[...].astype(F32) for c, ref in zip(from_b, (b1_ref, b2_ref, b3_ref)))
    running = [decays[0:1]]
    for f in range(1, frames):
        running.append(running[-1] * decays[f : f + 1])
    count = (height // 2 + 1) * 4
    for f in range(frames):
        for h in range(2):
            part = pc_ref[h, pl.ds(f, count, stride=frames), :]
            sc[f, h, 0:count, :] = part + running[f] * ib[base + count * h : base + count * (h + 1), :]
    def build(n, fs):
        if two and n == 0:
            return
        if two:
            src, at = ((pa_ref, ia), n - 1) if n < height else ((pb_ref, ib), n - height)
        elif 2 <= n < height:
            src, at = (pa_ref, ia), n - 2
        else:
            src, at = (pb_ref, ib), n if n < 2 else n - height + 2
        incoming = src[1][at * across : (at + 1) * across, :]
        for f in fs:
            slot = (n * frames + f) % rowbuf.shape[0]
            rowbuf[slot, 8 : 8 + across, :] = src[0][at, f].astype(F32) + running[f] * incoming
            corner = (n // 2) * 4
            h = n % 2
            rowbuf[slot, 7:9, :] = sc[f, h, corner : corner + 2, :]
            rowbuf[slot, 7 + across : 9 + across, :] = sc[f, h, corner + 2 : corner + 4, :]
            three_taps(rowbuf, slot, x3, n, f, rowbuf[slot, 8 : 8 + across, :].astype(BF16))

    def finish(p, fs, y):
        for rr in range(2):
            natural = jnp.where(flip == 1, height - 1 - (2 * p + rr), 2 * p + rr)
            for i, f in enumerate(fs):
                mixed = y[i * across : (i + 1) * across, rr * chan : (rr + 1) * chan]
                frame = frames_ref[f, natural].astype(F32)
                done[2 * p + rr, f] = (frame + jax.nn.gelu(mixed)).astype(BF16)
            if fs[-1] == frames - 1:
                copy = pltpu.make_async_copy(done.at[2 * p + rr], out_ref.at[:, natural], sems.at[2 * p + rr])
                copy.start()
                copies.append(copy)

    copies, waiting = [], None
    parts = [range(i, i + 4) for i in range(0, frames, 4)]
    for fs in parts:
        for n in range(4):
            build(n, fs)
    for p in range(height // 2):
        slots = [n if n > 0 or not two else None for n in range(2 * p, 2 * p + 4)]
        for fs in parts:
            y = pair_dot(x3, slots, wt, fs[0] * across, (fs[-1] + 1) * across)
            if waiting:
                finish(*waiting)
            waiting = (p, fs, y)
            for n in (2 * p + 4, 2 * p + 5):
                if n < height + 2:
                    build(n, fs)
    finish(*waiting)
    for copy in copies:
        copy.wait()


def call(body, outs, scratch, flops, near, far=(), out_place=VMEM, aliases=None):
    near = [pltpu.with_memory_space_constraint(a, pltpu.VMEM) for a in near]
    far = [pltpu.with_memory_space_constraint(a, pltpu.HBM) for a in far]
    return pl.pallas_call(
        body,
        out_shape=outs,
        in_specs=[VMEM] * len(near) + [HBM] * len(far),
        out_specs=jax.tree.map(lambda _: out_place, outs),
        scratch_shapes=scratch,
        input_output_aliases=aliases or {},
        compiler_params=pltpu.CompilerParams(vmem_limit_bytes=24 * 2**20),
        cost_estimate=pl.CostEstimate(flops=flops, bytes_accessed=4 * 2**20, transcendentals=0),
    )(*near, *far)


def mirrored(two):
    return lax.axis_index("gx") if two else 0


def swapped(value, axis, count, odd_first):
    off = 1 if odd_first else 0
    pairs = [((i + off) % count, (i + 1 + off) % count) for i in range(0, count, 2)]
    return lax.ppermute(value, axis, pairs + [(b, a) for a, b in pairs])


def exchange(low, high, axis, count):
    at = lax.axis_index(axis)
    odd = at % 2 == 1
    if count % 2:
        ups, downs = [(i, i + 1) for i in range(count - 1)], [(i + 1, i) for i in range(count - 1)]
        return lax.ppermute(high, axis, ups), lax.ppermute(low, axis, downs)
    near = swapped(jnp.where(odd, low, high), axis, count, False)
    if count == 2:
        far = jnp.zeros_like(near)
    else:
        far = swapped(jnp.where(odd, high, low), axis, count, True)
        far = jnp.where((at == 0) | (at == count - 1), jnp.zeros_like(far), far)
    return jnp.where(odd, near, far), jnp.where(odd, far, near)


def carry_general(locals_, total, ta):
    t = lax.axis_index("ta")

    def moved(value, step):
        got = lax.ppermute(value, "ta", [(i, (i + step) % ta) for i in range(ta)])
        return jnp.where(t >= step, got, jnp.zeros_like(got))

    step = 1
    while step < ta:
        came = [moved(v, step) for v in locals_]
        locals_ = [(v.astype(F32) + total * m.astype(F32)).astype(BF16) for v, m in zip(locals_, came)]
        total = jnp.where(t >= step, total * moved(total, step), total)
        step *= 2
    return [moved(v, 1) for v in locals_]


def on_device(gx, gy, ta, frames_far, in_weight, out_weight, decays_far):
    n_frames, height, across, chan = frames_far.shape
    two = gx == 2 and gy > 2 and gy % 2 == 0
    t = lax.axis_index("ta")
    near_mem = pltpu.VMEM
    sent = []
    if two:
        side = (height, 2 * n_frames, chan)
        sent = [near_mem(s, BF16) for s in ((2, 4 * n_frames, chan), (n_frames, 2, across, chan), side, side)]
    frames, decays, w_in, cols, *sent = call(
        functools.partial(fetch_kernel, two),
        [
            near_mem(frames_far.shape, BF16), near_mem(decays_far.shape, F32), near_mem(in_weight.shape, BF16),
            near_mem((height, 4 * n_frames, chan), BF16), *sent,
        ],
        [pltpu.VMEM((height * 4 * n_frames, chan), F32), pltpu.SemaphoreType.DMA((3,))],
        0, [], [frames_far, decays_far, in_weight],
    )
    if two:
        facing = [(0, 1), (1, 0)]
        corner = lax.ppermute(sent[0], "gx", facing)
        halo = lax.ppermute(sent[1], "gx", facing)
    else:
        above, below = exchange(frames[:, :2], frames[:, height - 2 :], "gx", gx)
        halo = jnp.concatenate([above, below], axis=1)
        over, under = exchange(cols[:2], cols[height - 2 :], "gx", gx)
        cols = jnp.concatenate([over, cols, under])
        sides = exchange(cols[:, : 2 * n_frames], cols[:, 2 * n_frames :], "gy", gy)
        corner = cols[:2]

    rows_a = height - 1 if two else height - 2
    rows_b = 2 if two else 4
    wt = pltpu.VMEM((12 * chan, 2 * chan), BF16)
    rowbuf = pltpu.VMEM((16, across + 16, chan), F32)
    cells = n_frames * across
    flops = 2 * 9 * chan * chan * cells
    pa, fa = call(
        functools.partial(inner_kernel, two),
        (near_mem((rows_a, n_frames, across, chan), BF16), near_mem((rows_a * across + 16, chan), BF16)),
        [wt, rowbuf, pltpu.VMEM((height, cells, 3 * chan), BF16)],
        flops * height, [frames, decays, w_in],
    )

    if two:
        fa, corner = lax.optimization_barrier((fa, corner))
        odd = lax.axis_index("gy") % 2 == 1
        low, high = corner[:, : 2 * n_frames], corner[:, 2 * n_frames :]
        near = jnp.concatenate([sent[2]] + [jnp.where(odd, low, high)] * 2)
        far = jnp.concatenate([sent[3]] + [jnp.where(odd, high, low)] * 2)
        sides = [swapped(near, "gy", gy, False), swapped(far, "gy", gy, True)]
    total = jnp.prod(decays, axis=0)[None]
    if ta == 4:
        ra = swapped(fa, "ta", ta, False)
        other = jnp.sum(ra[rows_a * across :].astype(F32), axis=0, keepdims=True)

        def joined(mine, theirs):
            mine, theirs = mine.astype(F32), theirs.astype(F32)
            return jnp.where(t == 0, theirs + other * mine, mine + total * theirs).astype(BF16)

        across_two = [(0, 2), (2, 0), (1, 3), (3, 1)]
        ga = joined(fa, ra)
        za = lax.ppermute(ga, "ta", across_two)
        _, *sides = lax.optimization_barrier((ga, *sides))

    n_cols = (height // 2 + 1) * 4
    tail_rows = (2 * n_cols + 8 + 15) // 16 * 16
    pb, pc, fb, wt_out = call(
        functools.partial(edge_kernel, two, gx, gy),
        (
            near_mem((rows_b, n_frames, across, chan), F32),
            near_mem((2, n_cols * n_frames, chan), F32),
            near_mem((rows_b * across + tail_rows, chan), BF16),
            near_mem((12 * chan, 2 * chan), BF16),
        ),
        [
            pltpu.VMEM(out_weight.shape, BF16), wt, rowbuf, pltpu.VMEM((2 * rows_b, cells, 3 * chan), BF16),
            pltpu.VMEM((n_cols * n_frames, 12 * chan), BF16), pltpu.VMEM((2, n_cols * n_frames, chan), F32),
            pltpu.SemaphoreType.DMA,
        ],
        flops * rows_b, [sent[1] if two else frames, decays, w_in, halo, cols, corner, *sides], [out_weight],
    )
    if ta == 4:
        edges = [swapped(fb, "ta", ta, False), lax.ppermute(fb, "ta", across_two), swapped(fb, "ta", ta, True)]
    else:
        ra, rb = carry_general([fa, fb], total, ta)
        za, edges = ra, [rb] * 3

    def last_kernel(early, near, far=()):
        return call(
            functools.partial(outer_kernel, two, ta, early, len(near) + len(far)),
            jax.ShapeDtypeStruct(frames.shape, BF16),
            [
                rowbuf, pltpu.VMEM((height + 2, cells, 3 * chan), BF16),
                pltpu.VMEM((n_frames, 2, (n_cols + 7) // 8 * 8, chan), F32),
                pltpu.VMEM((rows_a * across, chan), F32), pltpu.VMEM((rows_b * across + tail_rows, chan), F32),
                pltpu.VMEM((height, n_frames, across, chan), BF16), pltpu.SemaphoreType.DMA((height,)),
            ],
            flops * height, near, far, HBM, {len(near): 0} if far else None,
        )

    common = [pa, pb, pc, decays, wt_out, frames]
    if ta != 4:
        return last_kernel(False, common + [ra, edges[0]])
    begun = last_kernel(True, common)
    return last_kernel(False, common + [ra, *edges, za], [begun])


def solution(mesh):
    sizes = [mesh.shape[a] for a in ("gx", "gy", "ta")]
    placed = (P("ta", "gx", "gy", None), P(), P(), P("ta", None))
    return jax.shard_map(
        functools.partial(on_device, *sizes), mesh=mesh, in_specs=placed,
        out_specs=P("ta", "gx", "gy", None), check_vma=False,
    )
```

```python
import functools

import jax
import jax.numpy as jnp
from jax import lax
from jax.experimental import pallas as pl
from jax.experimental.pallas import tpu as pltpu
from jax.sharding import PartitionSpec as P

F32, BF16 = jnp.float32, jnp.bfloat16
VMEM = pl.BlockSpec(memory_space=pltpu.VMEM)
HBM = pl.BlockSpec(memory_space=pltpu.HBM)


def pair_weights(w_ref, wt, flip):
    chan_in, chan_out = w_ref.shape[2:]
    for k in range(4):
        for b in range(3):
            for rr in range(2):
                at = (k * 3 + b) * chan_in
                a = k - rr
                if 0 <= a <= 2:
                    block = w_ref[jnp.where(flip == 1, 2 - a, a), b]
                else:
                    block = jnp.zeros((chan_in, chan_out), BF16)
                wt[at : at + chan_in, rr * chan_out : (rr + 1) * chan_out] = block


def clear_margins(rowbuf):
    across = rowbuf.shape[1] - 16
    zeros = jnp.zeros((rowbuf.shape[0], 8, rowbuf.shape[2]), F32)
    rowbuf[:, 0:8, :] = zeros
    rowbuf[:, 8 + across : 16 + across, :] = zeros


def three_taps(rowbuf, slot, x3, row, f, middle):
    across = rowbuf.shape[1] - 16
    chan = rowbuf.shape[2]
    at = pl.ds(f * across, across)
    x3[row, at, 0:chan] = rowbuf[slot, 7 : 7 + across, :].astype(BF16)
    x3[row, at, chan : 2 * chan] = middle
    x3[row, at, 2 * chan : 3 * chan] = rowbuf[slot, 9 : 9 + across, :].astype(BF16)


def pair_dot(x3, slots, wt, lo=0, hi=None):
    width = x3.shape[2]
    first = next(k for k in range(4) if slots[k] is not None)
    hi = hi or x3.shape[1]
    rows = jnp.concatenate([x3[s, lo:hi, :] for s in slots[first:]], axis=1)
    return jnp.dot(rows, wt[first * width : 4 * width, :], preferred_element_type=F32)


def scan_rows(y, decays, scales, across, keep):
    frames = decays.shape[0]
    chan = decays.shape[1]
    finals = []
    for rr in range(2):
        s = None
        for f in range(frames):
            u = scales[f : f + 1] * y[f * across : (f + 1) * across, rr * chan : (rr + 1) * chan]
            s = u if s is None else decays[f : f + 1] * s + u
            keep(rr, f, s)
        finals.append(s)
    return finals


def load_decays(dec_ref):
    decays = dec_ref[...]
    return decays, jnp.sqrt(1.0 - decays * decays)


def gather_edges(src, row, edge, at):
    frames, across = src.shape[0], src.shape[2]
    for f in range(frames):
        edge[pl.ds(at + f, 2, stride=frames), :] = src[f, row, 0:16, :].astype(F32)[0:2]
        last = src[f, row, across - 16 : across, :].astype(F32)[14:16]
        edge[pl.ds(at + f + 2 * frames, 2, stride=frames), :] = last


def fetch_kernel(two, frames_hbm, dec_hbm, w_hbm, frames_ref, dec_ref, w_ref, cols_ref, *refs):
    *sent, edge, sems = refs
    pairs = [(frames_hbm, frames_ref), (dec_hbm, dec_ref), (w_hbm, w_ref)]
    copies = [pltpu.make_async_copy(src, dst, sems.at[i]) for i, (src, dst) in enumerate(pairs)]
    for copy in copies:
        copy.start()
    copies[0].wait()
    frames, height, across, chan = frames_ref.shape
    for r in range(height):
        gather_edges(frames_ref, r, edge, r * 4 * frames)
    for r in range(height):
        cols_ref[r] = edge[r * 4 * frames : (r + 1) * 4 * frames, :].astype(BF16)
    if two:
        corner_ref, halo_ref, near_ref, far_ref = sent
        odd = lax.axis_index("gy") % 2 == 1
        start = jnp.where(lax.axis_index("gx") == 1, 0, height - 2)
        halo_ref[...] = frames_ref[:, pl.ds(start, 2)]
        half = 2 * frames
        for r in range(height):
            low, high = edge[r * 2 * half : r * 2 * half + half, :], edge[r * 2 * half + half : (r + 1) * 2 * half, :]
            near_ref[r] = jnp.where(odd, low, high).astype(BF16)
            far_ref[r] = jnp.where(odd, high, low).astype(BF16)
        for i in range(2):
            corner_ref[i] = edge[pl.ds(pl.multiple_of((start + i) * 2 * half, 2 * half), 2 * half), :].astype(BF16)
    for copy in copies[1:]:
        copy.wait()


def addends(decays, rows):
    total = decays[0:1]
    for f in range(1, decays.shape[0]):
        total = total * decays[f : f + 1]
    high = total.astype(BF16).astype(F32)
    middle = (total - high).astype(BF16).astype(F32)
    low = total - high - middle
    row = lax.broadcasted_iota(jnp.int32, (rows, decays.shape[1]), 0)
    return jnp.where(row == 0, high, jnp.where(row == 1, middle, jnp.where(row == 2, low, 0.0)))


def inner_kernel(two, frames_ref, dec_ref, w_ref, p_ref, f_ref, wt, rowbuf, x3):
    frames, height, across, chan = frames_ref.shape
    flip = mirrored(two)
    pair_weights(w_ref, wt, flip)
    clear_margins(rowbuf)
    decays, scales = load_decays(dec_ref)
    def build(r):
        natural = jnp.where(flip == 1, height - 1 - r, r)
        for f in range(frames):
            slot = (r * frames + f) % rowbuf.shape[0]
            x = frames_ref[f, natural]
            rowbuf[slot, 8 : 8 + across, :] = x.astype(F32)
            three_taps(rowbuf, slot, x3, r, f, x)

    first, first_row = (0, 1) if two else (1, 0)
    for r in range(2 * first):
        build(r)
    for p in range(first, height // 2):
        build(2 * p)
        build(2 * p + 1)
        slots = [r if r >= 0 else None for r in range(2 * p - 2, 2 * p + 2)]
        y = pair_dot(x3, slots, wt)
        base = 2 * (p - first)

        def keep(rr, f, s, base=base):
            if base + rr >= first_row:
                p_ref[base + rr - first_row, f] = s.astype(BF16)

        for rr, s in enumerate(scan_rows(y, decays, scales, across, keep)):
            at = base + rr - first_row
            if at >= 0:
                f_ref[at * across : (at + 1) * across, :] = s.astype(BF16)
    end = f_ref.shape[0]
    f_ref[end - 16 : end, :] = addends(decays, 16).astype(BF16)


def edge_kernel(two, gx, gy, own_ref, dec_ref, w_ref, halo_ref, e_ref, corner_ref, *refs):
    *sides, p_ref, pc_ref, f_ref, wt, rowbuf, x3, xc, yc = refs
    frames, across, chan = own_ref.shape[0], *own_ref.shape[2:]
    height = e_ref.shape[0] if two else own_ref.shape[1]
    flip = mirrored(two)
    x, y_at = lax.axis_index("gx"), lax.axis_index("gy")
    has_left, has_right = (y_at > 0).astype(F32), (y_at < gy - 1).astype(F32)
    has_above, has_below = (x > 0).astype(F32), (x < gx - 1).astype(F32)
    pair_weights(w_ref, wt, flip)
    clear_margins(rowbuf)
    decays, scales = load_decays(dec_ref)
    pairs = [height // 2] if two else [0, height // 2]
    for i, p in enumerate(pairs):
        for k in range(4):
            r = 2 * p - 2 + k
            for f in range(frames):
                slot = (k * frames + f) % rowbuf.shape[0]
                if two and r < height:
                    x = own_ref[f, jnp.where(flip == 1, height - 1 - r, r - height + 2)]
                elif 0 <= r < height:
                    x = own_ref[f, r]
                elif two:
                    x = halo_ref[f, jnp.where(flip == 1, 1 - (r - height), r - height)]
                else:
                    x = halo_ref[f, r + 2 if r < 0 else r - height + 2]
                rowbuf[slot, 8 : 8 + across, :] = x.astype(F32)
                three_taps(rowbuf, slot, x3, i * 4 + k, f, x)
    odd = y_at % 2 == 1

    def beside(at, first, second):
        first, second = first[at].astype(F32), second[at].astype(F32)
        if not two:
            return first, second
        second = jnp.where((y_at == 0) | (y_at == gy - 1), 0.0, second)
        return jnp.where(odd, first, second), jnp.where(odd, second, first)

    n_pairs = height // 2 + 1
    for p in range(n_pairs):
        for k in range(4):
            r = 2 * p - 2 + k
            to = slice(p * 4 * frames, (p + 1) * 4 * frames)
            lanes = k * 3 * chan
            if two and r < 0:
                xc[to, lanes : lanes + 3 * chan] = jnp.zeros((4 * frames, 3 * chan), BF16)
                continue
            if two and r >= height:
                at = jnp.where(flip == 1, 1 - (r - height), r - height)
                own = corner_ref[at].astype(F32)
                left, right = beside(height + at, *sides)
            else:
                at = jnp.where(flip == 1, height - 1 - r, r) if two else r + 2
                own = e_ref[at].astype(F32)
                left, right = beside(at, *sides)
            cols = [left[:frames], left[frames:]] + [own[c * frames : (c + 1) * frames] for c in range(4)]
            cols += [right[:frames], right[frames:]]
            for b in range(3):
                piece = jnp.concatenate([cols[c + b] for c in (0, 1, 4, 5)], axis=0)
                xc[to, lanes + b * chan : lanes + (b + 1) * chan] = piece.astype(BF16)
    for i, p in enumerate(pairs):
        y = pair_dot(x3, [i * 4 + k for k in range(4)], wt)
        inside = 1.0
        if not two:
            inside = has_above if p == 0 else has_below

        def keep(rr, f, s, i=i, p=p, inside=inside):
            border = (rr == 0) if p == 0 else (rr == 1)
            p_ref[2 * i + rr, f] = s * inside if border and not two else s

        for rr, s in enumerate(scan_rows(y, decays, scales, across, keep)):
            border = (rr == 0) if p == 0 else (rr == 1)
            s = s * inside if border and not two else s
            f_ref[(2 * i + rr) * across : (2 * i + rr + 1) * across, :] = s.astype(BF16)

    wide = jnp.dot(xc[...], wt[...], preferred_element_type=F32)
    for h in range(2):
        yc[h] = wide[:, h * chan : (h + 1) * chan]
    count = n_pairs * 4
    place = lax.broadcasted_iota(jnp.int32, (count, 2 * chan), 0)
    lane = lax.broadcasted_iota(jnp.int32, (count, 2 * chan), 1)
    mask = jnp.where(place % 4 == 0, has_left, jnp.where(place % 4 == 3, has_right, 1.0))
    above = (place < 4) & (lane < chan)
    if two:
        mask = jnp.where(above, 0.0, mask)
    else:
        below = (place >= count - 4) & (lane >= chan)
        mask = jnp.where(above, mask * has_above, mask)
        mask = jnp.where(below, mask * has_below, mask)
    s = None
    for f in range(frames):
        both = [jnp.concatenate([v[f : f + 1]] * 2, axis=1) for v in (decays, scales)]
        halves = [yc[h, pl.ds(f, count, stride=frames), :] for h in range(2)]
        u = both[1] * jnp.concatenate(halves, axis=1) * mask
        s = u if s is None else both[0] * s + u
        for h in range(2):
            pc_ref[h, pl.ds(f, count, stride=frames), :] = s[:, h * chan : (h + 1) * chan]
    base = len(pairs) * 2 * across
    gap = (-2 * count - 8) % 16
    tail = [s[:, :chan], s[:, chan:]] + ([jnp.zeros((gap, chan), F32)] if gap else [])
    f_ref[base:, :] = jnp.concatenate(tail + [addends(decays, 8)], axis=0).astype(BF16)


def prepare_kernel(two, after_ref, w_hbm, wt, w_ref, sem):
    copy = pltpu.make_async_copy(w_hbm, w_ref, sem)
    copy.start()
    copy.wait()
    pair_weights(w_ref, wt, mirrored(two))


def outer_kernel(two, ta, early, n_in, *refs):
    pa_ref, pb_ref, pc_ref, dec_ref, wt, frames_ref, *others = refs[:n_in]
    out_ref, *scratch = refs[n_in:]
    if ta != 4:
        finish_frames(two, ta, early, pa_ref, pb_ref, pc_ref, dec_ref, wt, frames_ref, others, out_ref, *scratch)
        return
    here = lax.axis_index("ta") == 0 if early else lax.axis_index("ta") > 0

    @pl.when(here)
    def _():
        finish_frames(two, ta, early, pa_ref, pb_ref, pc_ref, dec_ref, wt, frames_ref, others, out_ref, *scratch)


def finish_frames(
    two, ta, early, pa_ref, pb_ref, pc_ref, dec_ref, wt, frames_ref, others,
    out_ref, rowbuf, x3, sc, ia, ib, done, sems,
):
    frames, height, across, chan = frames_ref.shape
    flip = mirrored(two)
    decays = dec_ref[...]
    rows_a = pa_ref.shape[0]
    base = pb_ref.shape[0] * across

    def product(ref):
        end = ref.shape[0]
        return jnp.sum(ref[end - 16 : end, :].astype(F32)[8:16], axis=0, keepdims=True)

    t = lax.axis_index("ta")
    if early:
        ia[...] = jnp.zeros_like(ia)
        ib[...] = jnp.zeros_like(ib)
    elif ta != 4:
        ia[...] = others[0][0 : rows_a * across].astype(F32)
        ib[...] = others[1][...].astype(F32)
    else:
        ra_ref, b1_ref, b2_ref, b3_ref, za_ref = others[:5]
        end = ra_ref.shape[0]
        other = jnp.sum(ra_ref[end - 16 : end, :].astype(F32), axis=0, keepdims=True)
        last = (t == 3).astype(F32)
        one, two_on = (t == 1).astype(F32) + last, (t == 2).astype(F32)
        from_a = one, two_on + last * other
        d1, d2, d3 = (product(ref) for ref in (b1_ref, b2_ref, b3_ref))
        from_b = one, two_on * d3 + last * d1, two_on + last * d1 * d2
        ia[...] = sum(c * ref[0 : rows_a * across].astype(F32) for c, ref in zip(from_a, (ra_ref, za_ref)))
        ib[...] = sum(c * ref[...].astype(F32) for c, ref in zip(from_b, (b1_ref, b2_ref, b3_ref)))
    running = [decays[0:1]]
    for f in range(1, frames):
        running.append(running[-1] * decays[f : f + 1])
    count = (height // 2 + 1) * 4
    for f in range(frames):
        for h in range(2):
            part = pc_ref[h, pl.ds(f, count, stride=frames), :]
            sc[f, h, 0:count, :] = part + running[f] * ib[base + count * h : base + count * (h + 1), :]
    def build(n, fs):
        if two and n == 0:
            return
        if two:
            src, at = ((pa_ref, ia), n - 1) if n < height else ((pb_ref, ib), n - height)
        elif 2 <= n < height:
            src, at = (pa_ref, ia), n - 2
        else:
            src, at = (pb_ref, ib), n if n < 2 else n - height + 2
        incoming = src[1][at * across : (at + 1) * across, :]
        for f in fs:
            slot = (n * frames + f) % rowbuf.shape[0]
            rowbuf[slot, 8 : 8 + across, :] = src[0][at, f].astype(F32) + running[f] * incoming
            corner = (n // 2) * 4
            h = n % 2
            rowbuf[slot, 7:9, :] = sc[f, h, corner : corner + 2, :]
            rowbuf[slot, 7 + across : 9 + across, :] = sc[f, h, corner + 2 : corner + 4, :]
            three_taps(rowbuf, slot, x3, n, f, rowbuf[slot, 8 : 8 + across, :].astype(BF16))

    def finish(p, fs, y):
        for rr in range(2):
            natural = jnp.where(flip == 1, height - 1 - (2 * p + rr), 2 * p + rr)
            for i, f in enumerate(fs):
                mixed = y[i * across : (i + 1) * across, rr * chan : (rr + 1) * chan]
                frame = frames_ref[f, natural].astype(F32)
                done[2 * p + rr, f] = (frame + jax.nn.gelu(mixed)).astype(BF16)
            if fs[-1] == frames - 1:
                copy = pltpu.make_async_copy(done.at[2 * p + rr], out_ref.at[:, natural], sems.at[2 * p + rr])
                copy.start()
                copies.append(copy)

    copies, waiting = [], None
    parts = [range(i, i + 4) for i in range(0, frames, 4)]
    for fs in parts:
        for n in range(4):
            build(n, fs)
    for p in range(height // 2):
        slots = [n if n > 0 or not two else None for n in range(2 * p, 2 * p + 4)]
        for fs in parts:
            y = pair_dot(x3, slots, wt, fs[0] * across, (fs[-1] + 1) * across)
            if waiting:
                finish(*waiting)
            waiting = (p, fs, y)
            for n in (2 * p + 4, 2 * p + 5):
                if n < height + 2:
                    build(n, fs)
    finish(*waiting)
    for copy in copies:
        copy.wait()


def call(body, outs, scratch, flops, near, far=(), out_place=VMEM, aliases=None):
    near = [pltpu.with_memory_space_constraint(a, pltpu.VMEM) for a in near]
    far = [pltpu.with_memory_space_constraint(a, pltpu.HBM) for a in far]
    return pl.pallas_call(
        body,
        out_shape=outs,
        in_specs=[VMEM] * len(near) + [HBM] * len(far),
        out_specs=jax.tree.map(lambda _: out_place, outs),
        scratch_shapes=scratch,
        input_output_aliases=aliases or {},
        compiler_params=pltpu.CompilerParams(vmem_limit_bytes=24 * 2**20),
        cost_estimate=pl.CostEstimate(flops=flops, bytes_accessed=4 * 2**20, transcendentals=0),
    )(*near, *far)


def mirrored(two):
    return lax.axis_index("gx") if two else 0


def swapped(value, axis, count, odd_first):
    off = 1 if odd_first else 0
    pairs = [((i + off) % count, (i + 1 + off) % count) for i in range(0, count, 2)]
    return lax.ppermute(value, axis, pairs + [(b, a) for a, b in pairs])


def exchange(low, high, axis, count):
    at = lax.axis_index(axis)
    odd = at % 2 == 1
    if count % 2:
        ups, downs = [(i, i + 1) for i in range(count - 1)], [(i + 1, i) for i in range(count - 1)]
        return lax.ppermute(high, axis, ups), lax.ppermute(low, axis, downs)
    near = swapped(jnp.where(odd, low, high), axis, count, False)
    if count == 2:
        far = jnp.zeros_like(near)
    else:
        far = swapped(jnp.where(odd, high, low), axis, count, True)
        far = jnp.where((at == 0) | (at == count - 1), jnp.zeros_like(far), far)
    return jnp.where(odd, near, far), jnp.where(odd, far, near)


def carry_general(locals_, total, ta):
    t = lax.axis_index("ta")

    def moved(value, step):
        got = lax.ppermute(value, "ta", [(i, (i + step) % ta) for i in range(ta)])
        return jnp.where(t >= step, got, jnp.zeros_like(got))

    step = 1
    while step < ta:
        came = [moved(v, step) for v in locals_]
        locals_ = [(v.astype(F32) + total * m.astype(F32)).astype(BF16) for v, m in zip(locals_, came)]
        total = jnp.where(t >= step, total * moved(total, step), total)
        step *= 2
    return [moved(v, 1) for v in locals_]


def on_device(gx, gy, ta, frames_far, in_weight, out_weight, decays_far):
    n_frames, height, across, chan = frames_far.shape
    two = gx == 2 and gy > 2 and gy % 2 == 0
    t = lax.axis_index("ta")
    near_mem = pltpu.VMEM
    sent = []
    if two:
        side = (height, 2 * n_frames, chan)
        sent = [near_mem(s, BF16) for s in ((2, 4 * n_frames, chan), (n_frames, 2, across, chan), side, side)]
    frames, decays, w_in, cols, *sent = call(
        functools.partial(fetch_kernel, two),
        [
            near_mem(frames_far.shape, BF16), near_mem(decays_far.shape, F32), near_mem(in_weight.shape, BF16),
            near_mem((height, 4 * n_frames, chan), BF16), *sent,
        ],
        [pltpu.VMEM((height * 4 * n_frames, chan), F32), pltpu.SemaphoreType.DMA((3,))],
        0, [], [frames_far, decays_far, in_weight],
    )
    if two:
        facing = [(0, 1), (1, 0)]
        corner = lax.ppermute(sent[0], "gx", facing)
        halo = lax.ppermute(sent[1], "gx", facing)
    else:
        above, below = exchange(frames[:, :2], frames[:, height - 2 :], "gx", gx)
        halo = jnp.concatenate([above, below], axis=1)
        over, under = exchange(cols[:2], cols[height - 2 :], "gx", gx)
        cols = jnp.concatenate([over, cols, under])
        sides = exchange(cols[:, : 2 * n_frames], cols[:, 2 * n_frames :], "gy", gy)
        corner = cols[:2]

    rows_a = height - 1 if two else height - 2
    rows_b = 2 if two else 4
    wt = pltpu.VMEM((12 * chan, 2 * chan), BF16)
    rowbuf = pltpu.VMEM((16, across + 16, chan), F32)
    cells = n_frames * across
    flops = 2 * 9 * chan * chan * cells
    pa, fa = call(
        functools.partial(inner_kernel, two),
        (near_mem((rows_a, n_frames, across, chan), BF16), near_mem((rows_a * across + 16, chan), BF16)),
        [wt, rowbuf, pltpu.VMEM((height, cells, 3 * chan), BF16)],
        flops * height, [frames, decays, w_in],
    )

    if two:
        fa, corner = lax.optimization_barrier((fa, corner))
        odd = lax.axis_index("gy") % 2 == 1
        low, high = corner[:, : 2 * n_frames], corner[:, 2 * n_frames :]
        near = jnp.concatenate([sent[2]] + [jnp.where(odd, low, high)] * 2)
        far = jnp.concatenate([sent[3]] + [jnp.where(odd, high, low)] * 2)
        sides = [swapped(near, "gy", gy, False), swapped(far, "gy", gy, True)]
    total = jnp.prod(decays, axis=0)[None]
    if ta == 4:
        ra = swapped(fa, "ta", ta, False)
        other = jnp.sum(ra[rows_a * across :].astype(F32), axis=0, keepdims=True)

        def joined(mine, theirs):
            mine, theirs = mine.astype(F32), theirs.astype(F32)
            return jnp.where(t == 0, theirs + other * mine, mine + total * theirs).astype(BF16)

        across_two = [(0, 2), (2, 0), (1, 3), (3, 1)]
        ga = joined(fa[: rows_a * across], ra[: rows_a * across])
        za = lax.ppermute(ga, "ta", across_two)
        _, *sides = lax.optimization_barrier((ga, *sides))

    n_cols = (height // 2 + 1) * 4
    tail_rows = (2 * n_cols + 8 + 15) // 16 * 16
    pb, pc, fb = call(
        functools.partial(edge_kernel, two, gx, gy),
        (
            near_mem((rows_b, n_frames, across, chan), F32),
            near_mem((2, n_cols * n_frames, chan), F32),
            near_mem((rows_b * across + tail_rows, chan), BF16),
        ),
        [
            wt, rowbuf, pltpu.VMEM((2 * rows_b, cells, 3 * chan), BF16),
            pltpu.VMEM((n_cols * n_frames, 12 * chan), BF16), pltpu.VMEM((2, n_cols * n_frames, chan), F32),
        ],
        flops * rows_b, [sent[1] if two else frames, decays, w_in, halo, cols, corner, *sides],
    )
    if ta == 4:
        edges = [swapped(fb, "ta", ta, False), lax.ppermute(fb, "ta", across_two), swapped(fb, "ta", ta, True)]
    else:
        ra, rb = carry_general([fa, fb], total, ta)
        za, edges = ra, [rb] * 3

    wt_out = call(
        functools.partial(prepare_kernel, two), near_mem((12 * chan, 2 * chan), BF16),
        [pltpu.VMEM(out_weight.shape, BF16), pltpu.SemaphoreType.DMA], 0, [fb], [out_weight],
    )

    def last_kernel(early, near, far=()):
        return call(
            functools.partial(outer_kernel, two, ta, early, len(near) + len(far)),
            jax.ShapeDtypeStruct(frames.shape, BF16),
            [
                rowbuf, pltpu.VMEM((height + 2, cells, 3 * chan), BF16),
                pltpu.VMEM((n_frames, 2, (n_cols + 7) // 8 * 8, chan), F32),
                pltpu.VMEM((rows_a * across, chan), F32), pltpu.VMEM((rows_b * across + tail_rows, chan), F32),
                pltpu.VMEM((height, n_frames, across, chan), BF16), pltpu.SemaphoreType.DMA((height,)),
            ],
            flops * height, near, far, HBM, {len(near): 0} if far else None,
        )

    common = [pa, pb, pc, decays, wt_out, frames]
    if ta != 4:
        return last_kernel(False, common + [ra, edges[0]])
    begun = last_kernel(True, common)
    return last_kernel(False, common + [ra, *edges, za], [begun])


def solution(mesh):
    sizes = [mesh.shape[a] for a in ("gx", "gy", "ta")]
    placed = (P("ta", "gx", "gy", None), P(), P(), P("ta", None))
    return jax.shard_map(
        functools.partial(on_device, *sizes), mesh=mesh, in_specs=placed,
        out_specs=P("ta", "gx", "gy", None), check_vma=False,
    )
```

```python
import functools

import jax
import jax.numpy as jnp
from jax import lax
from jax.experimental import pallas as pl
from jax.experimental.pallas import tpu as pltpu
from jax.sharding import PartitionSpec as P

F32, BF16 = jnp.float32, jnp.bfloat16
VMEM = pl.BlockSpec(memory_space=pltpu.VMEM)
HBM = pl.BlockSpec(memory_space=pltpu.HBM)


def pair_weights(w_ref, wt, flip):
    chan_in, chan_out = w_ref.shape[2:]
    for k in range(4):
        for b in range(3):
            for rr in range(2):
                at = (k * 3 + b) * chan_in
                a = k - rr
                if 0 <= a <= 2:
                    block = w_ref[jnp.where(flip == 1, 2 - a, a), b]
                else:
                    block = jnp.zeros((chan_in, chan_out), BF16)
                wt[at : at + chan_in, rr * chan_out : (rr + 1) * chan_out] = block


def clear_margins(rowbuf):
    across = rowbuf.shape[1] - 16
    zeros = jnp.zeros((rowbuf.shape[0], 8, rowbuf.shape[2]), F32)
    rowbuf[:, 0:8, :] = zeros
    rowbuf[:, 8 + across : 16 + across, :] = zeros


def three_taps(rowbuf, slot, x3, row, f, middle):
    across = rowbuf.shape[1] - 16
    chan = rowbuf.shape[2]
    at = pl.ds(f * across, across)
    x3[row, at, 0:chan] = rowbuf[slot, 7 : 7 + across, :].astype(BF16)
    x3[row, at, chan : 2 * chan] = middle
    x3[row, at, 2 * chan : 3 * chan] = rowbuf[slot, 9 : 9 + across, :].astype(BF16)


def pair_dot(x3, slots, wt, lo=0, hi=None):
    width = x3.shape[2]
    first = next(k for k in range(4) if slots[k] is not None)
    hi = hi or x3.shape[1]
    rows = jnp.concatenate([x3[s, lo:hi, :] for s in slots[first:]], axis=1)
    return jnp.dot(rows, wt[first * width : 4 * width, :], preferred_element_type=F32)


def scan_rows(y, decays, scales, across, keep):
    frames = decays.shape[0]
    chan = decays.shape[1]
    finals = []
    for rr in range(2):
        s = None
        for f in range(frames):
            u = scales[f : f + 1] * y[f * across : (f + 1) * across, rr * chan : (rr + 1) * chan]
            s = u if s is None else decays[f : f + 1] * s + u
            keep(rr, f, s)
        finals.append(s)
    return finals


def load_decays(dec_ref):
    decays = dec_ref[...]
    return decays, jnp.sqrt(1.0 - decays * decays)


def gather_edges(src, row, edge, at):
    frames, across = src.shape[0], src.shape[2]
    for f in range(frames):
        edge[pl.ds(at + f, 2, stride=frames), :] = src[f, row, 0:16, :].astype(F32)[0:2]
        last = src[f, row, across - 16 : across, :].astype(F32)[14:16]
        edge[pl.ds(at + f + 2 * frames, 2, stride=frames), :] = last


def fetch_kernel(two, frames_hbm, dec_hbm, w_hbm, frames_ref, dec_ref, w_ref, cols_ref, *refs):
    *sent, edge, sems = refs
    pairs = [(frames_hbm, frames_ref), (dec_hbm, dec_ref), (w_hbm, w_ref)]
    copies = [pltpu.make_async_copy(src, dst, sems.at[i]) for i, (src, dst) in enumerate(pairs)]
    for copy in copies:
        copy.start()
    copies[0].wait()
    frames, height, across, chan = frames_ref.shape
    for r in range(height):
        gather_edges(frames_ref, r, edge, r * 4 * frames)
    for r in range(height):
        cols_ref[r] = edge[r * 4 * frames : (r + 1) * 4 * frames, :].astype(BF16)
    if two:
        corner_ref, halo_ref, near_ref, far_ref = sent
        odd = lax.axis_index("gy") % 2 == 1
        start = jnp.where(lax.axis_index("gx") == 1, 0, height - 2)
        halo_ref[...] = frames_ref[:, pl.ds(start, 2)]
        half = 2 * frames
        for r in range(height):
            low, high = edge[r * 2 * half : r * 2 * half + half, :], edge[r * 2 * half + half : (r + 1) * 2 * half, :]
            near_ref[r] = jnp.where(odd, low, high).astype(BF16)
            far_ref[r] = jnp.where(odd, high, low).astype(BF16)
        for i in range(2):
            corner_ref[i] = edge[pl.ds(pl.multiple_of((start + i) * 2 * half, 2 * half), 2 * half), :].astype(BF16)
    for copy in copies[1:]:
        copy.wait()


def addends(decays, rows):
    total = decays[0:1]
    for f in range(1, decays.shape[0]):
        total = total * decays[f : f + 1]
    high = total.astype(BF16).astype(F32)
    middle = (total - high).astype(BF16).astype(F32)
    low = total - high - middle
    row = lax.broadcasted_iota(jnp.int32, (rows, decays.shape[1]), 0)
    return jnp.where(row == 0, high, jnp.where(row == 1, middle, jnp.where(row == 2, low, 0.0)))


def inner_kernel(two, frames_ref, dec_ref, w_ref, p_ref, f_ref, wt, rowbuf, x3):
    frames, height, across, chan = frames_ref.shape
    flip = mirrored(two)
    pair_weights(w_ref, wt, flip)
    clear_margins(rowbuf)
    decays, scales = load_decays(dec_ref)
    def build(r):
        natural = jnp.where(flip == 1, height - 1 - r, r)
        for f in range(frames):
            slot = (r * frames + f) % rowbuf.shape[0]
            x = frames_ref[f, natural]
            rowbuf[slot, 8 : 8 + across, :] = x.astype(F32)
            three_taps(rowbuf, slot, x3, r, f, x)

    first, first_row = (0, 1) if two else (1, 0)
    for r in range(2 * first):
        build(r)
    for p in range(first, height // 2):
        build(2 * p)
        build(2 * p + 1)
        slots = [r if r >= 0 else None for r in range(2 * p - 2, 2 * p + 2)]
        y = pair_dot(x3, slots, wt)
        base = 2 * (p - first)

        def keep(rr, f, s, base=base):
            if base + rr >= first_row:
                p_ref[base + rr - first_row, f] = s.astype(BF16)

        for rr, s in enumerate(scan_rows(y, decays, scales, across, keep)):
            at = base + rr - first_row
            if at >= 0:
                f_ref[at * across : (at + 1) * across, :] = s.astype(BF16)
    end = f_ref.shape[0]
    f_ref[end - 16 : end, :] = addends(decays, 16).astype(BF16)


def edge_kernel(two, gx, gy, own_ref, dec_ref, w_ref, halo_ref, e_ref, corner_ref, *refs):
    *sides, p_ref, pc_ref, f_ref, wt, rowbuf, x3, xc, yc = refs
    frames, across, chan = own_ref.shape[0], *own_ref.shape[2:]
    height = e_ref.shape[0] if two else own_ref.shape[1]
    flip = mirrored(two)
    x, y_at = lax.axis_index("gx"), lax.axis_index("gy")
    has_left, has_right = (y_at > 0).astype(F32), (y_at < gy - 1).astype(F32)
    has_above, has_below = (x > 0).astype(F32), (x < gx - 1).astype(F32)
    pair_weights(w_ref, wt, flip)
    clear_margins(rowbuf)
    decays, scales = load_decays(dec_ref)
    pairs = [height // 2] if two else [0, height // 2]
    for i, p in enumerate(pairs):
        for k in range(4):
            r = 2 * p - 2 + k
            for f in range(frames):
                slot = (k * frames + f) % rowbuf.shape[0]
                if two and r < height:
                    x = own_ref[f, jnp.where(flip == 1, height - 1 - r, r - height + 2)]
                elif 0 <= r < height:
                    x = own_ref[f, r]
                elif two:
                    x = halo_ref[f, jnp.where(flip == 1, 1 - (r - height), r - height)]
                else:
                    x = halo_ref[f, r + 2 if r < 0 else r - height + 2]
                rowbuf[slot, 8 : 8 + across, :] = x.astype(F32)
                three_taps(rowbuf, slot, x3, i * 4 + k, f, x)
    odd = y_at % 2 == 1

    def beside(at, first, second):
        first, second = first[at].astype(F32), second[at].astype(F32)
        if not two:
            return first, second
        second = jnp.where((y_at == 0) | (y_at == gy - 1), 0.0, second)
        return jnp.where(odd, first, second), jnp.where(odd, second, first)

    n_pairs = height // 2 + 1
    for p in range(n_pairs):
        for k in range(4):
            r = 2 * p - 2 + k
            to = slice(p * 4 * frames, (p + 1) * 4 * frames)
            lanes = k * 3 * chan
            if two and r < 0:
                xc[to, lanes : lanes + 3 * chan] = jnp.zeros((4 * frames, 3 * chan), BF16)
                continue
            if two and r >= height:
                at = jnp.where(flip == 1, 1 - (r - height), r - height)
                own = corner_ref[at].astype(F32)
                left, right = beside(height + at, *sides)
            else:
                at = jnp.where(flip == 1, height - 1 - r, r) if two else r + 2
                own = e_ref[at].astype(F32)
                left, right = beside(at, *sides)
            cols = [left[:frames], left[frames:]] + [own[c * frames : (c + 1) * frames] for c in range(4)]
            cols += [right[:frames], right[frames:]]
            for b in range(3):
                piece = jnp.concatenate([cols[c + b] for c in (0, 1, 4, 5)], axis=0)
                xc[to, lanes + b * chan : lanes + (b + 1) * chan] = piece.astype(BF16)
    for i, p in enumerate(pairs):
        y = pair_dot(x3, [i * 4 + k for k in range(4)], wt)
        inside = 1.0
        if not two:
            inside = has_above if p == 0 else has_below

        def keep(rr, f, s, i=i, p=p, inside=inside):
            border = (rr == 0) if p == 0 else (rr == 1)
            p_ref[2 * i + rr, f] = s * inside if border and not two else s

        for rr, s in enumerate(scan_rows(y, decays, scales, across, keep)):
            border = (rr == 0) if p == 0 else (rr == 1)
            s = s * inside if border and not two else s
            f_ref[(2 * i + rr) * across : (2 * i + rr + 1) * across, :] = s.astype(BF16)

    wide = jnp.dot(xc[...], wt[...], preferred_element_type=F32)
    for h in range(2):
        yc[h, 0 : wide.shape[0], :] = wide[:, h * chan : (h + 1) * chan]
    count = n_pairs * 4
    place = lax.broadcasted_iota(jnp.int32, (count, 2 * chan), 0)
    lane = lax.broadcasted_iota(jnp.int32, (count, 2 * chan), 1)
    mask = jnp.where(place % 4 == 0, has_left, jnp.where(place % 4 == 3, has_right, 1.0))
    above = (place < 4) & (lane < chan)
    if two:
        mask = jnp.where(above, 0.0, mask)
    else:
        below = (place >= count - 4) & (lane >= chan)
        mask = jnp.where(above, mask * has_above, mask)
        mask = jnp.where(below, mask * has_below, mask)
    s = None
    for f in range(frames):
        both = [jnp.concatenate([v[f : f + 1]] * 2, axis=1) for v in (decays, scales)]
        halves = [yc[h, pl.ds(f, count, stride=frames), :] for h in range(2)]
        u = both[1] * jnp.concatenate(halves, axis=1) * mask
        s = u if s is None else both[0] * s + u
        for h in range(2):
            pc_ref[h, pl.ds(f, count, stride=frames), :] = s[:, h * chan : (h + 1) * chan]
    base = len(pairs) * 2 * across
    gap = (-2 * count - 8) % 16
    tail = [s[:, :chan], s[:, chan:]] + ([jnp.zeros((gap, chan), F32)] if gap else [])
    f_ref[base:, :] = jnp.concatenate(tail + [addends(decays, 8)], axis=0).astype(BF16)


def prepare_kernel(two, after_ref, w_hbm, wt, w_ref, sem):
    copy = pltpu.make_async_copy(w_hbm, w_ref, sem)
    copy.start()
    copy.wait()
    pair_weights(w_ref, wt, mirrored(two))


def outer_kernel(two, ta, early, n_in, *refs):
    pa_ref, pb_ref, pc_ref, dec_ref, wt, frames_ref, *others = refs[:n_in]
    out_ref, *scratch = refs[n_in:]
    if ta != 4:
        finish_frames(two, ta, early, pa_ref, pb_ref, pc_ref, dec_ref, wt, frames_ref, others, out_ref, *scratch)
        return
    here = lax.axis_index("ta") == 0 if early else lax.axis_index("ta") > 0

    @pl.when(here)
    def _():
        finish_frames(two, ta, early, pa_ref, pb_ref, pc_ref, dec_ref, wt, frames_ref, others, out_ref, *scratch)


def finish_frames(
    two, ta, early, pa_ref, pb_ref, pc_ref, dec_ref, wt, frames_ref, others,
    out_ref, rowbuf, x3, sc, ia, ib, done, sems,
):
    frames, height, across, chan = frames_ref.shape
    flip = mirrored(two)
    decays = dec_ref[...]
    rows_a = pa_ref.shape[0]
    base = pb_ref.shape[0] * across

    def product(ref):
        end = ref.shape[0]
        return jnp.sum(ref[end - 16 : end, :].astype(F32)[8:16], axis=0, keepdims=True)

    t = lax.axis_index("ta")
    if early:
        ia[...] = jnp.zeros_like(ia)
        ib[...] = jnp.zeros_like(ib)
    elif ta != 4:
        ia[...] = others[0][0 : rows_a * across].astype(F32)
        ib[...] = others[1][...].astype(F32)
    else:
        ra_ref, b1_ref, b2_ref, b3_ref, za_ref = others[:5]
        end = ra_ref.shape[0]
        other = jnp.sum(ra_ref[end - 16 : end, :].astype(F32), axis=0, keepdims=True)
        last = (t == 3).astype(F32)
        one, two_on = (t == 1).astype(F32) + last, (t == 2).astype(F32)
        from_a = one, two_on + last * other
        d1, d2, d3 = (product(ref) for ref in (b1_ref, b2_ref, b3_ref))
        from_b = one, two_on * d3 + last * d1, two_on + last * d1 * d2
        ia[...] = sum(c * ref[0 : rows_a * across].astype(F32) for c, ref in zip(from_a, (ra_ref, za_ref)))
        ib[...] = sum(c * ref[...].astype(F32) for c, ref in zip(from_b, (b1_ref, b2_ref, b3_ref)))
    running = [decays[0:1]]
    for f in range(1, frames):
        running.append(running[-1] * decays[f : f + 1])
    count = (height // 2 + 1) * 4
    for f in range(frames):
        for h in range(2):
            part = pc_ref[h, pl.ds(f, count, stride=frames), :]
            sc[f, h, 0:count, :] = part + running[f] * ib[base + count * h : base + count * (h + 1), :]
    def build(n, fs):
        if two and n == 0:
            return
        if two:
            src, at = ((pa_ref, ia), n - 1) if n < height else ((pb_ref, ib), n - height)
        elif 2 <= n < height:
            src, at = (pa_ref, ia), n - 2
        else:
            src, at = (pb_ref, ib), n if n < 2 else n - height + 2
        incoming = src[1][at * across : (at + 1) * across, :]
        for f in fs:
            slot = (n * frames + f) % rowbuf.shape[0]
            rowbuf[slot, 8 : 8 + across, :] = src[0][at, f].astype(F32) + running[f] * incoming
            corner = (n // 2) * 4
            h = n % 2
            rowbuf[slot, 7:9, :] = sc[f, h, corner : corner + 2, :]
            rowbuf[slot, 7 + across : 9 + across, :] = sc[f, h, corner + 2 : corner + 4, :]
            three_taps(rowbuf, slot, x3, n, f, rowbuf[slot, 8 : 8 + across, :].astype(BF16))

    def finish(p, fs, y):
        for rr in range(2):
            natural = jnp.where(flip == 1, height - 1 - (2 * p + rr), 2 * p + rr)
            for i, f in enumerate(fs):
                mixed = y[i * across : (i + 1) * across, rr * chan : (rr + 1) * chan]
                frame = frames_ref[f, natural].astype(F32)
                done[2 * p + rr, f] = (frame + jax.nn.gelu(mixed)).astype(BF16)
            if fs[-1] == frames - 1:
                copy = pltpu.make_async_copy(done.at[2 * p + rr], out_ref.at[:, natural], sems.at[2 * p + rr])
                copy.start()
                copies.append(copy)

    copies, waiting = [], None
    parts = [range(i, i + 4) for i in range(0, frames, 4)]
    for fs in parts:
        for n in range(4):
            build(n, fs)
    for p in range(height // 2):
        slots = [n if n > 0 or not two else None for n in range(2 * p, 2 * p + 4)]
        for fs in parts:
            y = pair_dot(x3, slots, wt, fs[0] * across, (fs[-1] + 1) * across)
            if waiting:
                finish(*waiting)
            waiting = (p, fs, y)
            for n in (2 * p + 4, 2 * p + 5):
                if n < height + 2:
                    build(n, fs)
    finish(*waiting)
    for copy in copies:
        copy.wait()


def call(body, outs, scratch, flops, near, far=(), out_place=VMEM, aliases=None):
    near = [pltpu.with_memory_space_constraint(a, pltpu.VMEM) for a in near]
    far = [pltpu.with_memory_space_constraint(a, pltpu.HBM) for a in far]
    return pl.pallas_call(
        body,
        out_shape=outs,
        in_specs=[VMEM] * len(near) + [HBM] * len(far),
        out_specs=jax.tree.map(lambda _: out_place, outs),
        scratch_shapes=scratch,
        input_output_aliases=aliases or {},
        compiler_params=pltpu.CompilerParams(vmem_limit_bytes=24 * 2**20),
        cost_estimate=pl.CostEstimate(flops=flops, bytes_accessed=4 * 2**20, transcendentals=0),
    )(*near, *far)


def mirrored(two):
    return lax.axis_index("gx") if two else 0


def swapped(value, axis, count, odd_first):
    off = 1 if odd_first else 0
    pairs = [((i + off) % count, (i + 1 + off) % count) for i in range(0, count, 2)]
    return lax.ppermute(value, axis, pairs + [(b, a) for a, b in pairs])


def exchange(low, high, axis, count):
    at = lax.axis_index(axis)
    odd = at % 2 == 1
    if count % 2:
        ups, downs = [(i, i + 1) for i in range(count - 1)], [(i + 1, i) for i in range(count - 1)]
        return lax.ppermute(high, axis, ups), lax.ppermute(low, axis, downs)
    near = swapped(jnp.where(odd, low, high), axis, count, False)
    if count == 2:
        far = jnp.zeros_like(near)
    else:
        far = swapped(jnp.where(odd, high, low), axis, count, True)
        far = jnp.where((at == 0) | (at == count - 1), jnp.zeros_like(far), far)
    return jnp.where(odd, near, far), jnp.where(odd, far, near)


def carry_general(locals_, total, ta):
    t = lax.axis_index("ta")

    def moved(value, step):
        got = lax.ppermute(value, "ta", [(i, (i + step) % ta) for i in range(ta)])
        return jnp.where(t >= step, got, jnp.zeros_like(got))

    step = 1
    while step < ta:
        came = [moved(v, step) for v in locals_]
        locals_ = [(v.astype(F32) + total * m.astype(F32)).astype(BF16) for v, m in zip(locals_, came)]
        total = jnp.where(t >= step, total * moved(total, step), total)
        step *= 2
    return [moved(v, 1) for v in locals_]


def on_device(gx, gy, ta, frames_far, in_weight, out_weight, decays_far):
    n_frames, height, across, chan = frames_far.shape
    two = gx == 2 and gy > 2 and gy % 2 == 0
    t = lax.axis_index("ta")
    near_mem = pltpu.VMEM
    sent = []
    if two:
        side = (height, 2 * n_frames, chan)
        sent = [near_mem(s, BF16) for s in ((2, 4 * n_frames, chan), (n_frames, 2, across, chan), side, side)]
    frames, decays, w_in, cols, *sent = call(
        functools.partial(fetch_kernel, two),
        [
            near_mem(frames_far.shape, BF16), near_mem(decays_far.shape, F32), near_mem(in_weight.shape, BF16),
            near_mem((height, 4 * n_frames, chan), BF16), *sent,
        ],
        [pltpu.VMEM(((height * 4 + 8) * n_frames, chan), F32), pltpu.SemaphoreType.DMA((3,))],
        0, [], [frames_far, decays_far, in_weight],
    )
    if two:
        facing = [(0, 1), (1, 0)]
        corner = lax.ppermute(sent[0], "gx", facing)
        halo = lax.ppermute(sent[1], "gx", facing)
    else:
        above, below = exchange(frames[:, :2], frames[:, height - 2 :], "gx", gx)
        halo = jnp.concatenate([above, below], axis=1)
        over, under = exchange(cols[:2], cols[height - 2 :], "gx", gx)
        cols = jnp.concatenate([over, cols, under])
        sides = exchange(cols[:, : 2 * n_frames], cols[:, 2 * n_frames :], "gy", gy)
        corner = cols[:2]

    rows_a = height - 1 if two else height - 2
    rows_b = 2 if two else 4
    wt = pltpu.VMEM((12 * chan, 2 * chan), BF16)
    rowbuf = pltpu.VMEM((16, across + 16, chan), F32)
    cells = n_frames * across
    flops = 2 * 9 * chan * chan * cells
    pa, fa = call(
        functools.partial(inner_kernel, two),
        (near_mem((rows_a, n_frames, across, chan), BF16), near_mem((rows_a * across + 16, chan), BF16)),
        [wt, rowbuf, pltpu.VMEM((height, cells, 3 * chan), BF16)],
        flops * height, [frames, decays, w_in],
    )

    if two:
        fa, corner = lax.optimization_barrier((fa, corner))
        odd = lax.axis_index("gy") % 2 == 1
        low, high = corner[:, : 2 * n_frames], corner[:, 2 * n_frames :]
        near = jnp.concatenate([sent[2]] + [jnp.where(odd, low, high)] * 2)
        far = jnp.concatenate([sent[3]] + [jnp.where(odd, high, low)] * 2)
        sides = [swapped(near, "gy", gy, False), swapped(far, "gy", gy, True)]
    total = jnp.prod(decays, axis=0)[None]
    if ta == 4:
        ra = swapped(fa, "ta", ta, False)
        other = jnp.sum(ra[rows_a * across :].astype(F32), axis=0, keepdims=True)

        def joined(mine, theirs):
            mine, theirs = mine.astype(F32), theirs.astype(F32)
            return jnp.where(t == 0, theirs + other * mine, mine + total * theirs).astype(BF16)

        across_two = [(0, 2), (2, 0), (1, 3), (3, 1)]
        ga = joined(fa[: rows_a * across], ra[: rows_a * across])
        za = lax.ppermute(ga, "ta", across_two)
        _, *sides = lax.optimization_barrier((ga, *sides))

    n_cols = (height // 2 + 1) * 4
    tail_rows = (2 * n_cols + 8 + 15) // 16 * 16
    pb, pc, fb = call(
        functools.partial(edge_kernel, two, gx, gy),
        (
            near_mem((rows_b, n_frames, across, chan), F32),
            near_mem((2, (n_cols + 7) // 8 * 8 * n_frames, chan), F32),
            near_mem((rows_b * across + tail_rows, chan), BF16),
        ),
        [
            wt, rowbuf, pltpu.VMEM((2 * rows_b, cells, 3 * chan), BF16),
            pltpu.VMEM((n_cols * n_frames, 12 * chan), BF16), pltpu.VMEM((2, (n_cols + 7) // 8 * 8 * n_frames, chan), F32),
        ],
        flops * rows_b, [sent[1] if two else frames, decays, w_in, halo, cols, corner, *sides],
    )
    if ta == 4:
        edges = [swapped(fb, "ta", ta, False), lax.ppermute(fb, "ta", across_two), swapped(fb, "ta", ta, True)]
    else:
        ra, rb = carry_general([fa, fb], total, ta)
        za, edges = ra, [rb] * 3

    wt_out = call(
        functools.partial(prepare_kernel, two), near_mem((12 * chan, 2 * chan), BF16),
        [pltpu.VMEM(out_weight.shape, BF16), pltpu.SemaphoreType.DMA], 0, [fb], [out_weight],
    )

    def last_kernel(early, near, far=()):
        return call(
            functools.partial(outer_kernel, two, ta, early, len(near) + len(far)),
            jax.ShapeDtypeStruct(frames.shape, BF16),
            [
                rowbuf, pltpu.VMEM((height + 2, cells, 3 * chan), BF16),
                pltpu.VMEM((n_frames, 2, (n_cols + 15) // 8 * 8, chan), F32),
                pltpu.VMEM((rows_a * across, chan), F32), pltpu.VMEM((rows_b * across + tail_rows, chan), F32),
                pltpu.VMEM((height, n_frames, across, chan), BF16), pltpu.SemaphoreType.DMA((height,)),
            ],
            flops * height, near, far, HBM, {len(near): 0} if far else None,
        )

    common = [pa, pb, pc, decays, wt_out, frames]
    if ta != 4:
        return last_kernel(False, common + [ra, edges[0]])
    begun = last_kernel(True, common)
    return last_kernel(False, common + [ra, *edges, za], [begun])


def solution(mesh):
    sizes = [mesh.shape[a] for a in ("gx", "gy", "ta")]
    placed = (P("ta", "gx", "gy", None), P(), P(), P("ta", None))
    return jax.shard_map(
        functools.partial(on_device, *sizes), mesh=mesh, in_specs=placed,
        out_specs=P("ta", "gx", "gy", None), check_vma=False,
    )
```

```python
import functools

import jax
import jax.numpy as jnp
from jax import lax
from jax.experimental import pallas as pl
from jax.experimental.pallas import tpu as pltpu
from jax.sharding import PartitionSpec as P

F32, BF16 = jnp.float32, jnp.bfloat16
VMEM = pl.BlockSpec(memory_space=pltpu.VMEM)
HBM = pl.BlockSpec(memory_space=pltpu.HBM)


def pair_weights(w_ref, wt, flip):
    chan_in, chan_out = w_ref.shape[2:]
    for k in range(4):
        for b in range(3):
            for rr in range(2):
                at = (k * 3 + b) * chan_in
                a = k - rr
                if 0 <= a <= 2:
                    block = w_ref[jnp.where(flip == 1, 2 - a, a), b]
                else:
                    block = jnp.zeros((chan_in, chan_out), BF16)
                wt[at : at + chan_in, rr * chan_out : (rr + 1) * chan_out] = block


def clear_margins(rowbuf):
    across = rowbuf.shape[1] - 16
    zeros = jnp.zeros((rowbuf.shape[0], 8, rowbuf.shape[2]), F32)
    rowbuf[:, 0:8, :] = zeros
    rowbuf[:, 8 + across : 16 + across, :] = zeros


def three_taps(rowbuf, slot, x3, row, f, middle):
    across = rowbuf.shape[1] - 16
    chan = rowbuf.shape[2]
    at = pl.ds(f * across, across)
    x3[row, at, 0:chan] = rowbuf[slot, 7 : 7 + across, :].astype(BF16)
    x3[row, at, chan : 2 * chan] = middle
    x3[row, at, 2 * chan : 3 * chan] = rowbuf[slot, 9 : 9 + across, :].astype(BF16)


def pair_dot(x3, slots, wt, lo=0, hi=None):
    width = x3.shape[2]
    first = next(k for k in range(4) if slots[k] is not None)
    hi = hi or x3.shape[1]
    rows = jnp.concatenate([x3[s, lo:hi, :] for s in slots[first:]], axis=1)
    return jnp.dot(rows, wt[first * width : 4 * width, :], preferred_element_type=F32)


def scan_rows(y, decays, scales, across, keep):
    frames = decays.shape[0]
    chan = decays.shape[1]
    finals = []
    for rr in range(2):
        s = None
        for f in range(frames):
            u = scales[f : f + 1] * y[f * across : (f + 1) * across, rr * chan : (rr + 1) * chan]
            s = u if s is None else decays[f : f + 1] * s + u
            keep(rr, f, s)
        finals.append(s)
    return finals


def load_decays(dec_ref):
    decays = dec_ref[...]
    return decays, jnp.sqrt(1.0 - decays * decays)


def gather_edges(src, row, edge, at):
    frames, across = src.shape[0], src.shape[2]
    for f in range(frames):
        edge[pl.ds(at + f, 2, stride=frames), :] = src[f, row, 0:16, :].astype(F32)[0:2]
        last = src[f, row, across - 16 : across, :].astype(F32)[14:16]
        edge[pl.ds(at + f + 2 * frames, 2, stride=frames), :] = last


def fetch_kernel(two, frames_hbm, dec_hbm, w_hbm, frames_ref, dec_ref, w_ref, cols_ref, *refs):
    *sent, edge, sems = refs
    pairs = [(frames_hbm, frames_ref), (dec_hbm, dec_ref), (w_hbm, w_ref)]
    copies = [pltpu.make_async_copy(src, dst, sems.at[i]) for i, (src, dst) in enumerate(pairs)]
    for copy in copies:
        copy.start()
    copies[0].wait()
    frames, height, across, chan = frames_ref.shape
    for r in range(height):
        gather_edges(frames_ref, r, edge, r * 4 * frames)
    for r in range(height):
        cols_ref[r] = edge[r * 4 * frames : (r + 1) * 4 * frames, :].astype(BF16)
    if two:
        corner_ref, halo_ref, near_ref, far_ref = sent
        odd = lax.axis_index("gy") % 2 == 1
        start = jnp.where(lax.axis_index("gx") == 1, 0, height - 2)
        halo_ref[...] = frames_ref[:, pl.ds(start, 2)]
        half = 2 * frames
        for r in range(height):
            low, high = edge[r * 2 * half : r * 2 * half + half, :], edge[r * 2 * half + half : (r + 1) * 2 * half, :]
            near_ref[r] = jnp.where(odd, low, high).astype(BF16)
            far_ref[r] = jnp.where(odd, high, low).astype(BF16)
        for i in range(2):
            corner_ref[i] = edge[pl.ds(pl.multiple_of((start + i) * 2 * half, 2 * half), 2 * half), :].astype(BF16)
    for copy in copies[1:]:
        copy.wait()


def addends(decays, rows):
    total = decays[0:1]
    for f in range(1, decays.shape[0]):
        total = total * decays[f : f + 1]
    high = total.astype(BF16).astype(F32)
    middle = (total - high).astype(BF16).astype(F32)
    low = total - high - middle
    row = lax.broadcasted_iota(jnp.int32, (rows, decays.shape[1]), 0)
    return jnp.where(row == 0, high, jnp.where(row == 1, middle, jnp.where(row == 2, low, 0.0)))


def inner_kernel(two, frames_ref, dec_ref, w_ref, p_ref, f_ref, wt, rowbuf, x3):
    frames, height, across, chan = frames_ref.shape
    flip = mirrored(two)
    pair_weights(w_ref, wt, flip)
    clear_margins(rowbuf)
    decays, scales = load_decays(dec_ref)
    def build(r):
        natural = jnp.where(flip == 1, height - 1 - r, r)
        for f in range(frames):
            slot = (r * frames + f) % rowbuf.shape[0]
            x = frames_ref[f, natural]
            rowbuf[slot, 8 : 8 + across, :] = x.astype(F32)
            three_taps(rowbuf, slot, x3, r, f, x)

    first, first_row = (0, 1) if two else (1, 0)
    for r in range(2 * first):
        build(r)
    for p in range(first, height // 2):
        build(2 * p)
        build(2 * p + 1)
        slots = [r if r >= 0 else None for r in range(2 * p - 2, 2 * p + 2)]
        half = frames // 2 * across
        y = jnp.concatenate([pair_dot(x3, slots, wt, 0, half), pair_dot(x3, slots, wt, half, frames * across)])
        base = 2 * (p - first)

        def keep(rr, f, s, base=base):
            if base + rr >= first_row:
                p_ref[base + rr - first_row, f] = s.astype(BF16)

        for rr, s in enumerate(scan_rows(y, decays, scales, across, keep)):
            at = base + rr - first_row
            if at >= 0:
                f_ref[at * across : (at + 1) * across, :] = s.astype(BF16)
    end = f_ref.shape[0]
    f_ref[end - 16 : end, :] = addends(decays, 16).astype(BF16)


def edge_kernel(two, gx, gy, own_ref, dec_ref, w_ref, halo_ref, e_ref, corner_ref, *refs):
    *sides, p_ref, pc_ref, f_ref, wt, rowbuf, x3, xc, yc = refs
    frames, across, chan = own_ref.shape[0], *own_ref.shape[2:]
    height = e_ref.shape[0] if two else own_ref.shape[1]
    flip = mirrored(two)
    x, y_at = lax.axis_index("gx"), lax.axis_index("gy")
    has_left, has_right = (y_at > 0).astype(F32), (y_at < gy - 1).astype(F32)
    has_above, has_below = (x > 0).astype(F32), (x < gx - 1).astype(F32)
    pair_weights(w_ref, wt, flip)
    clear_margins(rowbuf)
    decays, scales = load_decays(dec_ref)
    pairs = [height // 2] if two else [0, height // 2]
    for i, p in enumerate(pairs):
        for k in range(4):
            r = 2 * p - 2 + k
            for f in range(frames):
                slot = (k * frames + f) % rowbuf.shape[0]
                if two and r < height:
                    x = own_ref[f, jnp.where(flip == 1, height - 1 - r, r - height + 2)]
                elif 0 <= r < height:
                    x = own_ref[f, r]
                elif two:
                    x = halo_ref[f, jnp.where(flip == 1, 1 - (r - height), r - height)]
                else:
                    x = halo_ref[f, r + 2 if r < 0 else r - height + 2]
                rowbuf[slot, 8 : 8 + across, :] = x.astype(F32)
                three_taps(rowbuf, slot, x3, i * 4 + k, f, x)
    odd = y_at % 2 == 1

    def beside(at, first, second):
        first, second = first[at].astype(F32), second[at].astype(F32)
        if not two:
            return first, second
        second = jnp.where((y_at == 0) | (y_at == gy - 1), 0.0, second)
        return jnp.where(odd, first, second), jnp.where(odd, second, first)

    n_pairs = height // 2 + 1
    for p in range(n_pairs):
        for k in range(4):
            r = 2 * p - 2 + k
            to = slice(p * 4 * frames, (p + 1) * 4 * frames)
            lanes = k * 3 * chan
            if two and r < 0:
                xc[to, lanes : lanes + 3 * chan] = jnp.zeros((4 * frames, 3 * chan), BF16)
                continue
            if two and r >= height:
                at = jnp.where(flip == 1, 1 - (r - height), r - height)
                own = corner_ref[at].astype(F32)
                left, right = beside(height + at, *sides)
            else:
                at = jnp.where(flip == 1, height - 1 - r, r) if two else r + 2
                own = e_ref[at].astype(F32)
                left, right = beside(at, *sides)
            cols = [left[:frames], left[frames:]] + [own[c * frames : (c + 1) * frames] for c in range(4)]
            cols += [right[:frames], right[frames:]]
            for b in range(3):
                piece = jnp.concatenate([cols[c + b] for c in (0, 1, 4, 5)], axis=0)
                xc[to, lanes + b * chan : lanes + (b + 1) * chan] = piece.astype(BF16)
    for i, p in enumerate(pairs):
        y = pair_dot(x3, [i * 4 + k for k in range(4)], wt)
        inside = 1.0
        if not two:
            inside = has_above if p == 0 else has_below

        def keep(rr, f, s, i=i, p=p, inside=inside):
            border = (rr == 0) if p == 0 else (rr == 1)
            p_ref[2 * i + rr, f] = s * inside if border and not two else s

        for rr, s in enumerate(scan_rows(y, decays, scales, across, keep)):
            border = (rr == 0) if p == 0 else (rr == 1)
            s = s * inside if border and not two else s
            f_ref[(2 * i + rr) * across : (2 * i + rr + 1) * across, :] = s.astype(BF16)

    wide = jnp.dot(xc[...], wt[...], preferred_element_type=F32)
    for h in range(2):
        yc[h, 0 : wide.shape[0], :] = wide[:, h * chan : (h + 1) * chan]
    count = n_pairs * 4
    place = lax.broadcasted_iota(jnp.int32, (count, 2 * chan), 0)
    lane = lax.broadcasted_iota(jnp.int32, (count, 2 * chan), 1)
    mask = jnp.where(place % 4 == 0, has_left, jnp.where(place % 4 == 3, has_right, 1.0))
    above = (place < 4) & (lane < chan)
    if two:
        mask = jnp.where(above, 0.0, mask)
    else:
        below = (place >= count - 4) & (lane >= chan)
        mask = jnp.where(above, mask * has_above, mask)
        mask = jnp.where(below, mask * has_below, mask)
    s = None
    for f in range(frames):
        both = [jnp.concatenate([v[f : f + 1]] * 2, axis=1) for v in (decays, scales)]
        halves = [yc[h, pl.ds(f, count, stride=frames), :] for h in range(2)]
        u = both[1] * jnp.concatenate(halves, axis=1) * mask
        s = u if s is None else both[0] * s + u
        for h in range(2):
            pc_ref[h, pl.ds(f, count, stride=frames), :] = s[:, h * chan : (h + 1) * chan]
    base = len(pairs) * 2 * across
    gap = (-2 * count - 8) % 16
    tail = [s[:, :chan], s[:, chan:]] + ([jnp.zeros((gap, chan), F32)] if gap else [])
    f_ref[base:, :] = jnp.concatenate(tail + [addends(decays, 8)], axis=0).astype(BF16)


def prepare_kernel(two, after_ref, w_hbm, wt, w_ref, sem):
    copy = pltpu.make_async_copy(w_hbm, w_ref, sem)
    copy.start()
    copy.wait()
    pair_weights(w_ref, wt, mirrored(two))


def outer_kernel(two, ta, early, n_in, *refs):
    pa_ref, pb_ref, pc_ref, dec_ref, wt, frames_ref, *others = refs[:n_in]
    out_ref, *scratch = refs[n_in:]
    if ta != 4:
        finish_frames(two, ta, early, pa_ref, pb_ref, pc_ref, dec_ref, wt, frames_ref, others, out_ref, *scratch)
        return
    here = lax.axis_index("ta") == 0 if early else lax.axis_index("ta") > 0

    @pl.when(here)
    def _():
        finish_frames(two, ta, early, pa_ref, pb_ref, pc_ref, dec_ref, wt, frames_ref, others, out_ref, *scratch)


def finish_frames(
    two, ta, early, pa_ref, pb_ref, pc_ref, dec_ref, wt, frames_ref, others,
    out_ref, rowbuf, x3, sc, ia, ib, done, sems,
):
    frames, height, across, chan = frames_ref.shape
    flip = mirrored(two)
    decays = dec_ref[...]
    rows_a = pa_ref.shape[0]
    base = pb_ref.shape[0] * across

    def product(ref):
        end = ref.shape[0]
        return jnp.sum(ref[end - 16 : end, :].astype(F32)[8:16], axis=0, keepdims=True)

    t = lax.axis_index("ta")
    if early:
        ia[...] = jnp.zeros_like(ia)
        ib[...] = jnp.zeros_like(ib)
    elif ta != 4:
        ia[...] = others[0][0 : rows_a * across].astype(F32)
        ib[...] = others[1][...].astype(F32)
    else:
        ra_ref, b1_ref, b2_ref, b3_ref, za_ref = others[:5]
        end = ra_ref.shape[0]
        other = jnp.sum(ra_ref[end - 16 : end, :].astype(F32), axis=0, keepdims=True)
        last = (t == 3).astype(F32)
        one, two_on = (t == 1).astype(F32) + last, (t == 2).astype(F32)
        from_a = one, two_on + last * other
        d1, d2, d3 = (product(ref) for ref in (b1_ref, b2_ref, b3_ref))
        from_b = one, two_on * d3 + last * d1, two_on + last * d1 * d2
        ia[...] = sum(c * ref[0 : rows_a * across].astype(F32) for c, ref in zip(from_a, (ra_ref, za_ref)))
        ib[...] = sum(c * ref[...].astype(F32) for c, ref in zip(from_b, (b1_ref, b2_ref, b3_ref)))
    running = [decays[0:1]]
    for f in range(1, frames):
        running.append(running[-1] * decays[f : f + 1])
    count = (height // 2 + 1) * 4
    for f in range(frames):
        for h in range(2):
            part = pc_ref[h, pl.ds(f, count, stride=frames), :]
            sc[f, h, 0:count, :] = part + running[f] * ib[base + count * h : base + count * (h + 1), :]
    def build(n, fs):
        if two and n == 0:
            return
        if two:
            src, at = ((pa_ref, ia), n - 1) if n < height else ((pb_ref, ib), n - height)
        elif 2 <= n < height:
            src, at = (pa_ref, ia), n - 2
        else:
            src, at = (pb_ref, ib), n if n < 2 else n - height + 2
        incoming = src[1][at * across : (at + 1) * across, :]
        for f in fs:
            slot = (n * frames + f) % rowbuf.shape[0]
            rowbuf[slot, 8 : 8 + across, :] = src[0][at, f].astype(F32) + running[f] * incoming
            corner = (n // 2) * 4
            h = n % 2
            rowbuf[slot, 7:9, :] = sc[f, h, corner : corner + 2, :]
            rowbuf[slot, 7 + across : 9 + across, :] = sc[f, h, corner + 2 : corner + 4, :]
            three_taps(rowbuf, slot, x3, n, f, rowbuf[slot, 8 : 8 + across, :].astype(BF16))

    def finish(p, fs, y):
        for rr in range(2):
            natural = jnp.where(flip == 1, height - 1 - (2 * p + rr), 2 * p + rr)
            for i, f in enumerate(fs):
                mixed = y[i * across : (i + 1) * across, rr * chan : (rr + 1) * chan]
                frame = frames_ref[f, natural].astype(F32)
                done[2 * p + rr, f] = (frame + jax.nn.gelu(mixed)).astype(BF16)
            if fs[-1] == frames - 1:
                copy = pltpu.make_async_copy(done.at[2 * p + rr], out_ref.at[:, natural], sems.at[2 * p + rr])
                copy.start()
                copies.append(copy)

    copies, waiting = [], None
    parts = [range(i, i + 4) for i in range(0, frames, 4)]
    for fs in parts:
        for n in range(4):
            build(n, fs)
    for p in range(height // 2):
        slots = [n if n > 0 or not two else None for n in range(2 * p, 2 * p + 4)]
        for fs in parts:
            y = pair_dot(x3, slots, wt, fs[0] * across, (fs[-1] + 1) * across)
            if waiting:
                finish(*waiting)
            waiting = (p, fs, y)
            for n in (2 * p + 4, 2 * p + 5):
                if n < height + 2:
                    build(n, fs)
    finish(*waiting)
    for copy in copies:
        copy.wait()


def call(body, outs, scratch, flops, near, far=(), out_place=VMEM, aliases=None):
    near = [pltpu.with_memory_space_constraint(a, pltpu.VMEM) for a in near]
    far = [pltpu.with_memory_space_constraint(a, pltpu.HBM) for a in far]
    return pl.pallas_call(
        body,
        out_shape=outs,
        in_specs=[VMEM] * len(near) + [HBM] * len(far),
        out_specs=jax.tree.map(lambda _: out_place, outs),
        scratch_shapes=scratch,
        input_output_aliases=aliases or {},
        compiler_params=pltpu.CompilerParams(vmem_limit_bytes=24 * 2**20),
        cost_estimate=pl.CostEstimate(flops=flops, bytes_accessed=4 * 2**20, transcendentals=0),
    )(*near, *far)


def mirrored(two):
    return lax.axis_index("gx") if two else 0


def swapped(value, axis, count, odd_first):
    off = 1 if odd_first else 0
    pairs = [((i + off) % count, (i + 1 + off) % count) for i in range(0, count, 2)]
    return lax.ppermute(value, axis, pairs + [(b, a) for a, b in pairs])


def exchange(low, high, axis, count):
    at = lax.axis_index(axis)
    odd = at % 2 == 1
    if count % 2:
        ups, downs = [(i, i + 1) for i in range(count - 1)], [(i + 1, i) for i in range(count - 1)]
        return lax.ppermute(high, axis, ups), lax.ppermute(low, axis, downs)
    near = swapped(jnp.where(odd, low, high), axis, count, False)
    if count == 2:
        far = jnp.zeros_like(near)
    else:
        far = swapped(jnp.where(odd, high, low), axis, count, True)
        far = jnp.where((at == 0) | (at == count - 1), jnp.zeros_like(far), far)
    return jnp.where(odd, near, far), jnp.where(odd, far, near)


def carry_general(locals_, total, ta):
    t = lax.axis_index("ta")

    def moved(value, step):
        got = lax.ppermute(value, "ta", [(i, (i + step) % ta) for i in range(ta)])
        return jnp.where(t >= step, got, jnp.zeros_like(got))

    step = 1
    while step < ta:
        came = [moved(v, step) for v in locals_]
        locals_ = [(v.astype(F32) + total * m.astype(F32)).astype(BF16) for v, m in zip(locals_, came)]
        total = jnp.where(t >= step, total * moved(total, step), total)
        step *= 2
    return [moved(v, 1) for v in locals_]


def on_device(gx, gy, ta, frames_far, in_weight, out_weight, decays_far):
    n_frames, height, across, chan = frames_far.shape
    two = gx == 2 and gy > 2 and gy % 2 == 0
    t = lax.axis_index("ta")
    near_mem = pltpu.VMEM
    sent = []
    if two:
        side = (height, 2 * n_frames, chan)
        sent = [near_mem(s, BF16) for s in ((2, 4 * n_frames, chan), (n_frames, 2, across, chan), side, side)]
    frames, decays, w_in, cols, *sent = call(
        functools.partial(fetch_kernel, two),
        [
            near_mem(frames_far.shape, BF16), near_mem(decays_far.shape, F32), near_mem(in_weight.shape, BF16),
            near_mem((height, 4 * n_frames, chan), BF16), *sent,
        ],
        [pltpu.VMEM(((height * 4 + 8) * n_frames, chan), F32), pltpu.SemaphoreType.DMA((3,))],
        0, [], [frames_far, decays_far, in_weight],
    )
    if two:
        facing = [(0, 1), (1, 0)]
        corner = lax.ppermute(sent[0], "gx", facing)
        halo = lax.ppermute(sent[1], "gx", facing)
    else:
        above, below = exchange(frames[:, :2], frames[:, height - 2 :], "gx", gx)
        halo = jnp.concatenate([above, below], axis=1)
        over, under = exchange(cols[:2], cols[height - 2 :], "gx", gx)
        cols = jnp.concatenate([over, cols, under])
        sides = exchange(cols[:, : 2 * n_frames], cols[:, 2 * n_frames :], "gy", gy)
        corner = cols[:2]

    rows_a = height - 1 if two else height - 2
    rows_b = 2 if two else 4
    wt = pltpu.VMEM((12 * chan, 2 * chan), BF16)
    rowbuf = pltpu.VMEM((16, across + 16, chan), F32)
    cells = n_frames * across
    flops = 2 * 9 * chan * chan * cells
    pa, fa = call(
        functools.partial(inner_kernel, two),
        (near_mem((rows_a, n_frames, across, chan), BF16), near_mem((rows_a * across + 16, chan), BF16)),
        [wt, rowbuf, pltpu.VMEM((height, cells, 3 * chan), BF16)],
        flops * height, [frames, decays, w_in],
    )

    if two:
        fa, corner = lax.optimization_barrier((fa, corner))
        odd = lax.axis_index("gy") % 2 == 1
        low, high = corner[:, : 2 * n_frames], corner[:, 2 * n_frames :]
        near = jnp.concatenate([sent[2]] + [jnp.where(odd, low, high)] * 2)
        far = jnp.concatenate([sent[3]] + [jnp.where(odd, high, low)] * 2)
        sides = [swapped(near, "gy", gy, False), swapped(far, "gy", gy, True)]
    total = jnp.prod(decays, axis=0)[None]
    if ta == 4:
        ra = swapped(fa, "ta", ta, False)
        other = jnp.sum(ra[rows_a * across :].astype(F32), axis=0, keepdims=True)

        def joined(mine, theirs):
            mine, theirs = mine.astype(F32), theirs.astype(F32)
            return jnp.where(t == 0, theirs + other * mine, mine + total * theirs).astype(BF16)

        across_two = [(0, 2), (2, 0), (1, 3), (3, 1)]
        ga = joined(fa[: rows_a * across], ra[: rows_a * across])
        za = lax.ppermute(ga, "ta", across_two)
        _, *sides = lax.optimization_barrier((ga, *sides))

    n_cols = (height // 2 + 1) * 4
    tail_rows = (2 * n_cols + 8 + 15) // 16 * 16
    pb, pc, fb = call(
        functools.partial(edge_kernel, two, gx, gy),
        (
            near_mem((rows_b, n_frames, across, chan), F32),
            near_mem((2, (n_cols + 7) // 8 * 8 * n_frames, chan), F32),
            near_mem((rows_b * across + tail_rows, chan), BF16),
        ),
        [
            wt, rowbuf, pltpu.VMEM((2 * rows_b, cells, 3 * chan), BF16),
            pltpu.VMEM((n_cols * n_frames, 12 * chan), BF16), pltpu.VMEM((2, (n_cols + 7) // 8 * 8 * n_frames, chan), F32),
        ],
        flops * rows_b, [sent[1] if two else frames, decays, w_in, halo, cols, corner, *sides],
    )
    if ta == 4:
        edges = [swapped(fb, "ta", ta, False), lax.ppermute(fb, "ta", across_two), swapped(fb, "ta", ta, True)]
    else:
        ra, rb = carry_general([fa, fb], total, ta)
        za, edges = ra, [rb] * 3

    wt_out = call(
        functools.partial(prepare_kernel, two), near_mem((12 * chan, 2 * chan), BF16),
        [pltpu.VMEM(out_weight.shape, BF16), pltpu.SemaphoreType.DMA], 0, [fb], [out_weight],
    )

    def last_kernel(early, near, far=()):
        return call(
            functools.partial(outer_kernel, two, ta, early, len(near) + len(far)),
            jax.ShapeDtypeStruct(frames.shape, BF16),
            [
                rowbuf, pltpu.VMEM((height + 2, cells, 3 * chan), BF16),
                pltpu.VMEM((n_frames, 2, (n_cols + 15) // 8 * 8, chan), F32),
                pltpu.VMEM((rows_a * across, chan), F32), pltpu.VMEM((rows_b * across + tail_rows, chan), F32),
                pltpu.VMEM((height, n_frames, across, chan), BF16), pltpu.SemaphoreType.DMA((height,)),
            ],
            flops * height, near, far, HBM, {len(near): 0} if far else None,
        )

    common = [pa, pb, pc, decays, wt_out, frames]
    if ta != 4:
        return last_kernel(False, common + [ra, edges[0]])
    begun = last_kernel(True, common)
    return last_kernel(False, common + [ra, *edges, za], [begun])


def solution(mesh):
    sizes = [mesh.shape[a] for a in ("gx", "gy", "ta")]
    placed = (P("ta", "gx", "gy", None), P(), P(), P("ta", None))
    return jax.shard_map(
        functools.partial(on_device, *sizes), mesh=mesh, in_specs=placed,
        out_specs=P("ta", "gx", "gy", None), check_vma=False,
    )
```
